32 devices in a mesh: rays: 8 (over z, y), rep: 4 (over x, core).
Axes of the slice: x: 2, y: 2, z: 4, core: 2. Of those that a mesh axis runs over, the one named last changes fastest.
Arguments:
- sample_means: float32 [2, 3, 2048, 128], P(None, None, ('rays', 'rep')), may hold values from -1.5 to 1.5
- sample_vars: float32 [2, 3, 2048, 128], P(None, None, ('rays', 'rep')), may hold values from 0.0001 to 0.01
- sample_spacing: float32 [2, 2048, 128], P(None, ('rays', 'rep')), may hold values from 0.01 to 0.1
- view_dirs: float32 [3, 2048], P(None, ('rays', 'rep')), may hold values from -2.5 to 2.5
- target_rgb: float32 [3, 2048], P(None, ('rays', 'rep')), may hold values from 0 to 1
- sample_counts: int32 [2, 2048], P(None, ('rays', 'rep')), may hold values from 10 to 128, as said below
- ray_mask: int32 [2048], P(('rays', 'rep')), may hold values from 0 to 1
- w_in: float32 [96, 256], replicated, may hold values from -0.625 to 0.625
- w_mid: float32 [2, 256, 256], replicated, may hold values from -0.375 to 0.375
- w_head: float32 [283, 128], replicated, may hold values from -0.375 to 0.375
- w_rgb: float32 [128, 3], replicated, may hold values from -0.5 to 0.5
- vectors: float32 [1156], replicated, may hold values from -0.6 to 0.6
- first_in: float32 [96, 256], replicated, may hold values from -9.1552734e-05 to 9.1552734e-05
- first_mid: float32 [2, 256, 256], replicated, may hold values from -9.1552734e-05 to 9.1552734e-05
- first_head: float32 [283, 128], replicated, may hold values from -9.1552734e-05 to 9.1552734e-05
- first_rgb: float32 [128, 3], replicated, may hold values from -9.1552734e-05 to 9.1552734e-05
- first_vec: float32 [1156], replicated, may hold values from -9.1552734e-05 to 9.1552734e-05
- second_in: float32 [96, 256], replicated, may hold values from 4.394531e-12 to 1.7578125e-11
- second_mid: float32 [2, 256, 256], replicated, may hold values from 4.394531e-12 to 1.7578125e-11
- second_head: float32 [283, 128], replicated, may hold values from 4.394531e-12 to 1.7578125e-11
- second_rgb: float32 [128, 3], replicated, may hold values from 4.394531e-12 to 1.7578125e-11
- second_vec: float32 [1156], replicated, may hold values from 4.394531e-12 to 1.7578125e-11
Outputs:
- loss_sum: float32 [], replicated
- ray_count: float32 [], replicated
- new_first_in: float32 [96, 256], replicated
- new_second_in: float32 [96, 256], replicated
- new_w_in: float32 [96, 256], replicated
- new_first_mid: float32 [2, 256, 256], replicated
- new_second_mid: float32 [2, 256, 256], replicated
- new_w_mid: float32 [2, 256, 256], replicated
- new_first_head: float32 [283, 128], replicated
- new_second_head: float32 [283, 128], replicated
- new_w_head: float32 [283, 128], replicated
- new_first_rgb: float32 [128, 3], replicated
- new_second_rgb: float32 [128, 3], replicated
- new_w_rgb: float32 [128, 3], replicated
- new_first_vec: float32 [1156], replicated
- new_second_vec: float32 [1156], replicated
- new_vectors: float32 [1156], replicated
The draws below stay inside these ranges and needn't reach their ends.
Inputs may be any that keep to these rules, and one draw needn't show every extreme that they name: `sample_counts`: in each pass a ray's valid samples are its first slots. Over the rays of one device a pass has at most 6144 valid samples, and some device of each group along rays has exactly 6144. Over the devices of one group along rays (one index of rep) the valid samples of a pass total exactly 20480.
All inputs are finite; a program needn't handle non-finite values.
Results may differ from the reference program's by a relative error of at most 0.0003.
The reference program's roundings to bfloat16 on the way count: a program that leaves them out, or rounds other values in their place, can miss the bound.
Values sent between devices are 32-bit elements; how exact they have to be, the bound alone decides.
No kernel may reach another device: no remote copies, remote signals or barrier semaphores. Data moves between devices by JAX's collectives and lax.ppermute only.
A program may use at most 64 MiB of HBM per device.

```python
import math
import jax
import jax.numpy as jnp
from jax import lax

H = 256
FEAT = 128
L_POS = 16
L_DIR = 4
NMID = 2
S = 128
CMIN = 10
STEP = 7
R_DEV = 64
RAYS = 2048
VEC = 1156
N_RAYS = 8
N_REP = 4


def draw_sample_counts(key, part):
    key = jax.random.fold_in(key, 5)
    first_key, second_key, third_key = jax.random.split(key, 3)
    high_level = 3 * S // 4
    low_level = S // 4
    busy_count = N_RAYS // 8
    places = jnp.arange(N_RAYS, dtype=jnp.int32)
    is_busy = places < busy_count
    extra = jax.random.randint(first_key, (2, N_REP, N_RAYS), 0, 9)
    extra = jnp.where(is_busy[None, None, :], 0, extra)
    following = jnp.where(places + 1 < N_RAYS, places + 1, busy_count)
    levels = jnp.where(is_busy[None, None, :], high_level, low_level + extra - jnp.take(extra, following, axis=2))
    scores = jax.random.randint(second_key, (2, N_REP, N_RAYS), 0, 1 << 20) * N_RAYS + places[None, None, :]
    order = jnp.argsort(scores, axis=2)
    levels = jnp.take_along_axis(levels, order, axis=2)
    spread = jnp.minimum(S - levels, levels - CMIN)[..., None]
    shifts = jax.random.randint(third_key, (2, N_REP, N_RAYS, R_DEV), 0, 1 << 20) % (spread + 1)
    shifts = shifts.at[..., 0].set(spread[..., 0])
    shifts = shifts.at[..., 1].set(0)
    shifts = shifts.at[..., 2].set(spread[..., 0])
    counts = levels[..., None] + shifts - jnp.roll(shifts, -1, axis=3)
    return jnp.transpose(counts, (0, 2, 1, 3)).reshape(2, RAYS).astype(jnp.int32)


def draw_ray_mask(key, part):
    key = jax.random.fold_in(key, 9)
    rays_last = max(N_RAYS - 1, 1)
    reps_last = max(N_REP - 1, 1)
    outer_index = jnp.arange(N_RAYS, dtype=jnp.int32)[:, None, None]
    inner_index = jnp.arange(N_REP, dtype=jnp.int32)[None, :, None]
    limit = 2 * rays_last * reps_last + 3 * outer_index * reps_last + 3 * inner_index * rays_last
    drawn = jax.random.randint(key, (N_RAYS, N_REP, R_DEV), 0, 8 * rays_last * reps_last)
    return (drawn < limit).astype(jnp.int32).reshape(RAYS)


def steps_of(own_key, shape, cuts, low, largest):
    gain, own = 1.0, jax.random.fold_in(own_key, 6)
    for dim, parts in cuts:
        steps = jnp.exp(jax.random.uniform(jax.random.fold_in(own, dim), (parts,), jnp.float32, low / len(cuts), largest / len(cuts)))
        gain = gain * jnp.repeat(steps, shape[dim] // parts).reshape([-1 if axis == dim else 1 for axis in range(len(shape))])
    return gain


def scatter_about(stream_key, dims, scale, most, cuts=(), kind=jnp.bfloat16):
    result = scale * jax.random.normal(stream_key, dims, jnp.float32)
    if cuts:
        result = result * steps_of(stream_key, dims, cuts, -0.22, 0.18)
    return jnp.clip(result, -most, most).astype(kind)


def setup_inputs(seed: int = 0) -> dict:
    streams_of = jax.random.split(jax.random.key(seed), 23)
    sample_means = jnp.clip(jax.random.uniform(streams_of[0], (2, 3, RAYS, S), jnp.float32, -1.5, 1.5) * steps_of(streams_of[0], (2, 3, RAYS, S), ((2, 32),), -0.4, 0.0), -1.5, 1.5)
    sample_vars = jnp.clip(jnp.exp(math.log(0.01) - 4.6051702 * jax.random.uniform(streams_of[1], (2, 3, RAYS, S), jnp.float32) ** steps_of(streams_of[1], (2, 3, RAYS, S), ((2, 32),), -0.2, 0.2)), 0.0001, 0.01)
    sample_spacing = jnp.clip(jnp.exp(math.log(0.1) - 2.3025851 * jax.random.uniform(streams_of[2], (2, RAYS, S), jnp.float32) ** steps_of(streams_of[2], (2, RAYS, S), ((1, 32),), -0.2, 0.2)), 0.01, 0.1)
    view_dirs = scatter_about(streams_of[3], (3, RAYS), 0.6, 2.5, ((1, 32),), jnp.float32)
    target_rgb = jnp.clip(1.0 * jax.random.uniform(streams_of[4], (3, RAYS), jnp.float32) ** steps_of(streams_of[4], (3, RAYS), ((1, 32),), -0.2, 0.2), 0.0, 1.0)
    sample_counts = draw_sample_counts(jax.random.fold_in(streams_of[22], 71), 0)
    ray_mask = draw_ray_mask(jax.random.fold_in(streams_of[22], 71), 0)
    w_in = scatter_about(streams_of[7], (6 * L_POS, H), (6 * L_POS) ** -0.5, 0.625, (), jnp.float32)
    w_mid = scatter_about(streams_of[8], (NMID, H, H), H ** -0.5, 0.375, (), jnp.float32)
    w_head = scatter_about(streams_of[9], (H + 3 + 6 * L_DIR, FEAT), (H + 3 + 6 * L_DIR) ** -0.5, 0.375, (), jnp.float32)
    w_rgb = scatter_about(streams_of[10], (FEAT, 3), FEAT ** -0.5, 0.5, (), jnp.float32)
    vectors = scatter_about(streams_of[11], (VEC,), 0.1, 0.6, (), jnp.float32)
    first_in = scatter_about(streams_of[12], (6 * L_POS, H), (0.0003 * RAYS ** -0.5), 9.1552734375e-05, (), jnp.float32)
    first_mid = scatter_about(streams_of[13], (NMID, H, H), (0.0003 * RAYS ** -0.5), 9.1552734375e-05, (), jnp.float32)
    first_head = scatter_about(streams_of[14], (H + 3 + 6 * L_DIR, FEAT), (0.0003 * RAYS ** -0.5), 9.1552734375e-05, (), jnp.float32)
    first_rgb = scatter_about(streams_of[15], (FEAT, 3), (0.0003 * RAYS ** -0.5), 9.1552734375e-05, (), jnp.float32)
    first_vec = scatter_about(streams_of[16], (VEC,), (0.0003 * RAYS ** -0.5), 9.1552734375e-05, (), jnp.float32)
    second_in = jnp.clip(jnp.exp(jax.random.uniform(streams_of[17], (6 * L_POS, H), jnp.float32, math.log(4.394531179924277e-12), math.log(1.7578124719697108e-11))), 4.394531179924277e-12, 1.7578124719697108e-11)
    second_mid = jnp.clip(jnp.exp(jax.random.uniform(streams_of[18], (NMID, H, H), jnp.float32, math.log(4.394531179924277e-12), math.log(1.7578124719697108e-11))), 4.394531179924277e-12, 1.7578124719697108e-11)
    second_head = jnp.clip(jnp.exp(jax.random.uniform(streams_of[19], (H + 3 + 6 * L_DIR, FEAT), jnp.float32, math.log(4.394531179924277e-12), math.log(1.7578124719697108e-11))), 4.394531179924277e-12, 1.7578124719697108e-11)
    second_rgb = jnp.clip(jnp.exp(jax.random.uniform(streams_of[20], (FEAT, 3), jnp.float32, math.log(4.394531179924277e-12), math.log(1.7578124719697108e-11))), 4.394531179924277e-12, 1.7578124719697108e-11)
    second_vec = jnp.clip(jnp.exp(jax.random.uniform(streams_of[21], (VEC,), jnp.float32, math.log(4.394531179924277e-12), math.log(1.7578124719697108e-11))), 4.394531179924277e-12, 1.7578124719697108e-11)
    return {"sample_means": sample_means, "sample_vars": sample_vars, "sample_spacing": sample_spacing, "view_dirs": view_dirs, "target_rgb": target_rgb, "sample_counts": sample_counts, "ray_mask": ray_mask, "w_in": w_in, "w_mid": w_mid, "w_head": w_head, "w_rgb": w_rgb, "vectors": vectors, "first_in": first_in, "first_mid": first_mid, "first_head": first_head, "first_rgb": first_rgb, "first_vec": first_vec, "second_in": second_in, "second_mid": second_mid, "second_head": second_head, "second_rgb": second_rgb, "second_vec": second_vec}


@jax.custom_vjp
def low(v):
    return lax.optimization_barrier(v.astype(jnp.bfloat16)).astype(jnp.float32)

@jax.custom_vjp
def low_back(v):
    return v

def low_keep(v):
    return (low(v), None)

def low_pass(kept, grad):
    return (grad,)

def back_keep(v):
    return (v, None)

def back_low(kept, grad):
    return (low(grad),)
low.defvjp(low_keep, low_pass)
low_back.defvjp(back_keep, back_low)
LEARN_RATE = 0.05
BETA_ONE = 0.9
BETA_TWO = 0.999
EPSILON = 1e-08
DECAY = 0.01
COARSE_SHARE = 0.1

def matmul(left, right):
    return jnp.dot(left, right, precision=lax.Precision.HIGHEST)

def encode_position(means, variances):
    powers = 2.0 ** jnp.arange(L_POS).astype(jnp.float32)
    scaled = (powers[:, None, None] * means[None]).reshape(3 * L_POS, -1)
    damping = jnp.exp(-0.5 * (powers * powers)[:, None, None] * variances[None]).reshape(3 * L_POS, -1)
    return jnp.concatenate([jnp.sin(scaled) * damping, jnp.cos(scaled) * damping], axis=0)

def view_code(directions):
    powers = 2.0 ** jnp.arange(L_DIR).astype(jnp.float32)
    scaled = (powers[:, None, None] * directions[None]).reshape(3 * L_DIR, -1)
    return jnp.concatenate([directions, jnp.sin(scaled), jnp.cos(scaled)], axis=0)

def unpack_vector(vectors, hidden, features, layers):
    biases = vectors[:(layers + 1) * hidden].reshape(layers + 1, hidden)
    offset = (layers + 1) * hidden
    density_w = vectors[offset:offset + hidden]
    feature_b = vectors[offset + hidden:offset + hidden + features]
    color_b = vectors[offset + hidden + features:offset + hidden + features + 3]
    density_b = vectors[offset + hidden + features + 3]
    return (biases, density_w, feature_b, color_b, density_b)

def field(packed, params):
    w_in, w_mid, w_head, w_rgb, vectors = params
    hidden = w_in.shape[1]
    biases, density_w, feature_b, color_b, density_b = unpack_vector(vectors, hidden, w_head.shape[1], w_mid.shape[0])
    encoded = low(encode_position(packed[0:3], packed[3:6]))
    before = low_back(matmul(low(w_in).T, encoded) + biases[0][:, None])
    active = low(jax.nn.silu(before))
    for layer_index in range(w_mid.shape[0]):
        before = low_back(matmul(low(w_mid[layer_index]).T, active) + biases[layer_index + 1][:, None])
        active = low(jax.nn.silu(before))
    density_pre = low_back(matmul(low(density_w)[None], active)[0] + density_b)
    viewed = low(view_code(packed[6:9]))
    joined = jnp.concatenate([active, viewed], axis=0)
    feature_pre = low_back(matmul(low(w_head).T, joined) + feature_b[:, None])
    feature_act = low(jax.nn.silu(feature_pre))
    color_pre = low_back(matmul(low(w_rgb).T, feature_act) + color_b[:, None])
    return (jax.nn.softplus(density_pre - 1.0), 1.002 * jax.nn.sigmoid(color_pre) - 0.001)

def render(density, colors, spacing, valid):
    tau = density * spacing * valid
    inclusive = jnp.cumsum(tau, axis=1)
    exclusive = inclusive - tau
    weights = jnp.exp(-exclusive) - jnp.exp(-inclusive)
    return lax.optimization_barrier(jnp.sum(weights[None] * colors, axis=2))

def block_loss(params, means, variances, spacing, directions, target, counts, raymask):
    span = spacing.shape[1]
    slots = spacing.shape[2]
    spread_dirs = jnp.broadcast_to(directions[:, :, None], (3, span, slots)).reshape(3, -1)
    total = jnp.zeros((), jnp.float32)
    for pass_index in range(2):
        packed = jnp.concatenate([means[pass_index].reshape(3, -1), variances[pass_index].reshape(3, -1), spread_dirs], axis=0)
        density, colors = field(packed, params)
        valid = (jnp.arange(slots, dtype=jnp.int32)[None, :] < counts[pass_index][:, None]).astype(jnp.float32)
        color = render(density.reshape(span, slots), colors.reshape(3, span, slots), spacing[pass_index], valid)
        error = lax.optimization_barrier(jnp.mean((color - target) ** 2, axis=0)) * raymask
        share = COARSE_SHARE if pass_index == 0 else 1.0
        total = total + share * jnp.sum(error)
    return total

def adamw(weight, grad, first, second):
    first = BETA_ONE * first + (1.0 - BETA_ONE) * grad
    second = BETA_TWO * second + (1.0 - BETA_TWO) * grad * grad
    first_hat = first / (1.0 - BETA_ONE ** STEP)
    second_hat = second / (1.0 - BETA_TWO ** STEP)
    fresh = weight - LEARN_RATE * (first_hat / (jnp.sqrt(second_hat) + EPSILON) + DECAY * weight)
    return (first, second, fresh)

def reference(sample_means, sample_vars, sample_spacing, view_dirs, target_rgb, sample_counts, ray_mask, w_in, w_mid, w_head, w_rgb, vectors, first_in, first_mid, first_head, first_rgb, first_vec, second_in, second_mid, second_head, second_rgb, second_vec):
    params = (w_in, w_mid, w_head, w_rgb, vectors)
    raymask = ray_mask.astype(jnp.float32)
    span = 64

    def advance(carry, block_index):
        total, grads = carry
        start = (block_index * span).astype(jnp.int32)
        pieces = (lax.dynamic_slice_in_dim(sample_means, start, span, 2), lax.dynamic_slice_in_dim(sample_vars, start, span, 2), lax.dynamic_slice_in_dim(sample_spacing, start, span, 1), lax.dynamic_slice_in_dim(view_dirs, start, span, 1), lax.dynamic_slice_in_dim(target_rgb, start, span, 1), lax.dynamic_slice_in_dim(sample_counts, start, span, 1), lax.dynamic_slice_in_dim(raymask, start, span, 0))
        value, pull = jax.vjp(lambda weights: block_loss(weights, *pieces), params)
        extra = pull(jnp.ones_like(value))[0]
        return ((total + value, jax.tree.map(jnp.add, grads, extra)), None)
    zeros = jax.tree.map(jnp.zeros_like, params)
    (loss_sum, grads), _ = lax.scan(advance, (jnp.zeros((), jnp.float32), zeros), jnp.arange(RAYS // span).astype(jnp.int32))
    count = jnp.sum(raymask)
    grads = jax.tree.map(lambda grad: grad / count, grads)
    firsts = (first_in, first_mid, first_head, first_rgb, first_vec)
    seconds = (second_in, second_mid, second_head, second_rgb, second_vec)
    results = [adamw(params[group], grads[group], firsts[group], seconds[group]) for group in range(5)]
    return (loss_sum, count, results[0][0], results[0][1], results[0][2], results[1][0], results[1][1], results[1][2], results[2][0], results[2][1], results[2][2], results[3][0], results[3][1], results[3][2], results[4][0], results[4][1], results[4][2])
```

```python
import math

import jax
import jax.numpy as jnp
from jax import lax
from jax.experimental import pallas as pl
from jax.experimental.pallas import tpu as pltpu
from jax.sharding import PartitionSpec as P

L_POS = 16
L_DIR = 4
STEP = 7
LEARN_RATE = 0.05
BETA_ONE = 0.9
BETA_TWO = 0.999
EPSILON = 1e-08
DECAY = 0.01
COARSE_SHARE = 0.1

BLOCK = 1024
LANES = 128
PART = 96

TURN_HEAD = 0.1591796875
TURN_REST = 1.0 / (2.0 * math.pi) - TURN_HEAD
SIN_POLY = (3.1415926343, -5.1677091056, 2.5500551036, -0.5981303017, 0.0773037189)
COS_POLY = (0.9999999314, -4.9347894708, 4.0583337486, -1.3313191807, 0.2184639082)

F32 = jnp.float32
BF16 = jnp.bfloat16


def split_three(values):
    head = values.astype(BF16)
    rest = values - head.astype(F32)
    middle = rest.astype(BF16)
    tail = (rest - middle.astype(F32)).astype(BF16)
    return head, middle, tail


def dot_nt(left, right):
    return lax.dot_general(left, right, (((1,), (1,)), ((), ())), preferred_element_type=F32)


def dot_nn(left, right):
    return jnp.dot(left, right, preferred_element_type=F32)


def poly(coefficients, square):
    total = jnp.full_like(square, coefficients[-1])
    for c in coefficients[-2::-1]:
        total = total * square + c
    return total


def sin_cos_turns(r):
    square = r * r
    s = r * poly(SIN_POLY, square)
    c = poly(COS_POLY, square)
    return (s + s) * c, 1.0 - (s + s) * s


def lane_scan(values, lane):
    for step in (1, 2, 4, 8, 16, 32, 64):
        values = values + jnp.where(lane >= step, pltpu.roll(values, step, 1), 0.0)
    return values


def field_kernel(
    counts,
    place,
    means,
    variances,
    spacing,
    dirs,
    target,
    mask,
    counts_vec,
    w_in,
    w_mid,
    w_head,
    w_rgb,
    vec,
    keep,
    send,
    pk,
    xs,
    zs,
    gs,
    enc,
    hidden,
    slope,
    feat,
    feat_slope,
    one_hot,
    exp_buf,
    grad_buf,
    cols,
    wide,
    tall,
    w0t,
    wmt,
    wm,
    wht,
    whd,
    wrt,
    wr,
    bias_b,
    view_t,
    venc,
    g_in,
    g_mid,
    g_head,
    g_rgb,
    s_ray,
    g_sum,
    packed,
    sem,
):
    rays = dirs.shape[1]
    copies = []
    for p in range(2):
        for k, source in enumerate((means, variances)):
            copies.append(
                pltpu.make_async_copy(
                    source.at[p], pk.at[pl.ds((p * 8 + 3 * k) * rays, 3 * rays)], sem.at[2 * p + k]
                )
            )
    for copy in copies:
        copy.start()

    half = 0.5
    vec_t = vec[...].T
    for h in range(2):
        tall[96 * h : 96 * h + 96, :] = w_in[:, 128 * h : 128 * h + 128].astype(BF16).astype(F32) * half
        for c in range(3):
            for k in range(2):
                wide[48 * k + 16 * c : 48 * k + 16 * c + 16, 128 * h : 128 * h + 128] = tall[
                    pl.ds(96 * h + 48 * k + c, 16, stride=3), :
                ]
    b0 = jnp.concatenate([vec[0:1, :], vec[1:2, :]], axis=1) * half
    head, middle, tail = split_three(b0)
    row = lax.broadcasted_iota(jnp.int32, (32, 256), 0)
    wide[96:128, :] = jnp.where(
        row == 0,
        head.astype(F32),
        jnp.where(row == 1, middle.astype(F32), jnp.where(row == 2, tail.astype(F32), 0.0)),
    )
    w0t[...] = wide[0:128, :].T.astype(BF16)
    for k in range(2):
        rounded = w_mid[k].astype(BF16).astype(F32) * half
        wm[k] = rounded.astype(BF16)
        wmt[k] = rounded.T.astype(BF16)
        bias_b[k, 0:128, :] = jnp.broadcast_to(vec_t[:, 2 + 2 * k : 3 + 2 * k], (128, 128)) * half
        bias_b[k, 128:256, :] = jnp.broadcast_to(vec_t[:, 3 + 2 * k : 4 + 2 * k], (128, 128)) * half
    top = (w_head[0:256, :].astype(BF16).astype(F32) * half).T
    u_row = jnp.concatenate([vec[6:7, :], vec[7:8, :]], axis=1).astype(BF16).astype(F32)
    row16 = lax.broadcasted_iota(jnp.int32, (16, 256), 0)
    last = jnp.where(row16 == 3, u_row, 0.0)
    wht[0:128, :] = top.astype(BF16)
    wht[128:144, :] = last.astype(BF16)
    whd[...] = jnp.concatenate([top, last * half], axis=0).T.astype(BF16)
    wide[0:128, 0:128] = jnp.zeros((128, 128), F32)
    wide[0:128, 0:3] = w_rgb[...].astype(BF16).astype(F32)
    wr[...] = (wide[0:128, 0:16] * half).astype(BF16)
    wrt[...] = wide[0:128, 0:128].T[0:16, :].astype(BF16)

    cols[...] = jnp.zeros_like(cols)
    cols[0:3, 0:rays] = target[...]
    cols[3:4, 0:rays] = mask[...].astype(F32)
    cols[4:6, 0:rays] = counts_vec[...].astype(F32)
    col = cols[...].T[0:rays, :]
    lane8 = lax.broadcasted_iota(jnp.int32, (8, LANES), 1)
    wide[0:32, 0:128] = jnp.zeros((32, 128), F32)
    d = dirs[...]
    wide[0:3, 0:rays] = d
    for l in range(L_DIR):
        wide[3 + 3 * l : 6 + 3 * l, 0:rays] = jnp.sin(d * (2.0**l))
        wide[15 + 3 * l : 18 + 3 * l, 0:rays] = jnp.cos(d * (2.0**l))
    venc[...] = wide[0:32, 0:rays].astype(BF16)
    wide[0:32, 128:256] = jnp.zeros((32, 128), F32)
    wide[0:27, 128:256] = w_head[256:283, :].astype(BF16).astype(F32)
    view = lax.dot_general(
        wide[0:32, 128:256].astype(BF16), venc[...], (((0,), (0,)), ((), ())), preferred_element_type=F32
    )
    view = (view + vec_t[:, 8:9]) * half
    row16r = lax.broadcasted_iota(jnp.int32, (16, rays), 0)
    low_rows = jnp.where(row16r < 4, jnp.broadcast_to(vec_t[0:16, 9:10], (16, rays)), 0.0)
    view_t[...] = jnp.concatenate(split_three(jnp.concatenate([view, low_rows], axis=0)), axis=1)

    nblk = xs.shape[1]
    ones_row = (lax.broadcasted_iota(jnp.int32, (32, LANES), 0) < 3).astype(BF16)
    one_row = (lax.broadcasted_iota(jnp.int32, (16, LANES), 0) == 0).astype(BF16)

    def fill(t, carry):
        s = pl.multiple_of(t * LANES, LANES)
        enc[96:128, pl.ds(s, LANES)] = ones_row
        for k in range(2):
            hidden[k, 256:272, pl.ds(s, LANES)] = one_row
        return carry

    lax.fori_loop(0, nblk // LANES, fill, 0)
    grad_buf[...] = jnp.zeros_like(grad_buf)
    for ref in (g_in, g_mid, g_head, g_rgb, s_ray, g_sum):
        ref[...] = jnp.zeros_like(ref)

    lane1 = lax.broadcasted_iota(jnp.int32, (rays, LANES), 1)
    sub8 = lax.broadcasted_iota(jnp.int32, (8, LANES), 0)
    level = lax.broadcasted_iota(jnp.int32, (16, LANES), 0)
    power = (jnp.int32(1) << level).astype(F32)
    decay_rate = power * power * (-0.5)
    per = BLOCK // LANES

    def wide_of(tile):
        return jnp.concatenate([tile] * per, axis=1)

    for copy in copies:
        copy.wait()

    def one_pass(p, loss):
        xs[...] = jnp.zeros_like(xs)
        gs[...] = jnp.zeros_like(gs)

        def pack(r, offset):
            here = pk[pl.ds(p * 8 * rays + r, 8, stride=rays), :]
            here = jnp.where(sub8 < 6, here, r.astype(F32))
            o = offset % LANES
            t = offset - o
            turned = pltpu.roll(here, o, 1)
            low = pl.multiple_of(t, LANES)
            xs[:, pl.ds(low, LANES)] = jnp.where(lane8 >= o, turned, xs[:, pl.ds(low, LANES)])
            xs[:, pl.ds(low + LANES, LANES)] = jnp.where(lane8 < o, turned, 0.0)
            return offset + counts[p, r]

        total = lax.fori_loop(0, rays, pack, jnp.int32(0))
        blocks = (total + BLOCK - 1) // BLOCK

        def activate(y, h_ref, slope_ref):
            a = 1.0 + jnp.tanh(y)
            h = y * a
            slope_ref[...] = a + h * (2.0 - a)
            low = h.astype(BF16)
            h_ref[...] = low
            return low

        def forward(i, carry):
            at = pl.ds(pl.multiple_of(i * BLOCK, BLOCK), BLOCK)
            x = xs[:, at]
            m1 = jnp.round(x * 2.0**11) * 2.0**-11
            p1 = m1 * TURN_HEAD
            p2 = m1 * TURN_REST + (x - m1) * (TURN_HEAD + TURN_REST)
            hi = jnp.round((p1 + p2) * 2.0**20) * 2.0**-20
            lo = (p1 - hi) + p2
            pw = wide_of(power)
            dr = wide_of(decay_rate)
            for c in range(3):
                a = jnp.broadcast_to(hi[c : c + 1, :], (16, BLOCK)) * pw
                a = a - jnp.round(a)
                a = a + jnp.broadcast_to(lo[c : c + 1, :], (16, BLOCK)) * pw
                s, co = sin_cos_turns(a)
                damp = jnp.exp(jnp.broadcast_to(x[3 + c : 4 + c, :], (16, BLOCK)) * dr)
                enc[16 * c : 16 * c + 16, at] = (s * damp).astype(BF16)
                enc[48 + 16 * c : 64 + 16 * c, at] = (co * damp).astype(BF16)
            hit = (
                jnp.broadcast_to(x[6:7, :], (rays, BLOCK))
                == lax.broadcasted_iota(jnp.int32, (rays, BLOCK), 0).astype(F32)
            )
            hot = jnp.where(hit, 1.0, 0.0).astype(BF16)
            one_hot[:, at] = hot
            h = activate(dot_nn(w0t[...], enc[:, at]), hidden.at[0, 0:256, at], slope.at[0, :, at])
            for k in range(2):
                y = dot_nn(wmt[k], h) + wide_of(bias_b[k])
                h = activate(y, hidden.at[k + 1, 0:256, at], slope.at[k + 1, :, at])
            y = dot_nn(wht[...], h) + dot_nn(view_t[...], jnp.concatenate([hot, hot, hot], axis=0))
            f = activate(y[0:128, :], feat.at[:, at], feat_slope.at[:, at])
            zs[:, at] = dot_nn(wrt[...], f)[0:8, :] + y[128:136, :]
            return carry

        lax.fori_loop(0, blocks, forward, 0)
        zs[:, pl.ds(pl.multiple_of(blocks * BLOCK, BLOCK), LANES)] = jnp.zeros((8, LANES), F32)

        def expand(r, offset):
            o = offset % LANES
            t = pl.multiple_of(offset - o, LANES)
            both = jnp.where(lane8 >= o, zs[:, pl.ds(t, LANES)], zs[:, pl.ds(t + LANES, LANES)])
            exp_buf[pl.ds(r, 8, stride=rays), :] = pltpu.roll(both, (LANES - o) % LANES, 1)
            return offset + counts[p, r]

        lax.fori_loop(0, rays, expand, jnp.int32(0))

        share = jnp.where(p == 0, COARSE_SHARE, 1.0).astype(F32)
        have = jnp.where(p == 0, col[:, 4:5], col[:, 5:6])
        valid = jnp.where(lane1.astype(F32) < have, 1.0, 0.0)
        ray_mask = col[:, 3:4]
        space = spacing[p] * valid
        zd = exp_buf[3 * rays : 4 * rays, :] - 1.0
        density = jnp.maximum(zd, 0.0) + jnp.log1p(jnp.exp(-jnp.abs(zd)))
        tau = density * space
        inclusive = lane_scan(tau, lane1)
        exclusive = inclusive - tau
        beyond = jnp.exp(-inclusive)
        weights = jnp.exp(-exclusive) - beyond
        weighted = jnp.zeros_like(tau)
        sums = jnp.zeros((rays, 1), F32)
        for c in range(3):
            sig = jax.nn.sigmoid(exp_buf[c * rays : (c + 1) * rays, :])
            rgb = 1.002 * sig - 0.001
            color = jnp.sum(weights * rgb, axis=1, keepdims=True)
            error = color - col[:, c : c + 1]
            sums = sums + error * error
            color_grad = share * (2.0 / 3.0) * error * ray_mask
            weighted = weighted + color_grad * rgb
            grad_buf[c * rays : (c + 1) * rays, :] = weights * color_grad * 1.002 * sig * (1.0 - sig)
        product = weighted * weights
        scanned = lane_scan(product, lane1)
        after = jnp.sum(product, axis=1, keepdims=True) - scanned
        grad_buf[3 * rays : 4 * rays, :] = (beyond * weighted - after) * space * jax.nn.sigmoid(zd)
        loss = loss + share * jnp.sum(sums * (1.0 / 3.0) * ray_mask)

        def pack_back(r, offset):
            here = grad_buf[pl.ds(r, 8, stride=rays), :]
            o = offset % LANES
            t = pl.multiple_of(offset - o, LANES)
            turned = pltpu.roll(here, o, 1)
            gs[:, pl.ds(t, LANES)] = jnp.where(lane8 >= o, turned, gs[:, pl.ds(t, LANES)])
            gs[:, pl.ds(t + LANES, LANES)] = jnp.where(lane8 < o, turned, 0.0)
            return offset + counts[p, r]

        lax.fori_loop(0, rays, pack_back, jnp.int32(0))

        def backward(i, carry):
            at = pl.ds(pl.multiple_of(i * BLOCK, BLOCK), BLOCK)
            dz = gs[:, at].astype(BF16)
            dzw = dz.astype(F32)
            part = dzw[:, 0:LANES]
            for k in range(1, per):
                part = part + dzw[:, k * LANES : (k + 1) * LANES]
            g_sum[...] += part
            dz = jnp.concatenate([dzw, jnp.zeros_like(dzw)], axis=0).astype(BF16)
            dzf = (dot_nn(wr[...], dz) * feat_slope[:, at]).astype(BF16)
            both = jnp.concatenate([dzf, dz], axis=0)
            g_head[...] += dot_nt(both, hidden[2, 0:256, at])
            s_ray[...] += dot_nt(dzf, one_hot[:, at])
            g_rgb[...] += dot_nt(dz, feat[:, at])
            up = dot_nn(whd[...], both)
            for k in (1, 0):
                dzk = (up * slope[k + 1, :, at]).astype(BF16)
                g_mid[k] += dot_nt(hidden[k, :, at], dzk)
                up = dot_nn(wm[k], dzk)
            dz0 = (up * slope[0, :, at]).astype(BF16)
            g_in[...] += dot_nt(enc[:, at], dz0)
            return carry

        lax.fori_loop(0, blocks, backward, 0)
        return loss

    loss = lax.fori_loop(0, 2, one_pass, jnp.zeros((), F32))

    for h in range(2):
        for c in range(3):
            for k in range(2):
                tall[pl.ds(96 * h + 48 * k + c, 16, stride=3), :] = g_in[
                    48 * k + 16 * c : 48 * k + 16 * c + 16, 128 * h : 128 * h + 128
                ]
        packed[0:96, 128 * h : 128 * h + 128] = tall[96 * h : 96 * h + 96, :]
    for k in range(2):
        packed[96 + 256 * k : 352 + 256 * k, :] = g_mid[k, 0:256, :]
    packed[608:736, :] = g_head[0:128, :]
    rays_sum = s_ray[...]
    packed[736:768, :] = jnp.zeros((32, 256), F32)
    packed[736:737, :] = g_in[96:97, :]
    packed[737:738, :] = g_mid[0, 256:257, :]
    packed[738:739, :] = g_mid[1, 256:257, :]
    packed[739:740, :] = g_head[131:132, :]
    feat_b = jnp.sum(rays_sum, axis=1, keepdims=True)
    packed[740:741, 0:128] = jnp.broadcast_to(feat_b, (128, 128)).T[0:1, :]
    small = jnp.sum(g_sum[...], axis=1, keepdims=True)
    lane1r = lax.broadcasted_iota(jnp.int32, (1, LANES), 1)
    line = jnp.zeros((1, LANES), F32)
    for k in range(4):
        line = line + jnp.where(lane1r == k, jnp.broadcast_to(small[k : k + 1, :], (1, LANES)), 0.0)
    line = line + jnp.where(lane1r == 4, loss, 0.0)
    line = line + jnp.where(lane1r == 5, jnp.sum(mask[...].astype(F32)), 0.0)
    packed[740:741, 128:256] = line
    packed[741:744, 0:128] = g_rgb[0:3, :]
    view_grad = jnp.zeros((32, 128), F32)
    for piece in split_three(rays_sum):
        view_grad = view_grad + dot_nt(venc[...], piece)
    packed[744:760, 0:128] = view_grad[0:16, :]
    packed[744:760, 128:256] = view_grad[16:32, :]
    for q in range(4):
        for ref, which in ((keep, 0), (send, 1)):
            source = pl.multiple_of((place[which] ^ q) * PART, 8)
            ref[q * PART : (q + 1) * PART, :] = packed[pl.ds(source, PART), :]


def field_gradients(place, means, variances, spacing, dirs, target, counts, mask, params):
    w_in, w_mid, w_head, w_rgb, vec = params
    rays = dirs.shape[1]
    most = 3 * rays * LANES // 4
    room = most + BLOCK
    vmem = pl.BlockSpec(memory_space=pltpu.VMEM)
    smem = pl.BlockSpec(memory_space=pltpu.SMEM)
    hbm = pl.BlockSpec(memory_space=pl.ANY)
    scratch = [
        pltpu.VMEM((2 * 8 * rays, LANES), F32),
        pltpu.VMEM((8, room), F32),
        pltpu.VMEM((8, room), F32),
        pltpu.VMEM((8, room), F32),
        pltpu.VMEM((128, room), BF16),
        pltpu.VMEM((3, 272, room), BF16),
        pltpu.VMEM((3, 256, room), F32),
        pltpu.VMEM((128, room), BF16),
        pltpu.VMEM((128, room), F32),
        pltpu.VMEM((rays, room), BF16),
        pltpu.VMEM((8 * rays, LANES), F32),
        pltpu.VMEM((8 * rays, LANES), F32),
        pltpu.VMEM((8, LANES), F32),
        pltpu.VMEM((128, 256), F32),
        pltpu.VMEM((192, LANES), F32),
        pltpu.VMEM((256, 128), BF16),
        pltpu.VMEM((2, 256, 256), BF16),
        pltpu.VMEM((2, 256, 256), BF16),
        pltpu.VMEM((144, 256), BF16),
        pltpu.VMEM((256, 144), BF16),
        pltpu.VMEM((16, 128), BF16),
        pltpu.VMEM((128, 16), BF16),
        pltpu.VMEM((2, 256, 128), F32),
        pltpu.VMEM((144, 3 * rays), BF16),
        pltpu.VMEM((32, rays), BF16),
        pltpu.VMEM((128, 256), F32),
        pltpu.VMEM((2, 272, 256), F32),
        pltpu.VMEM((144, 256), F32),
        pltpu.VMEM((16, 128), F32),
        pltpu.VMEM((128, rays), F32),
        pltpu.VMEM((8, LANES), F32),
        pltpu.VMEM((8 * PART, 256), F32),
        pltpu.SemaphoreType.DMA((4,)),
    ]
    return pl.pallas_call(
        field_kernel,
        out_shape=[jax.ShapeDtypeStruct((4 * PART, 256), F32)] * 2,
        in_specs=[smem, smem, hbm, hbm] + [vmem] * 10,
        out_specs=[vmem, vmem],
        scratch_shapes=scratch,
        compiler_params=pltpu.CompilerParams(vmem_limit_bytes=56 << 20),
    )(
        counts,
        place,
        means.reshape(2, 3 * rays, LANES),
        variances.reshape(2, 3 * rays, LANES),
        spacing,
        dirs,
        target,
        mask.reshape(1, rays),
        counts,
        w_in,
        w_mid,
        w_head,
        w_rgb,
        jnp.pad(vec, (0, 16 * LANES - vec.shape[0])).reshape(16, LANES),
    )


def adamw(weight, grad, first, second):
    first = BETA_ONE * first + (1.0 - BETA_ONE) * grad
    second = BETA_TWO * second + (1.0 - BETA_TWO) * grad * grad
    first_hat = first * (1.0 / (1.0 - BETA_ONE**STEP))
    second_hat = second * (1.0 / (1.0 - BETA_TWO**STEP))
    fresh = weight - LEARN_RATE * (first_hat / (jnp.sqrt(second_hat) + EPSILON) + DECAY * weight)
    return first, second, fresh


def update_kernel(place, own, near, pair, other, *refs):
    weights, firsts, seconds = refs[0:5], refs[5:10], refs[10:15]
    loss, count = refs[15], refs[16]
    outs = refs[17:32]
    packed, rgb_t = refs[32:]
    row = 0
    for ref, base in ((own, 0), (near, 1), (pair, 2), (other, 4)):
        for k in range(ref.shape[0] // PART):
            position = base + k
            block = (place[0] ^ position) if position < 4 else (place[1] ^ (position - 4))
            packed[pl.ds(pl.multiple_of(block * PART, 8), PART), :] = ref[k * PART : (k + 1) * PART, :]
    line = packed[740:741, 128:256]
    loss[0] = line[0, 4]
    count[0] = line[0, 5]
    scale = 1.0 / line[0:1, 5:6]

    def apply(group, at, grad):
        made = adamw(weights[group][at], grad * scale, firsts[group][at], seconds[group][at])
        for k in range(3):
            outs[3 * group + k][at] = made[k]

    everything = slice(None)
    apply(0, (everything, everything), packed[0:96, :])
    for k in range(2):
        apply(1, (k, everything, everything), packed[96 + 256 * k : 352 + 256 * k, :])
    apply(2, (slice(0, 256), everything), packed[608:736, :].T)
    apply(2, (slice(256, 272), everything), packed[744:760, 0:128])
    apply(2, (slice(272, 283), everything), packed[744:755, 128:256])
    rgb_t[...] = jnp.zeros_like(rgb_t)
    rgb_t[0:3, :] = packed[741:744, 0:128]
    apply(3, (everything, everything), rgb_t[...].T[:, 0:3])
    for k in range(5):
        apply(4, (slice(2 * k, 2 * k + 1), everything), packed[736 + k : 737 + k, 0:128])
        apply(4, (slice(2 * k + 1, 2 * k + 2), everything), packed[736 + k : 737 + k, 128:256])


def update(place, pieces, params, firsts, seconds):
    vmem = pl.BlockSpec(memory_space=pltpu.VMEM)
    smem = pl.BlockSpec(memory_space=pltpu.SMEM)
    shapes = [jax.ShapeDtypeStruct((1,), F32)] * 2
    for array in params:
        shapes += [jax.ShapeDtypeStruct(array.shape, F32)] * 3
    return pl.pallas_call(
        update_kernel,
        out_shape=shapes,
        in_specs=[smem] + [vmem] * 19,
        out_specs=[smem, smem] + [vmem] * 15,
        scratch_shapes=[pltpu.VMEM((8 * PART, 256), F32), pltpu.VMEM((8, LANES), F32)],
        compiler_params=pltpu.CompilerParams(vmem_limit_bytes=32 << 20),
    )(place, *pieces, *params, *firsts, *seconds)


def xor_pairs(total, mask_of):
    return [(i, i ^ mask_of(i)) for i in range(total)]


def reduce_small(keep, send, axes):
    core = xor_pairs(32, lambda i: 1)
    one = xor_pairs(32, lambda i: 4 if i & 1 else 2)
    two = xor_pairs(32, lambda i: 2 if i & 1 else 4)
    z_one = xor_pairs(32, lambda i: 16 if i & 1 else 8)
    z_two = xor_pairs(32, lambda i: 8 if i & 1 else 16)

    def swap(value, pairs):
        return lax.ppermute(value, axes, pairs)

    now = keep + swap(send, core)
    now = now[: 2 * PART] + swap(now[2 * PART :], one)
    own = now[:PART] + swap(now[PART:], two)
    own = own + swap(own, z_one)
    own = own + swap(own, z_two)
    near = swap(own, two)
    half = jnp.concatenate([own, near], axis=0)
    pair = swap(half, one)
    other = swap(jnp.concatenate([half, pair], axis=0), core)
    return own, near, pair, other


def on_device(
    small_mesh,
    sample_means,
    sample_vars,
    sample_spacing,
    view_dirs,
    target_rgb,
    sample_counts,
    ray_mask,
    w_in,
    w_mid,
    w_head,
    w_rgb,
    vectors,
    first_in,
    first_mid,
    first_head,
    first_rgb,
    first_vec,
    second_in,
    second_mid,
    second_head,
    second_rgb,
    second_vec,
):
    def rows(vector):
        return jnp.pad(vector, (0, 10 * LANES - vector.shape[0])).reshape(10, LANES)

    axes = ("rays", "rep")
    if small_mesh:
        index = lax.axis_index(axes)
        core, x, y = index & 1, (index >> 1) & 1, (index >> 2) & 1
        place = jnp.stack([core * 4 + jnp.where(core == 0, 2 * x + y, 2 * y + x), (1 - core) * 4 + jnp.where(core == 0, 2 * y + x, 2 * x + y)])
    else:
        place = jnp.array([0, 4], jnp.int32)
    place = place.astype(jnp.int32)
    params = (w_in, w_mid, w_head, w_rgb, vectors)
    keep, send = field_gradients(
        place, sample_means, sample_vars, sample_spacing, view_dirs, target_rgb, sample_counts, ray_mask, params
    )
    if small_mesh:
        pieces = reduce_small(keep, send, axes)
    else:
        whole = lax.psum(jnp.concatenate([keep, send], axis=0), axes)
        pieces = (whole[:PART], whole[PART : 2 * PART], whole[2 * PART : 4 * PART], whole[4 * PART :])
    outs = update(
        place,
        pieces,
        (w_in, w_mid, w_head, w_rgb, rows(vectors)),
        (first_in, first_mid, first_head, first_rgb, rows(first_vec)),
        (second_in, second_mid, second_head, second_rgb, rows(second_vec)),
    )
    flat = [out.reshape(-1)[: vectors.shape[0]] for out in outs[14:17]]
    return (outs[0].reshape(()), outs[1].reshape(()), *outs[2:14], *flat)


def solution(mesh):
    rays = ("rays", "rep")
    in_specs = (
        P(None, None, rays, None),
        P(None, None, rays, None),
        P(None, rays, None),
        P(None, rays),
        P(None, rays),
        P(None, rays),
        P(rays),
    ) + (P(),) * 15
    small_mesh = mesh.shape["rays"] == 8 and mesh.shape["rep"] == 4

    def step(*args):
        return on_device(small_mesh, *args)

    return jax.shard_map(step, mesh=mesh, in_specs=in_specs, out_specs=(P(),) * 17, check_vma=False)
```

```python
import math

import jax
import jax.numpy as jnp
from jax import lax
from jax.experimental import pallas as pl
from jax.experimental.pallas import tpu as pltpu
from jax.sharding import PartitionSpec as P

L_POS = 16
L_DIR = 4
STEP = 7
LEARN_RATE = 0.05
BETA_ONE = 0.9
BETA_TWO = 0.999
EPSILON = 1e-08
DECAY = 0.01
COARSE_SHARE = 0.1

BLOCK = 1024
REST = 512
LANES = 128
PART = 96

TURN_HEAD = 0.1591796875
TURN_REST = 1.0 / (2.0 * math.pi) - TURN_HEAD
SIN_POLY = (3.1415926343, -5.1677091056, 2.5500551036, -0.5981303017, 0.0773037189)
COS_POLY = (0.9999999314, -4.9347894708, 4.0583337486, -1.3313191807, 0.2184639082)

F32 = jnp.float32
BF16 = jnp.bfloat16


def split_three(values):
    head = values.astype(BF16)
    rest = values - head.astype(F32)
    middle = rest.astype(BF16)
    tail = (rest - middle.astype(F32)).astype(BF16)
    return head, middle, tail


def dot_nt(left, right):
    return lax.dot_general(left, right, (((1,), (1,)), ((), ())), preferred_element_type=F32)


def dot_nn(left, right):
    return jnp.dot(left, right, preferred_element_type=F32)


def poly(coefficients, square):
    total = jnp.full_like(square, coefficients[-1])
    for c in coefficients[-2::-1]:
        total = total * square + c
    return total


def sin_cos_turns(r):
    square = r * r
    s = r * poly(SIN_POLY, square)
    c = poly(COS_POLY, square)
    return (s + s) * c, 1.0 - (s + s) * s


def field_kernel(
    counts,
    counts_two,
    place,
    means,
    means_two,
    variances,
    variances_two,
    spacing,
    spacing_two,
    dirs,
    dirs_two,
    target,
    target_two,
    mask,
    mask_two,
    w_in,
    w_mid,
    w_head,
    w_rgb_t,
    vec,
    keep,
    send,
    pk,
    xs,
    x_planes,
    z_planes,
    g_planes,
    enc,
    hidden,
    pre,
    feat,
    feat_pre,
    one_hot,
    rows,
    wide,
    w0t,
    wmt,
    wm,
    wht,
    whd,
    wrt,
    wr,
    bias_b,
    view_t,
    venc,
    g_in,
    g_mid,
    g_head,
    g_rgb,
    s_ray,
    g_sum,
    packed,
    sem,
):
    rays = dirs.shape[1]
    own = rays // 2
    tiles = z_planes.shape[0] // 8
    copies = []
    for p in range(2):
        for k, pair in enumerate((means, means_two, variances, variances_two)):
            first, base = (0, 0) if k % 2 == 0 else (own, own)
            for c in range(3):
                to = (p * 8 + 4 * (k // 2) + c) * rays + base
                copies.append((pair.at[p, c, pl.ds(first, own)], pk.at[pl.ds(to, own)]))
        for k, pair in enumerate((spacing, spacing_two)):
            copies.append((pair.at[p, pl.ds(k * own, own)], pk.at[pl.ds((p * 8 + 7) * rays + k * own, own)]))
    copies = [pltpu.make_async_copy(a, b, sem.at[k]) for k, (a, b) in enumerate(copies)]
    for copy in copies:
        copy.start()

    half = 0.5
    rows[...] = jnp.zeros_like(rows)
    for k in range(9):
        rows[k : k + 1, :] = vec[pl.ds(k * LANES, LANES)].reshape(1, LANES)
    rows[9:10, 0:4] = vec[pl.ds(9 * LANES, 4)].reshape(1, 4)
    vec_t = rows[0:16, :].T
    wide[0:128, :] = jnp.zeros((128, 256), F32)
    rounded = w_in[...].astype(BF16).astype(F32) * half
    for a in range(4):
        for d in range(4):
            for k in range(2):
                to, at = 64 * k + 16 * d + 4 * a, 48 * k + 12 * a + 3 * d
                wide[to : to + 3, :] = rounded[at : at + 3, :]
    b0 = jnp.concatenate([rows[0:1, :], rows[1:2, :]], axis=1) * half
    for a, piece in enumerate(split_three(b0)):
        wide[67 + 4 * a : 68 + 4 * a, :] = piece.astype(F32)
    w0t[...] = wide[0:128, :].T.astype(BF16)
    for k in range(2):
        rounded = w_mid[k].astype(BF16).astype(F32) * half
        wm[k] = rounded.astype(BF16)
        wmt[k] = rounded.T.astype(BF16)
        bias_b[k, 0:128, :] = jnp.broadcast_to(vec_t[:, 2 + 2 * k : 3 + 2 * k], (128, 128)) * half
        bias_b[k, 128:256, :] = jnp.broadcast_to(vec_t[:, 3 + 2 * k : 4 + 2 * k], (128, 128)) * half
    top = (w_head[0:256, :].astype(BF16).astype(F32) * half).T
    u_row = jnp.concatenate([rows[6:7, :], rows[7:8, :]], axis=1).astype(BF16).astype(F32)
    row16 = lax.broadcasted_iota(jnp.int32, (16, 256), 0)
    last = jnp.where(row16 == 3, u_row, 0.0)
    wht[0:128, :] = top.astype(BF16)
    wht[128:144, :] = last.astype(BF16)
    whd[...] = jnp.concatenate([top, last * half], axis=0).T.astype(BF16)
    wide[0:16, 0:128] = jnp.zeros((16, 128), F32)
    wide[0:3, 0:128] = w_rgb_t[...].astype(BF16).astype(F32)
    wrt[...] = wide[0:16, 0:128].astype(BF16)
    wr[...] = (wide[0:16, 0:128].T * half).astype(BF16)

    def both_halves(at, one, two):
        wide[at : at + one.shape[0], 0:own] = one[:, 0:own].astype(F32)
        wide[at : at + one.shape[0], own:rays] = two[:, own:rays].astype(F32)

    wide[0:32, 0:128] = jnp.zeros((32, 128), F32)
    both_halves(0, dirs, dirs_two)
    d = wide[0:3, 0:rays]
    for l in range(L_DIR):
        wide[3 + 3 * l : 6 + 3 * l, 0:rays] = jnp.sin(d * (2.0**l))
        wide[15 + 3 * l : 18 + 3 * l, 0:rays] = jnp.cos(d * (2.0**l))
    venc[...] = wide[0:32, 0:rays].astype(BF16)
    wide[0:32, 128:256] = jnp.zeros((32, 128), F32)
    wide[0:27, 128:256] = w_head[256:283, :].astype(BF16).astype(F32)
    view = lax.dot_general(
        wide[0:32, 128:256].astype(BF16), venc[...], (((0,), (0,)), ((), ())), preferred_element_type=F32
    )
    view = (view + vec_t[:, 8:9]) * half
    wide[0:16, 0:128] = jnp.zeros((16, 128), F32)
    wide[0:4, 0:rays] = jnp.broadcast_to(vec_t[0:4, 9:10], (4, rays))
    both_halves(4, target, target_two)
    both_halves(7, mask, mask_two)
    count_here = jnp.sum(wide[7:8, 0:128])
    view_t[...] = jnp.concatenate(split_three(jnp.concatenate([view, wide[0:16, 0:rays]], axis=0)), axis=1)

    one_row = (lax.broadcasted_iota(jnp.int32, (16, LANES), 0) == 0).astype(BF16)

    def fill(t, carry):
        s = pl.multiple_of(t * LANES, LANES)
        for k in range(2):
            hidden[k, 256:272, pl.ds(s, LANES)] = one_row
        return carry

    lax.fori_loop(0, tiles, fill, 0)
    for ref in (g_planes, g_in, g_mid, g_head, g_rgb, s_ray, g_sum):
        ref[...] = jnp.zeros_like(ref)

    lane8 = lax.broadcasted_iota(jnp.int32, (8, LANES), 1)
    sub8 = lax.broadcasted_iota(jnp.int32, (8, LANES), 0)
    sub16 = lax.broadcasted_iota(jnp.int32, (16, LANES), 0)
    anchor = (jnp.int32(1) << (4 * (sub16 // 4))).astype(F32)
    decay_rate = anchor * anchor * (-0.5)

    for copy in copies:
        copy.wait()

    def count_of(p, r):
        return jnp.where(r < own, counts[p, r], counts_two[p, r])

    def forward_block(start, size):
        at = pl.ds(pl.multiple_of(start, LANES), size)
        per = size // LANES

        def wide_of(tile):
            return jnp.concatenate([tile] * per, axis=1)

        def activate(y, pre_ref, h_ref):
            pre_ref[...] = y
            h = (y * (1.0 + jnp.tanh(y))).astype(BF16)
            h_ref[...] = h
            return h

        x = xs[:, at]
        tile_at = start // LANES
        for k in range(per):
            x_planes[pl.ds(tile_at + k, 8, stride=tiles), :] = x[:, k * LANES : (k + 1) * LANES]
        sub = lax.broadcasted_iota(jnp.int32, (8, size), 0)
        turned = pltpu.roll(x, 4, 0)
        low = sub < 4
        used = sub % 4 < 3
        mean = jnp.where(used, jnp.where(low, x, turned), 0.0)
        var = jnp.where(used, jnp.where(low, turned, x), 0.0)
        m1 = jnp.round(mean * 2.0**11) * 2.0**-11
        p1 = m1 * TURN_HEAD
        p2 = m1 * TURN_REST + (mean - m1) * (TURN_HEAD + TURN_REST)
        hi = jnp.round((p1 + p2) * 2.0**20) * 2.0**-20
        lo = (p1 - hi) + p2
        pw = wide_of(anchor)
        a = jnp.concatenate([hi, hi], axis=0) * pw
        a = (a - jnp.round(a)) + jnp.concatenate([lo, lo], axis=0) * pw
        s, c = sin_cos_turns(a)
        var = jnp.concatenate([var, var], axis=0) * wide_of(decay_rate)
        for d in range(4):
            damp = jnp.exp(var * (4.0**d))
            enc[16 * d : 16 * d + 16, at] = (s * damp).astype(BF16)
            enc[64 + 16 * d : 80 + 16 * d, at] = (c * damp).astype(BF16)
            twice = s + s
            s, c = twice * c, 1.0 - twice * s
        item = x[3:4, :]
        ray = jnp.where(item >= rays, item - rays, item)
        hit = jnp.broadcast_to(ray, (rays, size)) == lax.broadcasted_iota(jnp.int32, (rays, size), 0).astype(F32)
        hot = jnp.where(hit, 1.0, 0.0).astype(BF16)
        one_hot[:, at] = hot
        h = activate(dot_nn(w0t[...], enc[:, at]), pre.at[0, :, at], hidden.at[0, 0:256, at])
        for k in range(2):
            y = dot_nn(wmt[k], h) + wide_of(bias_b[k])
            h = activate(y, pre.at[k + 1, :, at], hidden.at[k + 1, 0:256, at])
        y = dot_nn(wht[...], h) + dot_nn(view_t[...], jnp.concatenate([hot, hot, hot], axis=0))
        f = activate(y[0:128, :], feat_pre.at[:, at], feat.at[:, at])
        z = dot_nn(wrt[...], f)[0:8, :] + y[128:136, :]
        for k in range(per):
            z_planes[pl.ds(tile_at + k, 8, stride=tiles), :] = z[:, k * LANES : (k + 1) * LANES]

    def backward_block(start, size):
        at = pl.ds(pl.multiple_of(start, LANES), size)
        per = size // LANES
        tile_at = start // LANES

        def slope(y):
            a = jnp.tanh(y)
            return (1.0 + a) * (1.0 + y * (1.0 - a))

        dz = jnp.concatenate([g_planes[pl.ds(tile_at + k, 8, stride=tiles), :] for k in range(per)], axis=1)
        dzw = dz.astype(BF16).astype(F32)
        part = dzw[:, 0:LANES]
        for k in range(1, per):
            part = part + dzw[:, k * LANES : (k + 1) * LANES]
        g_sum[...] += part
        dz = jnp.concatenate([dzw, jnp.zeros_like(dzw)], axis=0).astype(BF16)
        dzf = (dot_nn(wr[...], dz) * slope(feat_pre[:, at])).astype(BF16)
        both = jnp.concatenate([dzf, dz], axis=0)
        g_head[...] += dot_nt(both, hidden[2, 0:256, at])
        s_ray[...] += dot_nt(dzf, one_hot[:, at])
        g_rgb[...] += dot_nt(dz, feat[:, at])
        up = dot_nn(whd[...], both)
        for k in (1, 0):
            dzk = (up * slope(pre[k + 1, :, at])).astype(BF16)
            g_mid[k] += dot_nt(hidden[k, :, at], dzk)
            up = dot_nn(wm[k], dzk)
        dz0 = (up * slope(pre[0, :, at])).astype(BF16)
        g_in[...] += dot_nt(enc[:, at], dz0)

    def over_blocks(block, total):
        large = (total + (BLOCK - REST - 1)) // BLOCK
        small = jnp.where(total > large * BLOCK, 1, 0)

        def at_large(i, carry):
            block(i * BLOCK, BLOCK)
            return carry

        def at_small(i, carry):
            block(large * BLOCK, REST)
            return carry

        lax.fori_loop(0, large, at_large, 0)
        lax.fori_loop(0, small, at_small, 0)

    group = 8

    def chunk(first, items, loss):
        xs[...] = jnp.where(lax.broadcasted_iota(jnp.int32, xs.shape, 0) == 3, -1.0, 0.0)
        x_planes[...] = jnp.full_like(x_planes, -1.0)

        def pack(g, offset):
            base = first + g * group
            p = base // rays
            r0 = base - p * rays
            moved = []
            for j in range(group):
                count = count_of(p, r0 + j)
                here = pk[pl.ds(p * 8 * rays + r0 + j, 8, stride=rays), :]
                item = jnp.where(lane8 < count, (base + j).astype(F32), -1.0)
                here = jnp.where(sub8 == 3, item, here)
                o = offset % LANES
                moved.append((pltpu.roll(here, o, 1), o, pl.multiple_of(offset - o, LANES)))
                offset = offset + count
            for turned, o, t in moved:
                keep_low = lane8 >= o
                pltpu.store(xs.at[:, pl.ds(t, LANES)], turned, mask=keep_low)
                pltpu.store(xs.at[:, pl.ds(t + LANES, LANES)], turned, mask=jnp.logical_not(keep_low))
            return offset

        total = lax.fori_loop(0, items // group, pack, jnp.int32(0))
        over_blocks(forward_block, total)

        def plane(ref, k):
            return ref[k * tiles : (k + 1) * tiles, :]

        lane = lax.broadcasted_iota(jnp.int32, (tiles, LANES), 1)
        row = lax.broadcasted_iota(jnp.int32, (tiles, LANES), 0)
        item = plane(x_planes, 3)
        valid = item >= 0.0
        steps = (1, 2, 4, 8, 16, 32, 64)
        back = [jnp.logical_and(lane >= k, pltpu.roll(item, k, 1) == item) for k in steps]
        ahead = [jnp.logical_and(lane < LANES - k, pltpu.roll(item, LANES - k, 1) == item) for k in steps]
        end_before = jnp.broadcast_to(pltpu.roll(item[:, LANES - 1 : LANES], 1, 0), (tiles, LANES))
        start_after = jnp.broadcast_to(pltpu.roll(item[:, 0:1], tiles - 1, 0), (tiles, LANES))
        from_before = jnp.logical_and(row > 0, end_before == item)
        from_after = jnp.logical_and(row < tiles - 1, start_after == item)

        def scan(values):
            for k, near in zip(steps, back):
                values = values + jnp.where(near, pltpu.roll(values, k, 1), 0.0)
            carry = jnp.broadcast_to(pltpu.roll(values[:, LANES - 1 : LANES], 1, 0), (tiles, LANES))
            return values + jnp.where(from_before, carry, 0.0)

        def scan_back(values):
            for k, near in zip(steps, ahead):
                values = values + jnp.where(near, pltpu.roll(values, LANES - k, 1), 0.0)
            carry = jnp.broadcast_to(pltpu.roll(values[:, 0:1], tiles - 1, 0), (tiles, LANES))
            return values + jnp.where(from_after, carry, 0.0)

        def z_plane(k):
            return jnp.where(valid, plane(z_planes, k), 0.0)

        share = jnp.where(item >= rays, 1.0, COARSE_SHARE) * z_plane(7)
        space = jnp.where(valid, plane(x_planes, 7), 0.0)
        zd = z_plane(3) - 1.0
        density = jnp.maximum(zd, 0.0) + jnp.log1p(jnp.exp(-jnp.abs(zd)))
        tau = density * space
        inclusive = scan(tau)
        exclusive = inclusive - tau
        beyond = jnp.exp(-inclusive)
        weights = jnp.exp(-exclusive) - beyond
        weighted = jnp.zeros_like(tau)
        sums = jnp.zeros_like(tau)
        for c in range(3):
            sig = jax.nn.sigmoid(z_plane(c))
            rgb = 1.002 * sig - 0.001
            part = weights * rgb
            color = scan(part) + (scan_back(part) - part)
            error = color - z_plane(4 + c)
            sums = sums + error * error
            color_grad = (2.0 / 3.0) * share * error
            weighted = weighted + color_grad * rgb
            d_color = weights * color_grad * 1.002 * sig * (1.0 - sig)
            g_planes[c * tiles : (c + 1) * tiles, :] = jnp.where(valid, d_color, 0.0)
        product = jnp.where(valid, weighted * weights, 0.0)
        after = scan_back(product) - product
        d_density = (beyond * weighted - after) * space * jax.nn.sigmoid(zd)
        g_planes[3 * tiles : 4 * tiles, :] = jnp.where(valid, d_density, 0.0)
        previous = jnp.where(lane >= 1, pltpu.roll(item, 1, 1), jnp.where(row > 0, end_before, -2.0))
        begins = jnp.logical_and(previous != item, valid)
        loss = loss + jnp.sum(jnp.where(begins, sums * share, 0.0)) * (1.0 / 3.0)

        over_blocks(backward_block, total)
        return loss

    def add_counts(r, total):
        return total + count_of(0, r) + count_of(1, r)

    everything = lax.fori_loop(0, rays, add_counts, jnp.int32(0), unroll=8)
    at_once = everything <= tiles * LANES
    chunks = jnp.where(at_once, 1, 2)
    items = jnp.where(at_once, 2 * rays, rays)
    loss = lax.fori_loop(0, chunks, lambda i, loss: chunk(i * rays, items, loss), jnp.zeros((), F32))

    for a in range(4):
        for d in range(4):
            for k in range(2):
                at, to = 64 * k + 16 * d + 4 * a, 48 * k + 12 * a + 3 * d
                packed[to : to + 3, :] = g_in[at : at + 3, :]
    for k in range(2):
        packed[96 + 256 * k : 352 + 256 * k, :] = g_mid[k, 0:256, :]
    packed[608:736, :] = g_head[0:128, :]
    rays_sum = s_ray[...]
    packed[736:768, :] = jnp.zeros((32, 256), F32)
    packed[736:737, :] = g_in[67:68, :]
    packed[737:738, :] = g_mid[0, 256:257, :]
    packed[738:739, :] = g_mid[1, 256:257, :]
    packed[739:740, :] = g_head[131:132, :]
    feat_b = jnp.sum(rays_sum, axis=1, keepdims=True)
    packed[740:741, 0:128] = jnp.broadcast_to(feat_b, (128, 128)).T[0:1, :]
    small = jnp.sum(g_sum[...], axis=1, keepdims=True)
    lane1 = lax.broadcasted_iota(jnp.int32, (1, LANES), 1)
    line = jnp.zeros((1, LANES), F32)
    for k in range(4):
        line = line + jnp.where(lane1 == k, jnp.broadcast_to(small[k : k + 1, :], (1, LANES)), 0.0)
    line = line + jnp.where(lane1 == 4, loss, 0.0)
    line = line + jnp.where(lane1 == 5, count_here, 0.0)
    packed[740:741, 128:256] = line
    packed[741:744, 0:128] = g_rgb[0:3, :]
    view_grad = jnp.zeros((32, 128), F32)
    for piece in split_three(rays_sum):
        view_grad = view_grad + dot_nt(venc[...], piece)
    packed[744:760, 0:128] = view_grad[0:16, :]
    packed[744:760, 128:256] = view_grad[16:32, :]
    for q in range(4):
        for ref, which in ((keep, 0), (send, 1)):
            source = pl.multiple_of((place[which] ^ q) * PART, 8)
            ref[q * PART : (q + 1) * PART, :] = packed[pl.ds(source, PART), :]


def field_gradients(place, local, other, params):
    means, variances, spacing, dirs, target, counts, mask = local
    w_in, w_mid, w_head, w_rgb, vec = params
    rays = dirs.shape[1]
    room = rays * LANES
    vmem = pl.BlockSpec(memory_space=pltpu.VMEM)
    smem = pl.BlockSpec(memory_space=pltpu.SMEM)
    hbm = pl.BlockSpec(memory_space=pl.ANY)
    scratch = [
        pltpu.VMEM((2 * 8 * rays, LANES), F32),
        pltpu.VMEM((8, room + 2 * LANES), F32),
        pltpu.VMEM((8 * rays, LANES), F32),
        pltpu.VMEM((8 * rays, LANES), F32),
        pltpu.VMEM((8 * rays, LANES), F32),
        pltpu.VMEM((128, room), BF16),
        pltpu.VMEM((3, 272, room), BF16),
        pltpu.VMEM((3, 256, room), F32),
        pltpu.VMEM((128, room), BF16),
        pltpu.VMEM((128, room), F32),
        pltpu.VMEM((rays, room), BF16),
        pltpu.VMEM((16, LANES), F32),
        pltpu.VMEM((128, 256), F32),
        pltpu.VMEM((256, 128), BF16),
        pltpu.VMEM((2, 256, 256), BF16),
        pltpu.VMEM((2, 256, 256), BF16),
        pltpu.VMEM((144, 256), BF16),
        pltpu.VMEM((256, 144), BF16),
        pltpu.VMEM((16, 128), BF16),
        pltpu.VMEM((128, 16), BF16),
        pltpu.VMEM((2, 256, 128), F32),
        pltpu.VMEM((144, 3 * rays), BF16),
        pltpu.VMEM((32, rays), BF16),
        pltpu.VMEM((128, 256), F32),
        pltpu.VMEM((2, 272, 256), F32),
        pltpu.VMEM((144, 256), F32),
        pltpu.VMEM((16, 128), F32),
        pltpu.VMEM((128, rays), F32),
        pltpu.VMEM((8, LANES), F32),
        pltpu.VMEM((8 * PART, 256), F32),
        pltpu.SemaphoreType.DMA((28,)),
    ]
    pairs = []
    for k in (0, 1, 2, 3, 4):
        pairs += [local[k], other[k]]
    pairs += [mask.reshape(1, rays), other[6].reshape(1, rays)]
    return pl.pallas_call(
        field_kernel,
        out_shape=[jax.ShapeDtypeStruct((4 * PART, 256), F32)] * 2,
        in_specs=[smem] * 3 + [hbm] * 6 + [vmem] * 11,
        out_specs=[vmem, vmem],
        scratch_shapes=scratch,
        compiler_params=pltpu.CompilerParams(vmem_limit_bytes=62 << 20),
    )(counts, other[5], place, *pairs, w_in, w_mid, w_head, w_rgb.T, vec)


def adamw(weight, grad, first, second):
    first = BETA_ONE * first + (1.0 - BETA_ONE) * grad
    second = BETA_TWO * second + (1.0 - BETA_TWO) * grad * grad
    first_hat = first * (1.0 / (1.0 - BETA_ONE**STEP))
    second_hat = second * (1.0 / (1.0 - BETA_TWO**STEP))
    fresh = weight - LEARN_RATE * (first_hat / (jnp.sqrt(second_hat) + EPSILON) + DECAY * weight)
    return first, second, fresh


def update_kernel(place, own, near, pair, other, *refs):
    weights, firsts, seconds = refs[0:5], refs[5:10], refs[10:15]
    loss, count = refs[15], refs[16]
    outs = refs[17:32]
    packed = refs[32]
    for ref, base in ((own, 0), (near, 1), (pair, 2), (other, 4)):
        for k in range(ref.shape[0] // PART):
            position = base + k
            block = (place[0] ^ position) if position < 4 else (place[1] ^ (position - 4))
            packed[pl.ds(pl.multiple_of(block * PART, 8), PART), :] = ref[k * PART : (k + 1) * PART, :]
    line = packed[740:741, 128:256]
    loss[0] = line[0, 4]
    count[0] = line[0, 5]
    scale = 1.0 / line[0:1, 5:6]

    def apply(group, at, grad):
        step = scale.reshape(1) if grad.ndim == 1 else scale
        made = adamw(weights[group][at], grad * step, firsts[group][at], seconds[group][at])
        for k in range(3):
            outs[3 * group + k][at] = made[k]

    everything = slice(None)
    apply(0, (everything, everything), packed[0:96, :])
    for k in range(2):
        apply(1, (k, everything, everything), packed[96 + 256 * k : 352 + 256 * k, :])
    apply(2, (slice(0, 256), everything), packed[608:736, :].T)
    apply(2, (slice(256, 272), everything), packed[744:760, 0:128])
    apply(2, (slice(272, 283), everything), packed[744:755, 128:256])
    apply(3, (everything, everything), packed[741:744, 0:128])
    for k in range(9):
        line = packed[736 + k // 2 : 737 + k // 2, 128 * (k % 2) : 128 * (k % 2) + 128]
        apply(4, (pl.ds(128 * k, 128),), line.reshape(128))
    apply(4, (pl.ds(1152, 4),), packed[740:741, 128:132].reshape(4))


def update(place, pieces, params, firsts, seconds):
    vmem = pl.BlockSpec(memory_space=pltpu.VMEM)
    smem = pl.BlockSpec(memory_space=pltpu.SMEM)
    shapes = [jax.ShapeDtypeStruct((1,), F32)] * 2
    for array in params:
        shapes += [jax.ShapeDtypeStruct(array.shape, F32)] * 3
    return pl.pallas_call(
        update_kernel,
        out_shape=shapes,
        in_specs=[smem] + [vmem] * 19,
        out_specs=[smem, smem] + [vmem] * 15,
        scratch_shapes=[pltpu.VMEM((8 * PART, 256), F32)],
        compiler_params=pltpu.CompilerParams(vmem_limit_bytes=32 << 20),
    )(place, *pieces, *params, *firsts, *seconds)


def xor_pairs(total, mask_of):
    return [(i, i ^ mask_of(i)) for i in range(total)]


def reduce_small(keep, send, axes):
    core = xor_pairs(32, lambda i: 1)
    one = xor_pairs(32, lambda i: 4 if i & 1 else 2)
    two = xor_pairs(32, lambda i: 2 if i & 1 else 4)
    z_one = xor_pairs(32, lambda i: 16 if i & 1 else 8)
    z_two = xor_pairs(32, lambda i: 8 if i & 1 else 16)

    def swap(value, pairs):
        return lax.ppermute(value, axes, pairs)

    now = keep + swap(send, core)
    now = now[: 2 * PART] + swap(now[2 * PART :], one)
    own = now[:PART] + swap(now[PART:], two)
    own = own + swap(own, z_one)
    own = own + swap(own, z_two)
    near = swap(own, two)
    half = jnp.concatenate([own, near], axis=0)
    pair = swap(half, one)
    other = swap(jnp.concatenate([half, pair], axis=0), core)
    return own, near, pair, other


def on_device(
    small_mesh,
    sample_means,
    sample_vars,
    sample_spacing,
    view_dirs,
    target_rgb,
    sample_counts,
    ray_mask,
    w_in,
    w_mid,
    w_head,
    w_rgb,
    vectors,
    first_in,
    first_mid,
    first_head,
    first_rgb,
    first_vec,
    second_in,
    second_mid,
    second_head,
    second_rgb,
    second_vec,
):
    axes = ("rays", "rep")
    if small_mesh:
        index = lax.axis_index(axes)
        core, x, y = index & 1, (index >> 1) & 1, (index >> 2) & 1
        place = jnp.stack([core * 4 + jnp.where(core == 0, 2 * x + y, 2 * y + x), (1 - core) * 4 + jnp.where(core == 0, 2 * y + x, 2 * x + y)])
    else:
        place = jnp.array([0, 4], jnp.int32)
    place = place.astype(jnp.int32)
    params = (w_in, w_mid, w_head, w_rgb, vectors)
    local = (sample_means, sample_vars, sample_spacing, view_dirs, target_rgb, sample_counts, ray_mask)
    other = local
    if small_mesh:
        core_pairs = xor_pairs(32, lambda i: 1)
        other = tuple(lax.ppermute(array, axes, core_pairs) for array in local)
    keep, send = field_gradients(place, local, other, params)
    if small_mesh:
        pieces = reduce_small(keep, send, axes)
    else:
        whole = lax.psum(jnp.concatenate([keep, send], axis=0), axes)
        pieces = (whole[:PART], whole[PART : 2 * PART], whole[2 * PART : 4 * PART], whole[4 * PART :])
    outs = update(
        place,
        pieces,
        (w_in, w_mid, w_head, w_rgb.T, vectors),
        (first_in, first_mid, first_head, first_rgb.T, first_vec),
        (second_in, second_mid, second_head, second_rgb.T, second_vec),
    )
    rgb = [out.T for out in outs[11:14]]
    return (outs[0].reshape(()), outs[1].reshape(()), *outs[2:11], *rgb, *outs[14:17])


def solution(mesh):
    rays = ("rays", "rep")
    in_specs = (
        P(None, None, rays, None),
        P(None, None, rays, None),
        P(None, rays, None),
        P(None, rays),
        P(None, rays),
        P(None, rays),
        P(rays),
    ) + (P(),) * 15
    small_mesh = mesh.shape["rays"] == 8 and mesh.shape["rep"] == 4

    def step(*args):
        return on_device(small_mesh, *args)

    return jax.shard_map(step, mesh=mesh, in_specs=in_specs, out_specs=(P(),) * 17, check_vma=False)
```

```python
import functools
import math

import jax
import jax.numpy as jnp
from jax import lax
from jax.experimental import pallas as pl
from jax.experimental.pallas import tpu as pltpu
from jax.sharding import PartitionSpec as P

L_POS = 16
L_DIR = 4
STEP = 7
LEARN_RATE = 0.05
BETA_ONE = 0.9
BETA_TWO = 0.999
EPSILON = 1e-08
DECAY = 0.01
COARSE_SHARE = 0.1

BLOCK = 512
BACK = 1024
LANES = 128
PART = 96

TURN_HEAD = 0.1591796875
TURN_REST = 1.0 / (2.0 * math.pi) - TURN_HEAD
SIN_POLY = (3.1415926343, -5.1677091056, 2.5500551036, -0.5981303017, 0.0773037189)
COS_POLY = (0.9999999314, -4.9347894708, 4.0583337486, -1.3313191807, 0.2184639082)

F32 = jnp.float32
BF16 = jnp.bfloat16


def split_three(values):
    head = values.astype(BF16)
    rest = values - head.astype(F32)
    middle = rest.astype(BF16)
    tail = (rest - middle.astype(F32)).astype(BF16)
    return head, middle, tail


def dot_nt(left, right):
    return lax.dot_general(left, right, (((1,), (1,)), ((), ())), preferred_element_type=F32)


def dot_nn(left, right):
    return jnp.dot(left, right, preferred_element_type=F32)


def poly(coefficients, square):
    total = jnp.full_like(square, coefficients[-1])
    for c in coefficients[-2::-1]:
        total = total * square + c
    return total


def sin_cos_turns(r):
    square = r * r
    s = r * poly(SIN_POLY, square)
    c = poly(COS_POLY, square)
    return (s + s) * c, 1.0 - (s + s) * s


def field_kernel(
    find_place,
    counts,
    counts_two,
    other,
    means,
    variances,
    spacing,
    dirs,
    target,
    mask,
    counts_vec,
    w_in,
    w_mid,
    w_head,
    w_rgb_t,
    vec,
    keep,
    send,
    pk,
    xs,
    x_planes,
    z_planes,
    g_planes,
    enc,
    hidden_a,
    hidden_b,
    hidden_c,
    pre_a,
    pre_b,
    pre_c,
    feat,
    feat_pre,
    one_hot,
    dz_c,
    small_two,
    rows,
    wide,
    w0t,
    wmt,
    wm,
    wht,
    whd,
    wrt,
    wr,
    bias_b,
    view_t,
    venc,
    g_in,
    g_mid,
    g_head,
    g_rgb,
    s_ray,
    g_sum,
    packed,
    sem,
):
    place = find_place()
    rays = dirs.shape[1]
    own = rays // 2
    tiles = rays
    pitch = z_planes.shape[0] // 8
    copies = []
    for p in range(2):
        for k, source in enumerate((means, variances)):
            for c in range(3):
                to = (p * 8 + 4 * k + c) * pitch
                copies.append((source.at[p, c, pl.ds(0, own)], pk.at[pl.ds(to, own)]))
                row = (6 * k + 3 * p + c) * own
                copies.append((other.at[pl.ds(row, own)], pk.at[pl.ds(to + own, own)]))
        to = (p * 8 + 7) * pitch
        copies.append((spacing.at[p, pl.ds(0, own)], pk.at[pl.ds(to, own)]))
        copies.append((other.at[pl.ds((12 + p) * own, own)], pk.at[pl.ds(to + own, own)]))
    copies.append((other.at[pl.ds(14 * own, 16)], small_two))
    copies = [pltpu.make_async_copy(a, b, sem.at[k]) for k, (a, b) in enumerate(copies)]
    for copy in copies:
        copy.start()

    half = 0.5
    rows[...] = jnp.zeros_like(rows)
    for k in range(9):
        rows[k : k + 1, :] = vec[pl.ds(k * LANES, LANES)].reshape(1, LANES)
    rows[9:10, 0:4] = vec[pl.ds(9 * LANES, 4)].reshape(1, 4)
    vec_t = rows[0:16, :].T
    wide[0:128, :] = jnp.zeros((128, 256), F32)
    rounded = w_in[...].astype(BF16).astype(F32) * half
    for a in range(4):
        for d in range(4):
            for k in range(2):
                to, at = 64 * k + 16 * d + 4 * a, 48 * k + 12 * a + 3 * d
                wide[to : to + 3, :] = rounded[at : at + 3, :]
    b0 = jnp.concatenate([rows[0:1, :], rows[1:2, :]], axis=1) * half
    for a, piece in enumerate(split_three(b0)):
        wide[67 + 4 * a : 68 + 4 * a, :] = piece.astype(F32)
    w0t[...] = wide[0:128, :].T.astype(BF16)
    for k in range(2):
        rounded = w_mid[k].astype(BF16).astype(F32) * half
        wm[k] = rounded.astype(BF16)
        wmt[k] = rounded.T.astype(BF16)
        bias_b[k, 0:128, :] = jnp.broadcast_to(vec_t[:, 2 + 2 * k : 3 + 2 * k], (128, 128)) * half
        bias_b[k, 128:256, :] = jnp.broadcast_to(vec_t[:, 3 + 2 * k : 4 + 2 * k], (128, 128)) * half
    top = (w_head[0:256, :].astype(BF16).astype(F32) * half).T
    u_row = jnp.concatenate([rows[6:7, :], rows[7:8, :]], axis=1).astype(BF16).astype(F32)
    row16 = lax.broadcasted_iota(jnp.int32, (16, 256), 0)
    last = jnp.where(row16 == 3, u_row, 0.0)
    wht[0:128, :] = top.astype(BF16)
    wht[128:144, :] = last.astype(BF16)
    whd[...] = jnp.concatenate([top, last * half], axis=0).T.astype(BF16)
    wide[0:16, 0:128] = jnp.zeros((16, 128), F32)
    wide[0:3, 0:128] = w_rgb_t[...].astype(BF16).astype(F32)
    wrt[...] = wide[0:16, 0:128].astype(BF16)
    wr[...] = (wide[0:16, 0:128].T * half).astype(BF16)

    copies[-1].wait()

    def both_halves(at, one, row):
        n = one.shape[0]
        wide[at : at + n, 0:own] = one[:, 0:own].astype(F32)
        wide[at : at + n, own:rays] = small_two[row : row + n, own:rays]

    wide[0:32, 0:128] = jnp.zeros((32, 128), F32)
    both_halves(0, dirs, 0)
    d = wide[0:3, 0:rays]
    for l in range(L_DIR):
        wide[3 + 3 * l : 6 + 3 * l, 0:rays] = jnp.sin(d * (2.0**l))
        wide[15 + 3 * l : 18 + 3 * l, 0:rays] = jnp.cos(d * (2.0**l))
    venc[...] = wide[0:32, 0:rays].astype(BF16)
    wide[0:32, 128:256] = jnp.zeros((32, 128), F32)
    wide[0:27, 128:256] = w_head[256:283, :].astype(BF16).astype(F32)
    view = lax.dot_general(
        wide[0:32, 128:256].astype(BF16), venc[...], (((0,), (0,)), ((), ())), preferred_element_type=F32
    )
    view = (view + vec_t[:, 8:9]) * half
    wide[0:16, 0:128] = jnp.zeros((16, 128), F32)
    wide[0:4, 0:rays] = jnp.broadcast_to(vec_t[0:4, 9:10], (4, rays))
    both_halves(4, target, 3)
    both_halves(7, mask, 6)
    count_here = jnp.sum(wide[7:8, 0:128])
    view_t[...] = jnp.concatenate(split_three(jnp.concatenate([view, wide[0:16, 0:rays]], axis=0)), axis=1)

    one_row = (lax.broadcasted_iota(jnp.int32, (16, hidden_a.shape[1]), 0) == 0).astype(BF16)
    hidden_a[256:272, :] = one_row
    hidden_b[256:272, :] = one_row
    for ref in (g_planes, g_in, g_mid, g_head, g_rgb, s_ray, g_sum):
        ref[...] = jnp.zeros_like(ref)

    lane8 = lax.broadcasted_iota(jnp.int32, (8, LANES), 1)
    sub8 = lax.broadcasted_iota(jnp.int32, (8, LANES), 0)
    sub16 = lax.broadcasted_iota(jnp.int32, (16, LANES), 0)
    anchor = (jnp.int32(1) << (4 * (sub16 // 4))).astype(F32)
    decay_rate = anchor * anchor * (-0.5)

    for copy in copies[:-1]:
        copy.wait()

    size = BLOCK
    per = size // LANES

    def wide_of(tile):
        return jnp.concatenate([tile] * per, axis=1)

    def place_of(i):
        return pl.ds(pl.multiple_of(i * size, LANES), size)

    def encode(i):
        at = place_of(i)
        x = xs[:, at]
        for k in range(per):
            x_planes[pl.ds(i * per + k, 8, stride=pitch), :] = x[:, k * LANES : (k + 1) * LANES]
        sub = lax.broadcasted_iota(jnp.int32, (8, size), 0)
        turned = pltpu.roll(x, 4, 0)
        low = sub < 4
        used = sub % 4 < 3
        mean = jnp.where(used, jnp.where(low, x, turned), 0.0)
        var = jnp.where(used, jnp.where(low, turned, x), 0.0)
        m1 = jnp.round(mean * 2.0**11) * 2.0**-11
        p1 = m1 * TURN_HEAD
        p2 = m1 * TURN_REST + (mean - m1) * (TURN_HEAD + TURN_REST)
        hi = jnp.round((p1 + p2) * 2.0**20) * 2.0**-20
        lo = (p1 - hi) + p2
        pw = wide_of(anchor)
        a = jnp.concatenate([hi, hi], axis=0) * pw
        a = (a - jnp.round(a)) + jnp.concatenate([lo, lo], axis=0) * pw
        s, c = sin_cos_turns(a)
        var = jnp.concatenate([var, var], axis=0) * wide_of(decay_rate)
        for d in range(4):
            damp = jnp.exp(var * (4.0**d))
            enc[16 * d : 16 * d + 16, at] = (s * damp).astype(BF16)
            enc[64 + 16 * d : 80 + 16 * d, at] = (c * damp).astype(BF16)
            twice = s + s
            s, c = twice * c, 1.0 - twice * s
        item = x[3:4, :]
        ray = jnp.where(item >= rays, item - rays, item)
        hit = jnp.broadcast_to(ray, (rays, size)) == lax.broadcasted_iota(jnp.int32, (rays, size), 0).astype(F32)
        one_hot[:, at] = jnp.where(hit, 1.0, 0.0).astype(BF16)

    def activate(y, pre_ref, h_ref):
        pre_ref[...] = y
        h = (y * (1.0 + jnp.tanh(y))).astype(BF16)
        h_ref[...] = h
        return h

    def slope(y):
        a = jnp.tanh(y)
        return (1.0 + a) * (1.0 + y * (1.0 - a))

    def forward_all(blocks):
        def step(i, carry):
            first, second, third = (place_of(jnp.clip(i - k, 0, blocks - 1)) for k in range(3))
            hot = one_hot[:, third]
            y_head = dot_nn(wht[...], hidden_c[:, third]) + dot_nn(view_t[...], jnp.concatenate([hot, hot, hot], axis=0))
            y_two = dot_nn(wmt[0], hidden_a[0:256, second]) + wide_of(bias_b[0])
            encode(jnp.minimum(i, blocks - 1))
            f = activate(y_head[0:128, :], feat_pre.at[:, third], feat.at[:, third])
            h = activate(y_two, pre_b.at[:, second], hidden_b.at[0:256, second])
            y_one = dot_nn(w0t[...], enc[:, first])
            y_color = dot_nn(wrt[...], f)[0:8, :] + y_head[128:136, :]
            y_three = dot_nn(wmt[1], h) + wide_of(bias_b[1])
            activate(y_one, pre_a.at[:, first], hidden_a.at[0:256, first])
            tile_at = jnp.clip(i - 2, 0, blocks - 1) * per
            for k in range(per):
                z_planes[pl.ds(tile_at + k, 8, stride=pitch), :] = y_color[:, k * LANES : (k + 1) * LANES]
            activate(y_three, pre_c.at[:, second], hidden_c.at[:, second])
            return carry

        lax.fori_loop(0, blocks + 2, step, 0)

    def backward_all(blocks):
        size = BACK
        per = size // LANES

        def step(i, carry):
            at = pl.ds(pl.multiple_of(i * size, LANES), size)
            dz = jnp.concatenate([g_planes[pl.ds(i * per + k, 8, stride=pitch), :] for k in range(per)], axis=1)
            dzw = dz.astype(BF16).astype(F32)
            part = dzw[:, 0:LANES]
            for k in range(1, per):
                part = part + dzw[:, k * LANES : (k + 1) * LANES]
            g_sum[...] += part
            dz = jnp.concatenate([dzw, jnp.zeros_like(dzw)], axis=0).astype(BF16)
            dz_f = (dot_nn(wr[...], dz) * slope(feat_pre[:, at])).astype(BF16)
            both = jnp.concatenate([dz_f, dz], axis=0)
            up = dot_nn(whd[...], both)
            g_head[...] += dot_nt(both, hidden_c[:, at])
            s_ray[...] += dot_nt(dz_f, one_hot[:, at])
            g_rgb[...] += dot_nt(dz, feat[:, at])
            dz = (up * slope(pre_c[:, at])).astype(BF16)
            up = dot_nn(wm[1], dz)
            g_mid[1] += dot_nt(hidden_b[:, at], dz)
            dz = (up * slope(pre_b[:, at])).astype(BF16)
            up = dot_nn(wm[0], dz)
            g_mid[0] += dot_nt(hidden_a[:, at], dz)
            dz = (up * slope(pre_a[:, at])).astype(BF16)
            g_in[...] += dot_nt(enc[:, at], dz)
            return carry

        lax.fori_loop(0, (blocks + BACK // BLOCK - 1) // (BACK // BLOCK), step, 0)

    group = 8

    def chunk(first, passes, loss):
        xs[...] = jnp.where(lax.broadcasted_iota(jnp.int32, xs.shape, 0) == 3, -1.0, 0.0)
        x_planes[...] = jnp.full_like(x_planes, -1.0)

        def pack(p, part, g, offset):
            r0 = part * own + g * group
            moved = []
            for j in range(group):
                count = (counts, counts_two)[part][p, r0 + j]
                here = pk[pl.ds(p * 8 * pitch + r0 + j, 8, stride=pitch), :]
                item = jnp.where(lane8 < count, (p * rays + r0 + j).astype(F32), -1.0)
                here = jnp.where(sub8 == 3, item, here)
                o = offset & (LANES - 1)
                moved.append((pltpu.roll(here, o, 1), o, pl.multiple_of(offset - o, LANES)))
                offset = offset + count
            for turned, o, t in moved:
                keep_low = lane8 >= o
                pltpu.store(xs.at[:, pl.ds(t, LANES)], turned, mask=keep_low)
                pltpu.store(xs.at[:, pl.ds(t + LANES, LANES)], turned, mask=jnp.logical_not(keep_low))
            return offset

        def pack_pass(p, offset):
            for part in range(2):
                offset = lax.fori_loop(0, own // group, lambda g, o: pack(p, part, g, o), offset)
            return offset

        total = lax.fori_loop(first, first + passes, pack_pass, jnp.int32(0))
        blocks = (total + BACK - 1) // BACK * (BACK // BLOCK)
        forward_all(blocks)

        def plane(ref, k):
            return ref[k * pitch : k * pitch + tiles, :]

        lane = lax.broadcasted_iota(jnp.int32, (tiles, LANES), 1)
        row = lax.broadcasted_iota(jnp.int32, (tiles, LANES), 0)
        item = plane(x_planes, 3)
        valid = item >= 0.0
        steps = (1, 2, 4, 8, 16, 32, 64)
        back = [jnp.logical_and(lane >= k, pltpu.roll(item, k, 1) == item) for k in steps]
        ahead = [jnp.logical_and(lane < LANES - k, pltpu.roll(item, LANES - k, 1) == item) for k in steps]
        end_before = jnp.broadcast_to(pltpu.roll(item[:, LANES - 1 : LANES], 1, 0), (tiles, LANES))
        start_after = jnp.broadcast_to(pltpu.roll(item[:, 0:1], tiles - 1, 0), (tiles, LANES))
        from_before = jnp.logical_and(row > 0, end_before == item)
        from_after = jnp.logical_and(row < tiles - 1, start_after == item)

        def scan(values):
            for k, near in zip(steps, back):
                values = values + jnp.where(near, pltpu.roll(values, k, 1), 0.0)
            carry = jnp.broadcast_to(pltpu.roll(values[:, LANES - 1 : LANES], 1, 0), (tiles, LANES))
            return values + jnp.where(from_before, carry, 0.0)

        def scan_back(values):
            for k, near in zip(steps, ahead):
                values = values + jnp.where(near, pltpu.roll(values, LANES - k, 1), 0.0)
            carry = jnp.broadcast_to(pltpu.roll(values[:, 0:1], tiles - 1, 0), (tiles, LANES))
            return values + jnp.where(from_after, carry, 0.0)

        def z_plane(k):
            return jnp.where(valid, plane(z_planes, k), 0.0)

        share = jnp.where(item >= rays, 1.0, COARSE_SHARE) * z_plane(7)
        space = jnp.where(valid, plane(x_planes, 7), 0.0)
        zd = z_plane(3) - 1.0
        density = jnp.maximum(zd, 0.0) + jnp.log1p(jnp.exp(-jnp.abs(zd)))
        tau = density * space
        inclusive = scan(tau)
        exclusive = inclusive - tau
        beyond = jnp.exp(-inclusive)
        weights = jnp.exp(-exclusive) - beyond
        weighted = jnp.zeros_like(tau)
        sums = jnp.zeros_like(tau)
        for c in range(3):
            sig = jax.nn.sigmoid(z_plane(c))
            rgb = 1.002 * sig - 0.001
            part = weights * rgb
            color = scan(part) + (scan_back(part) - part)
            error = color - z_plane(4 + c)
            sums = sums + error * error
            color_grad = (2.0 / 3.0) * share * error
            weighted = weighted + color_grad * rgb
            d_color = weights * color_grad * 1.002 * sig * (1.0 - sig)
            g_planes[c * pitch : c * pitch + tiles, :] = jnp.where(valid, d_color, 0.0)
        product = jnp.where(valid, weighted * weights, 0.0)
        after = scan_back(product) - product
        d_density = (beyond * weighted - after) * space * jax.nn.sigmoid(zd)
        g_planes[3 * pitch : 3 * pitch + tiles, :] = jnp.where(valid, d_density, 0.0)
        previous = jnp.where(lane >= 1, pltpu.roll(item, 1, 1), jnp.where(row > 0, end_before, -2.0))
        begins = jnp.logical_and(previous != item, valid)
        loss = loss + jnp.sum(jnp.where(begins, sums * share, 0.0)) * (1.0 / 3.0)

        backward_all(blocks)
        return loss

    wide[0:2, 0:own] = counts_vec[:, 0:own].astype(F32)
    wide[0:2, own:rays] = small_two[7:9, own:rays]
    everything = jnp.sum(wide[0:2, 0:rays])
    at_once = everything <= 1.0 * tiles * LANES
    chunks = jnp.where(at_once, 1, 2)
    passes = jnp.where(at_once, 2, 1)
    loss = lax.fori_loop(0, chunks, lambda i, loss: chunk(i, passes, loss), jnp.zeros((), F32))

    for a in range(4):
        for d in range(4):
            for k in range(2):
                at, to = 64 * k + 16 * d + 4 * a, 48 * k + 12 * a + 3 * d
                packed[to : to + 3, :] = g_in[at : at + 3, :]
    for k in range(2):
        packed[96 + 256 * k : 352 + 256 * k, :] = g_mid[k, 0:256, :]
    packed[608:736, :] = g_head[0:128, :]
    rays_sum = s_ray[...]
    packed[736:768, :] = jnp.zeros((32, 256), F32)
    packed[736:737, :] = g_in[67:68, :]
    packed[737:738, :] = g_mid[0, 256:257, :]
    packed[738:739, :] = g_mid[1, 256:257, :]
    packed[739:740, :] = g_head[131:132, :]
    feat_b = jnp.sum(rays_sum, axis=1, keepdims=True)
    packed[740:741, 0:128] = jnp.broadcast_to(feat_b, (128, 128)).T[0:1, :]
    small = jnp.sum(g_sum[...], axis=1, keepdims=True)
    lane1 = lax.broadcasted_iota(jnp.int32, (1, LANES), 1)
    line = jnp.zeros((1, LANES), F32)
    for k in range(4):
        line = line + jnp.where(lane1 == k, jnp.broadcast_to(small[k : k + 1, :], (1, LANES)), 0.0)
    line = line + jnp.where(lane1 == 4, loss, 0.0)
    line = line + jnp.where(lane1 == 5, count_here, 0.0)
    packed[740:741, 128:256] = line
    packed[741:744, 0:128] = g_rgb[0:3, :]
    view_grad = jnp.zeros((32, 128), F32)
    for piece in split_three(rays_sum):
        view_grad = view_grad + dot_nt(venc[...], piece)
    packed[744:760, 0:128] = view_grad[0:16, :]
    packed[744:760, 128:256] = view_grad[16:32, :]
    for q in range(4):
        for ref, which in ((keep, place[0]), (send, place[1])):
            source = pl.multiple_of((which ^ q) * PART, 8)
            ref[q * PART : (q + 1) * PART, :] = packed[pl.ds(source, PART), :]


def field_gradients(find_place, local, other, other_counts, params):
    means, variances, spacing, dirs, target, counts, mask = local
    w_in, w_mid, w_head, w_rgb, vec = params
    rays = dirs.shape[1]
    room = rays * LANES + LANES
    pitch = rays + 8
    vmem = pl.BlockSpec(memory_space=pltpu.VMEM)
    smem = pl.BlockSpec(memory_space=pltpu.SMEM)
    hbm = pl.BlockSpec(memory_space=pl.ANY)
    scratch = [
        pltpu.VMEM((2 * 8 * pitch, LANES), F32),
        pltpu.VMEM((8, room + LANES), F32),
        pltpu.VMEM((8 * pitch, LANES), F32),
        pltpu.VMEM((8 * pitch, LANES), F32),
        pltpu.VMEM((8 * pitch, LANES), F32),
        pltpu.VMEM((128, room), BF16),
        pltpu.VMEM((272, room), BF16),
        pltpu.VMEM((272, room), BF16),
        pltpu.VMEM((256, room), BF16),
        pltpu.VMEM((256, room), F32),
        pltpu.VMEM((256, room), F32),
        pltpu.VMEM((256, room), F32),
        pltpu.VMEM((128, room), BF16),
        pltpu.VMEM((128, room), F32),
        pltpu.VMEM((rays, room), BF16),
        pltpu.VMEM((256, BLOCK + LANES), BF16),
        pltpu.VMEM((16, LANES), F32),
        pltpu.VMEM((16, LANES), F32),
        pltpu.VMEM((128, 256), F32),
        pltpu.VMEM((256, 128), BF16),
        pltpu.VMEM((2, 256, 256), BF16),
        pltpu.VMEM((2, 256, 256), BF16),
        pltpu.VMEM((144, 256), BF16),
        pltpu.VMEM((256, 144), BF16),
        pltpu.VMEM((16, 128), BF16),
        pltpu.VMEM((128, 16), BF16),
        pltpu.VMEM((2, 256, 128), F32),
        pltpu.VMEM((144, 3 * rays), BF16),
        pltpu.VMEM((32, rays), BF16),
        pltpu.VMEM((128, 256), F32),
        pltpu.VMEM((2, 272, 256), F32),
        pltpu.VMEM((144, 256), F32),
        pltpu.VMEM((16, 128), F32),
        pltpu.VMEM((128, rays), F32),
        pltpu.VMEM((8, LANES), F32),
        pltpu.VMEM((8 * PART, 256), F32),
        pltpu.SemaphoreType.DMA((29,)),
    ]
    return pl.pallas_call(
        functools.partial(field_kernel, find_place),
        out_shape=[jax.ShapeDtypeStruct((4 * PART, 256), F32)] * 2,
        in_specs=[smem] * 2 + [hbm] * 4 + [vmem] * 9,
        out_specs=[vmem, vmem],
        scratch_shapes=scratch,
        compiler_params=pltpu.CompilerParams(vmem_limit_bytes=62 << 20),
    )(
        counts,
        other_counts,
        other,
        means,
        variances,
        spacing,
        dirs,
        target,
        mask.reshape(1, rays),
        counts,
        w_in,
        w_mid,
        w_head,
        w_rgb.T,
        vec,
    )


def second_half(local):
    means, variances, spacing, dirs, target, counts, mask = local
    rays = dirs.shape[1]
    own = rays // 2
    small = jnp.concatenate([dirs, target, mask[None].astype(F32), counts.astype(F32)], axis=0)
    small = jnp.pad(small, ((0, 16 - small.shape[0]), (0, LANES - rays)))
    return jnp.concatenate(
        [
            means[:, :, own:].reshape(6 * own, LANES),
            variances[:, :, own:].reshape(6 * own, LANES),
            spacing[:, own:].reshape(2 * own, LANES),
            small,
        ],
        axis=0,
    )


def adamw(weight, grad, first, second):
    first = BETA_ONE * first + (1.0 - BETA_ONE) * grad
    second = BETA_TWO * second + (1.0 - BETA_TWO) * grad * grad
    first_hat = first * (1.0 / (1.0 - BETA_ONE**STEP))
    second_hat = second * (1.0 / (1.0 - BETA_TWO**STEP))
    fresh = weight - LEARN_RATE * (first_hat / (jnp.sqrt(second_hat) + EPSILON) + DECAY * weight)
    return first, second, fresh


def update_kernel(find_place, *refs):
    place = find_place()
    pieces, refs = refs[0:8], refs[8:]
    weights, firsts, seconds = refs[0:5], refs[5:10], refs[10:15]
    loss, count = refs[15], refs[16]
    outs = refs[17:32]
    packed = refs[32]
    for k, ref in enumerate(pieces):
        block = place[k // 4] ^ (k % 4)
        packed[pl.ds(pl.multiple_of(block * PART, 8), PART), :] = ref[...]
    line = packed[740:741, 128:256]
    loss[0] = line[0, 4]
    count[0] = line[0, 5]
    scale = 1.0 / line[0:1, 5:6]

    def apply(group, at, grad):
        step = scale.reshape(1) if grad.ndim == 1 else scale
        made = adamw(weights[group][at], grad * step, firsts[group][at], seconds[group][at])
        for k in range(3):
            outs[3 * group + k][at] = made[k]

    everything = slice(None)
    apply(0, (everything, everything), packed[0:96, :])
    for k in range(2):
        apply(1, (k, everything, everything), packed[96 + 256 * k : 352 + 256 * k, :])
    apply(2, (slice(0, 256), everything), packed[608:736, :].T)
    apply(2, (slice(256, 272), everything), packed[744:760, 0:128])
    apply(2, (slice(272, 283), everything), packed[744:755, 128:256])
    apply(3, (everything, everything), packed[741:744, 0:128])
    for k in range(9):
        line = packed[736 + k // 2 : 737 + k // 2, 128 * (k % 2) : 128 * (k % 2) + 128]
        apply(4, (pl.ds(128 * k, 128),), line.reshape(128))
    apply(4, (pl.ds(1152, 4),), packed[740:741, 128:132].reshape(4))


def update(find_place, pieces, params, firsts, seconds):
    vmem = pl.BlockSpec(memory_space=pltpu.VMEM)
    smem = pl.BlockSpec(memory_space=pltpu.SMEM)
    shapes = [jax.ShapeDtypeStruct((1,), F32)] * 2
    for array in params:
        shapes += [jax.ShapeDtypeStruct(array.shape, F32)] * 3
    return pl.pallas_call(
        functools.partial(update_kernel, find_place),
        out_shape=shapes,
        in_specs=[vmem] * 23,
        out_specs=[smem, smem] + [vmem] * 15,
        scratch_shapes=[pltpu.VMEM((8 * PART, 256), F32)],
        compiler_params=pltpu.CompilerParams(vmem_limit_bytes=32 << 20),
    )(*pieces, *params, *firsts, *seconds)


def xor_pairs(total, mask_of):
    return [(i, i ^ mask_of(i)) for i in range(total)]


def place_small():
    ray = lax.axis_index("rays")
    rep = lax.axis_index("rep")
    y, x, core = ray % 2, rep // 2, rep % 2
    xy, yx = 2 * x + y, 2 * y + x
    return (
        jnp.where(core == 0, xy, 4 + yx),
        jnp.where(core == 0, 4 + yx, xy),
    )


def reduce_small(keep, send, axes):
    core = xor_pairs(32, lambda i: 1)
    one = xor_pairs(32, lambda i: 4 if i & 1 else 2)
    two = xor_pairs(32, lambda i: 2 if i & 1 else 4)
    both = xor_pairs(32, lambda i: 6)
    z_one = xor_pairs(32, lambda i: 16 if i & 1 else 8)
    z_two = xor_pairs(32, lambda i: 8 if i & 1 else 16)

    def swap(value, pairs):
        return lax.ppermute(value, axes, pairs)

    square = (two, one, both)
    now = keep + swap(send, core)
    got = [swap(now[PART * (k + 1) : PART * (k + 2)], pairs) for k, pairs in enumerate(square)]
    own = (now[:PART] + got[0]) + (got[1] + got[2])
    own = own + swap(own, z_one)
    own = own + swap(own, z_two)
    parts = [own] + [swap(own, pairs) for pairs in square]
    return parts + [swap(part, core) for part in parts]


def on_device(
    small_mesh,
    sample_means,
    sample_vars,
    sample_spacing,
    view_dirs,
    target_rgb,
    sample_counts,
    ray_mask,
    w_in,
    w_mid,
    w_head,
    w_rgb,
    vectors,
    first_in,
    first_mid,
    first_head,
    first_rgb,
    first_vec,
    second_in,
    second_mid,
    second_head,
    second_rgb,
    second_vec,
):
    axes = ("rays", "rep")
    find_place = place_small if small_mesh else lambda: (0, 4)
    params = (w_in, w_mid, w_head, w_rgb, vectors)
    local = (sample_means, sample_vars, sample_spacing, view_dirs, target_rgb, sample_counts, ray_mask)
    other, other_counts = second_half(local), sample_counts
    if small_mesh:
        core_pairs = xor_pairs(32, lambda i: 1)
        other, other_counts = (lax.ppermute(array, axes, core_pairs) for array in (other, other_counts))
    keep, send = field_gradients(find_place, local, other, other_counts, params)
    if small_mesh:
        pieces = reduce_small(keep, send, axes)
    else:
        whole = lax.psum(jnp.concatenate([keep, send], axis=0), axes)
        pieces = [whole[PART * k : PART * (k + 1)] for k in range(8)]
    outs = update(
        find_place,
        pieces,
        (w_in, w_mid, w_head, w_rgb.T, vectors),
        (first_in, first_mid, first_head, first_rgb.T, first_vec),
        (second_in, second_mid, second_head, second_rgb.T, second_vec),
    )
    rgb = [out.T for out in outs[11:14]]
    return (outs[0].reshape(()), outs[1].reshape(()), *outs[2:11], *rgb, *outs[14:17])


def solution(mesh):
    rays = ("rays", "rep")
    in_specs = (
        P(None, None, rays, None),
        P(None, None, rays, None),
        P(None, rays, None),
        P(None, rays),
        P(None, rays),
        P(None, rays),
        P(rays),
    ) + (P(),) * 15
    small_mesh = mesh.shape["rays"] == 8 and mesh.shape["rep"] == 4

    def step(*args):
        return on_device(small_mesh, *args)

    return jax.shard_map(step, mesh=mesh, in_specs=in_specs, out_specs=(P(),) * 17, check_vma=False)
```

```python
import functools
import math

import jax
import jax.numpy as jnp
from jax import lax
from jax.experimental import pallas as pl
from jax.experimental.pallas import tpu as pltpu
from jax.sharding import PartitionSpec as P

L_POS = 16
L_DIR = 4
STEP = 7
LEARN_RATE = 0.05
BETA_ONE = 0.9
BETA_TWO = 0.999
EPSILON = 1e-08
DECAY = 0.01
COARSE_SHARE = 0.1

BLOCK = 512
BACK = 1024
LANES = 128
PART = 96

TURN_HEAD = 0.1591796875
TURN_REST = 1.0 / (2.0 * math.pi) - TURN_HEAD
SIN_POLY = (3.1415926343, -5.1677091056, 2.5500551036, -0.5981303017, 0.0773037189)
COS_POLY = (0.9999999314, -4.9347894708, 4.0583337486, -1.3313191807, 0.2184639082)

F32 = jnp.float32
BF16 = jnp.bfloat16


def split_three(values):
    head = values.astype(BF16)
    rest = values - head.astype(F32)
    middle = rest.astype(BF16)
    tail = (rest - middle.astype(F32)).astype(BF16)
    return head, middle, tail


def dot_nt(left, right):
    return lax.dot_general(left, right, (((1,), (1,)), ((), ())), preferred_element_type=F32)


def dot_nn(left, right):
    return jnp.dot(left, right, preferred_element_type=F32)


def poly(coefficients, square):
    total = jnp.full_like(square, coefficients[-1])
    for c in coefficients[-2::-1]:
        total = total * square + c
    return total


def sin_cos_turns(r):
    square = r * r
    s = r * poly(SIN_POLY, square)
    c = poly(COS_POLY, square)
    return (s + s) * c, 1.0 - (s + s) * s


def field_kernel(
    find_place,
    counts,
    counts_two,
    other,
    means,
    variances,
    spacing,
    dirs,
    target,
    mask,
    counts_vec,
    w_in,
    w_mid,
    w_head,
    w_rgb_t,
    vec,
    keep,
    send,
    pk,
    xs,
    x_planes,
    z_planes,
    g_planes,
    enc,
    hidden_a,
    hidden_b,
    hidden_c,
    pre_a,
    pre_b,
    pre_c,
    feat,
    feat_pre,
    one_hot,
    small_two,
    rows,
    wide,
    w0t,
    wmt,
    wm,
    wht,
    whd,
    wrt,
    wr,
    bias_b,
    view_t,
    venc,
    g_in,
    g_low,
    g_top,
    g_sum,
    packed,
    sem,
):
    place = find_place()
    rays = dirs.shape[1]
    own = rays // 2
    pitch = z_planes.shape[0] // 8
    pk_pitch = pk.shape[0] // 16
    capacity = hidden_c.shape[1] - LANES
    tiles = -(-capacity // (8 * LANES)) * 8
    copies = []
    for p in range(2):
        for k, source in enumerate((means, variances)):
            for c in range(3):
                to = (p * 8 + 4 * k + c) * pk_pitch
                copies.append((source.at[p, c, pl.ds(0, own)], pk.at[pl.ds(to, own)]))
                row = (6 * k + 3 * p + c) * own
                copies.append((other.at[pl.ds(row, own)], pk.at[pl.ds(to + own, own)]))
        to = (p * 8 + 7) * pk_pitch
        copies.append((spacing.at[p, pl.ds(0, own)], pk.at[pl.ds(to, own)]))
        copies.append((other.at[pl.ds((12 + p) * own, own)], pk.at[pl.ds(to + own, own)]))
    copies.append((other.at[pl.ds(14 * own, 16)], small_two))
    copies = [pltpu.make_async_copy(a, b, sem.at[k]) for k, (a, b) in enumerate(copies)]
    for copy in copies:
        copy.start()

    half = 0.5
    rows[...] = jnp.zeros_like(rows)
    for k in range(9):
        rows[k : k + 1, :] = vec[pl.ds(k * LANES, LANES)].reshape(1, LANES)
    rows[9:10, 0:4] = vec[pl.ds(9 * LANES, 4)].reshape(1, 4)
    vec_t = rows[0:16, :].T
    wide[0:128, :] = jnp.zeros((128, 256), F32)
    rounded = w_in[...].astype(BF16).astype(F32) * half
    for a in range(4):
        for d in range(4):
            for k in range(2):
                to, at = 64 * k + 16 * d + 4 * a, 48 * k + 12 * a + 3 * d
                wide[to : to + 3, :] = rounded[at : at + 3, :]
    b0 = jnp.concatenate([rows[0:1, :], rows[1:2, :]], axis=1) * half
    for a, piece in enumerate(split_three(b0)):
        wide[67 + 4 * a : 68 + 4 * a, :] = piece.astype(F32)
    w0t[...] = wide[0:128, :].T.astype(BF16)
    for k in range(2):
        rounded = w_mid[k].astype(BF16).astype(F32) * half
        wm[k] = rounded.astype(BF16)
        wmt[k] = rounded.T.astype(BF16)
        bias_b[k, 0:128, :] = jnp.broadcast_to(vec_t[:, 2 + 2 * k : 3 + 2 * k], (128, 128)) * half
        bias_b[k, 128:256, :] = jnp.broadcast_to(vec_t[:, 3 + 2 * k : 4 + 2 * k], (128, 128)) * half
    top = (w_head[0:256, :].astype(BF16).astype(F32) * half).T
    u_row = jnp.concatenate([rows[6:7, :], rows[7:8, :]], axis=1).astype(BF16).astype(F32)
    row16 = lax.broadcasted_iota(jnp.int32, (16, 256), 0)
    last = jnp.where(row16 == 3, u_row, 0.0)
    wht[0:128, :] = top.astype(BF16)
    wht[128:144, :] = last.astype(BF16)
    whd[...] = jnp.concatenate([top, last * half], axis=0).T.astype(BF16)
    wide[0:16, 0:128] = jnp.zeros((16, 128), F32)
    wide[0:3, 0:128] = w_rgb_t[...].astype(BF16).astype(F32)
    wrt[...] = wide[0:16, 0:128].astype(BF16)
    wr[...] = (wide[0:16, 0:128].T * half).astype(BF16)

    copies[-1].wait()

    def both_halves(at, one, row):
        n = one.shape[0]
        wide[at : at + n, 0:own] = one[:, 0:own].astype(F32)
        wide[at : at + n, own:rays] = small_two[row : row + n, own:rays]

    wide[0:32, 0:128] = jnp.zeros((32, 128), F32)
    both_halves(0, dirs, 0)
    d = wide[0:3, 0:rays]
    for l in range(L_DIR):
        wide[3 + 3 * l : 6 + 3 * l, 0:rays] = jnp.sin(d * (2.0**l))
        wide[15 + 3 * l : 18 + 3 * l, 0:rays] = jnp.cos(d * (2.0**l))
    venc[...] = wide[0:32, 0:rays].astype(BF16)
    wide[0:32, 128:256] = jnp.zeros((32, 128), F32)
    wide[0:27, 128:256] = w_head[256:283, :].astype(BF16).astype(F32)
    view = lax.dot_general(
        wide[0:32, 128:256].astype(BF16), venc[...], (((0,), (0,)), ((), ())), preferred_element_type=F32
    )
    view = (view + vec_t[:, 8:9]) * half
    wide[0:16, 0:128] = jnp.zeros((16, 128), F32)
    wide[0:4, 0:rays] = jnp.broadcast_to(vec_t[0:4, 9:10], (4, rays))
    both_halves(4, target, 3)
    both_halves(7, mask, 6)
    count_here = jnp.sum(wide[7:8, 0:128])
    view_t[...] = jnp.concatenate(split_three(jnp.concatenate([view, wide[0:16, 0:rays]], axis=0)), axis=1)

    one_row = (lax.broadcasted_iota(jnp.int32, (16, hidden_a.shape[1]), 0) == 0).astype(BF16)
    hidden_a[256:272, :] = one_row
    hidden_b[256:272, :] = one_row
    for ref in (g_planes, g_in, g_low, g_top, g_sum, packed):
        ref[...] = jnp.zeros_like(ref)

    lane8 = lax.broadcasted_iota(jnp.int32, (8, LANES), 1)
    sub8 = lax.broadcasted_iota(jnp.int32, (8, LANES), 0)
    sub16 = lax.broadcasted_iota(jnp.int32, (16, LANES), 0)
    anchor = (jnp.int32(1) << (4 * (sub16 // 4))).astype(F32)
    decay_rate = anchor * anchor * (-0.5)

    for copy in copies[:-1]:
        copy.wait()

    size = BLOCK
    per = size // LANES

    def wide_of(tile):
        return jnp.concatenate([tile] * per, axis=1)

    def place_of(i):
        return pl.ds(pl.multiple_of(i * size, LANES), size)

    def encode(i):
        at = place_of(i)
        x = [xs[i * per + k] for k in range(per)]
        for k in range(per):
            x_planes[pl.ds(i * per + k, 8, stride=pitch), :] = x[k]
        x = jnp.concatenate(x, axis=1)
        sub = lax.broadcasted_iota(jnp.int32, (8, size), 0)
        turned = pltpu.roll(x, 4, 0)
        low = sub < 4
        used = sub % 4 < 3
        mean = jnp.where(used, jnp.where(low, x, turned), 0.0)
        var = jnp.where(used, jnp.where(low, turned, x), 0.0)
        m1 = jnp.round(mean * 2.0**11) * 2.0**-11
        p1 = m1 * TURN_HEAD
        p2 = m1 * TURN_REST + (mean - m1) * (TURN_HEAD + TURN_REST)
        hi = jnp.round((p1 + p2) * 2.0**20) * 2.0**-20
        lo = (p1 - hi) + p2
        pw = wide_of(anchor)
        a = jnp.concatenate([hi, hi], axis=0) * pw
        a = (a - jnp.round(a)) + jnp.concatenate([lo, lo], axis=0) * pw
        s, c = sin_cos_turns(a)
        var = jnp.concatenate([var, var], axis=0) * wide_of(decay_rate)
        for d in range(4):
            damp = jnp.exp(var * (4.0**d))
            enc[16 * d : 16 * d + 16, at] = (s * damp).astype(BF16)
            enc[64 + 16 * d : 80 + 16 * d, at] = (c * damp).astype(BF16)
            twice = s + s
            s, c = twice * c, 1.0 - twice * s
        item = x[3:4, :]
        ray = jnp.where(item >= rays, item - rays, item)
        hit = jnp.broadcast_to(ray, (rays, size)) == lax.broadcasted_iota(jnp.int32, (rays, size), 0).astype(F32)
        one_hot[:, at] = jnp.where(hit, 1.0, 0.0).astype(BF16)

    def activate(y, pre_ref, h_ref):
        pre_ref[...] = y
        h = (y * (1.0 + jnp.tanh(y))).astype(BF16)
        h_ref[...] = h
        return h

    def slope(y):
        a = jnp.tanh(y)
        return (1.0 + a) * (1.0 + y * (1.0 - a))

    def forward_all(blocks):
        def step(i, carry):
            first, second, third = (place_of(jnp.clip(i - k, 0, blocks - 1)) for k in range(3))
            hot = one_hot[:, third]
            y_head = dot_nn(wht[...], hidden_c[:, third]) + dot_nn(view_t[...], jnp.concatenate([hot, hot, hot], axis=0))
            y_two = dot_nn(wmt[0], hidden_a[0:256, second]) + wide_of(bias_b[0])
            encode(jnp.minimum(i, blocks - 1))
            f = activate(y_head[0:128, :], feat_pre.at[:, third], feat.at[:, third])
            h = activate(y_two, pre_b.at[:, second], hidden_b.at[0:256, second])
            y_one = dot_nn(w0t[...], enc[:, first])
            y_color = dot_nn(wrt[...], f)[0:8, :] + y_head[128:136, :]
            y_three = dot_nn(wmt[1], h) + wide_of(bias_b[1])
            activate(y_one, pre_a.at[:, first], hidden_a.at[0:256, first])
            tile_at = jnp.clip(i - 2, 0, blocks - 1) * per
            for k in range(per):
                z_planes[pl.ds(tile_at + k, 8, stride=pitch), :] = y_color[:, k * LANES : (k + 1) * LANES]
            activate(y_three, pre_c.at[:, second], hidden_c.at[:, second])
            return carry

        lax.fori_loop(0, blocks + 2, step, 0)

    def backward_all(blocks):
        def step(start, size):
            per = size // LANES
            at = pl.ds(pl.multiple_of(start, LANES), size)
            dz = jnp.concatenate(
                [g_planes[pl.ds(start // LANES + k, 8, stride=pitch), :] for k in range(per)], axis=1
            )
            dzw = dz.astype(BF16).astype(F32)
            part = dzw[:, 0:LANES]
            for k in range(1, per):
                part = part + dzw[:, k * LANES : (k + 1) * LANES]
            g_sum[...] += part
            dz = jnp.concatenate([dzw, jnp.zeros_like(dzw)], axis=0).astype(BF16)
            dz_f = (dot_nn(wr[...], dz) * slope(feat_pre[:, at])).astype(BF16)
            both = jnp.concatenate([dz_f, dz], axis=0)
            up = dot_nn(whd[...], both)
            g_top[:, 0:144] += dot_nt(jnp.concatenate([hidden_c[:, at], one_hot[:, at], feat[:, at]], axis=0), both)
            dz = (up * slope(pre_c[:, at])).astype(BF16)
            up = dot_nn(wm[1], dz)
            made = dot_nt(hidden_b[:, at], dz)
            packed[352:608, :] += made[0:256, :]
            g_low[1] += made[256:272, :]
            dz = (up * slope(pre_b[:, at])).astype(BF16)
            up = dot_nn(wm[0], dz)
            made = dot_nt(hidden_a[:, at], dz)
            packed[96:352, :] += made[0:256, :]
            g_low[0] += made[256:272, :]
            dz = (up * slope(pre_a[:, at])).astype(BF16)
            g_in[...] += dot_nt(enc[:, at], dz)

        def large(i, carry):
            step(i * BACK, BACK)
            return carry

        def small(i, carry):
            step(i * BLOCK, BLOCK)
            return carry

        lax.fori_loop(0, blocks // 2, large, 0)
        lax.fori_loop(blocks // 2 * 2, blocks, small, 0)

    group = 8

    def chunk(first, passes, loss):
        xs[...] = jnp.where(lax.broadcasted_iota(jnp.int32, xs.shape, 1) == 3, -1.0, 0.0)
        x_planes[...] = jnp.full_like(x_planes, -1.0)

        def pack(p, part, g, offset):
            r0 = part * own + g * group
            item0 = (p * rays + r0).astype(F32)
            base = p * 8 * pk_pitch + r0
            moved = []
            for j in range(group):
                count = (counts, counts_two)[part][p, r0 + j]
                here = pk[pl.ds(base + j, 8, stride=pk_pitch), :]
                item = jnp.where(lane8 < count, item0 + float(j), -1.0)
                here = jnp.where(sub8 == 3, item, here)
                o = offset & (LANES - 1)
                moved.append((pltpu.roll(here, o, 1), o, offset >> 7))
                offset = offset + count
            for turned, o, t in moved:
                keep_low = lane8 >= o
                pltpu.store(xs.at[t], turned, mask=keep_low)
                pltpu.store(xs.at[t + 1], turned, mask=jnp.logical_not(keep_low))
            return offset

        def pack_pass(p, offset):
            for part in range(2):
                offset = lax.fori_loop(0, own // group, lambda g, o: pack(p, part, g, o), offset)
            return offset

        total = lax.fori_loop(first, first + passes, pack_pass, jnp.int32(0))
        blocks = (total + BLOCK - 1) // BLOCK
        forward_all(blocks)

        def plane(ref, k):
            return ref[k * pitch : k * pitch + tiles, :]

        lane = lax.broadcasted_iota(jnp.int32, (tiles, LANES), 1)
        row = lax.broadcasted_iota(jnp.int32, (tiles, LANES), 0)
        item = plane(x_planes, 3)
        valid = item >= 0.0
        steps = (1, 2, 4, 8, 16, 32, 64)
        back = [jnp.logical_and(lane >= k, pltpu.roll(item, k, 1) == item) for k in steps]
        ahead = [jnp.logical_and(lane < LANES - k, pltpu.roll(item, LANES - k, 1) == item) for k in steps]
        end_before = jnp.broadcast_to(pltpu.roll(item[:, LANES - 1 : LANES], 1, 0), (tiles, LANES))
        start_after = jnp.broadcast_to(pltpu.roll(item[:, 0:1], tiles - 1, 0), (tiles, LANES))
        from_before = jnp.logical_and(row > 0, end_before == item)
        from_after = jnp.logical_and(row < tiles - 1, start_after == item)

        def scan(values):
            for k, near in zip(steps, back):
                values = values + jnp.where(near, pltpu.roll(values, k, 1), 0.0)
            carry = jnp.broadcast_to(pltpu.roll(values[:, LANES - 1 : LANES], 1, 0), (tiles, LANES))
            return values + jnp.where(from_before, carry, 0.0)

        def scan_back(values):
            for k, near in zip(steps, ahead):
                values = values + jnp.where(near, pltpu.roll(values, LANES - k, 1), 0.0)
            carry = jnp.broadcast_to(pltpu.roll(values[:, 0:1], tiles - 1, 0), (tiles, LANES))
            return values + jnp.where(from_after, carry, 0.0)

        def z_plane(k):
            return jnp.where(valid, plane(z_planes, k), 0.0)

        share = jnp.where(item >= rays, 1.0, COARSE_SHARE) * z_plane(7)
        space = jnp.where(valid, plane(x_planes, 7), 0.0)
        zd = z_plane(3) - 1.0
        density = jnp.maximum(zd, 0.0) + jnp.log1p(jnp.exp(-jnp.abs(zd)))
        tau = density * space
        inclusive = scan(tau)
        exclusive = inclusive - tau
        beyond = jnp.exp(-inclusive)
        weights = jnp.exp(-exclusive) - beyond
        weighted = jnp.zeros_like(tau)
        sums = jnp.zeros_like(tau)
        for c in range(3):
            sig = jax.nn.sigmoid(z_plane(c))
            rgb = 1.002 * sig - 0.001
            part = weights * rgb
            color = scan(part) + (scan_back(part) - part)
            error = color - z_plane(4 + c)
            sums = sums + error * error
            color_grad = (2.0 / 3.0) * share * error
            weighted = weighted + color_grad * rgb
            d_color = weights * color_grad * 1.002 * sig * (1.0 - sig)
            g_planes[c * pitch : c * pitch + tiles, :] = jnp.where(valid, d_color, 0.0)
        product = jnp.where(valid, weighted * weights, 0.0)
        after = scan_back(product) - product
        d_density = (beyond * weighted - after) * space * jax.nn.sigmoid(zd)
        g_planes[3 * pitch : 3 * pitch + tiles, :] = jnp.where(valid, d_density, 0.0)
        previous = jnp.where(lane >= 1, pltpu.roll(item, 1, 1), jnp.where(row > 0, end_before, -2.0))
        begins = jnp.logical_and(previous != item, valid)
        loss = loss + jnp.sum(jnp.where(begins, sums * share, 0.0)) * (1.0 / 3.0)

        backward_all(blocks)
        return loss

    wide[0:2, 0:own] = counts_vec[:, 0:own].astype(F32)
    wide[0:2, own:rays] = small_two[7:9, own:rays]
    everything = jnp.sum(wide[0:2, 0:rays])
    at_once = everything <= 1.0 * capacity
    chunks = jnp.where(at_once, 1, 2)
    passes = jnp.where(at_once, 2, 1)
    loss = lax.fori_loop(0, chunks, lambda i, loss: chunk(i, passes, loss), jnp.zeros((), F32))

    for a in range(4):
        for d in range(4):
            for k in range(2):
                at, to = 64 * k + 16 * d + 4 * a, 48 * k + 12 * a + 3 * d
                packed[to : to + 3, :] = g_in[at : at + 3, :]
    rays_sum = g_top[256 : 256 + rays, 0:128]
    packed[736:737, :] = g_in[67:68, :]
    packed[737:738, :] = g_low[0, 0:1, :]
    packed[738:739, :] = g_low[1, 0:1, :]
    for k in range(2):
        packed[608:736, 128 * k : 128 * k + 128] = g_top[128 * k : 128 * k + 128, 0:128]
        packed[739:740, 128 * k : 128 * k + 128] = g_top[128 * k : 128 * k + 128, 128:256].T[3:4, :]
    packed[740:741, 0:128] = jnp.sum(rays_sum, axis=0, keepdims=True)
    small = jnp.sum(g_sum[...], axis=1, keepdims=True)
    lane1 = lax.broadcasted_iota(jnp.int32, (1, LANES), 1)
    line = jnp.zeros((1, LANES), F32)
    for k in range(4):
        line = line + jnp.where(lane1 == k, jnp.broadcast_to(small[k : k + 1, :], (1, LANES)), 0.0)
    line = line + jnp.where(lane1 == 4, loss, 0.0)
    line = line + jnp.where(lane1 == 5, count_here, 0.0)
    packed[740:741, 128:256] = line
    packed[741:744, 0:128] = g_top[256 + rays : 384 + rays, 128:256].T[0:3, :]
    view_grad = jnp.zeros((32, 128), F32)
    for piece in split_three(rays_sum):
        view_grad = view_grad + dot_nn(venc[...], piece)
    packed[744:760, 0:128] = view_grad[0:16, :]
    packed[744:760, 128:256] = view_grad[16:32, :]
    for q in range(4):
        for ref, which in ((keep, place[0]), (send, place[1])):
            source = pl.multiple_of((which ^ q) * PART, 8)
            ref[q * PART : (q + 1) * PART, :] = packed[pl.ds(source, PART), :]


def field_gradients(find_place, local, other, other_counts, params):
    means, variances, spacing, dirs, target, counts, mask = local
    w_in, w_mid, w_head, w_rgb, vec = params
    rays = dirs.shape[1]
    room = 17 * rays * LANES // 16 + LANES
    tiles = -(-(room - LANES) // (8 * LANES)) * 8
    pitch = tiles + 8 * (1 - tiles // 8 % 2)
    vmem = pl.BlockSpec(memory_space=pltpu.VMEM)
    smem = pl.BlockSpec(memory_space=pltpu.SMEM)
    hbm = pl.BlockSpec(memory_space=pl.ANY)
    scratch = [
        pltpu.VMEM((2 * 8 * (rays + 8), LANES), F32),
        pltpu.VMEM((room // LANES + 1, 8, LANES), F32),
        pltpu.VMEM((8 * pitch, LANES), F32),
        pltpu.VMEM((8 * pitch, LANES), F32),
        pltpu.VMEM((8 * pitch, LANES), F32),
        pltpu.VMEM((128, room), BF16),
        pltpu.VMEM((272, room), BF16),
        pltpu.VMEM((272, room), BF16),
        pltpu.VMEM((256, room), BF16),
        pltpu.VMEM((256, room), F32),
        pltpu.VMEM((256, room), F32),
        pltpu.VMEM((256, room), F32),
        pltpu.VMEM((128, room), BF16),
        pltpu.VMEM((128, room), F32),
        pltpu.VMEM((rays, room), BF16),
        pltpu.VMEM((16, LANES), F32),
        pltpu.VMEM((16, LANES), F32),
        pltpu.VMEM((128, 256), F32),
        pltpu.VMEM((256, 128), BF16),
        pltpu.VMEM((2, 256, 256), BF16),
        pltpu.VMEM((2, 256, 256), BF16),
        pltpu.VMEM((144, 256), BF16),
        pltpu.VMEM((256, 144), BF16),
        pltpu.VMEM((16, 128), BF16),
        pltpu.VMEM((128, 16), BF16),
        pltpu.VMEM((2, 256, 128), F32),
        pltpu.VMEM((144, 3 * rays), BF16),
        pltpu.VMEM((32, rays), BF16),
        pltpu.VMEM((128, 256), F32),
        pltpu.VMEM((2, 16, 256), F32),
        pltpu.VMEM((384 + rays, 256), F32),
        pltpu.VMEM((8, LANES), F32),
        pltpu.VMEM((8 * PART, 256), F32),
        pltpu.SemaphoreType.DMA((29,)),
    ]
    return pl.pallas_call(
        functools.partial(field_kernel, find_place),
        out_shape=[jax.ShapeDtypeStruct((4 * PART, 256), F32)] * 2,
        in_specs=[smem] * 2 + [hbm] * 4 + [vmem] * 9,
        out_specs=[vmem, vmem],
        scratch_shapes=scratch,
        compiler_params=pltpu.CompilerParams(vmem_limit_bytes=63 << 20),
    )(
        counts,
        other_counts,
        other,
        means,
        variances,
        spacing,
        dirs,
        target,
        mask.reshape(1, rays),
        counts,
        w_in,
        w_mid,
        w_head,
        w_rgb.T,
        vec,
    )


def second_half(local):
    means, variances, spacing, dirs, target, counts, mask = local
    rays = dirs.shape[1]
    own = rays // 2
    small = jnp.concatenate([dirs, target, mask[None].astype(F32), counts.astype(F32)], axis=0)
    small = jnp.pad(small, ((0, 16 - small.shape[0]), (0, LANES - rays)))
    return jnp.concatenate(
        [
            means[:, :, own:].reshape(6 * own, LANES),
            variances[:, :, own:].reshape(6 * own, LANES),
            spacing[:, own:].reshape(2 * own, LANES),
            small,
        ],
        axis=0,
    )


def adamw(weight, grad, first, second):
    first = BETA_ONE * first + (1.0 - BETA_ONE) * grad
    second = BETA_TWO * second + (1.0 - BETA_TWO) * grad * grad
    first_hat = first * (1.0 / (1.0 - BETA_ONE**STEP))
    second_hat = second * (1.0 / (1.0 - BETA_TWO**STEP))
    fresh = weight - LEARN_RATE * (first_hat / (jnp.sqrt(second_hat) + EPSILON) + DECAY * weight)
    return first, second, fresh


def update_kernel(find_place, *refs):
    place = find_place()
    pieces, refs = refs[0:8], refs[8:]
    weights, firsts, seconds = refs[0:5], refs[5:10], refs[10:15]
    loss, count = refs[15], refs[16]
    results, outs = refs[17:32], refs[32:47]
    packed, sem = refs[47:]
    for k, ref in enumerate(pieces):
        block = place[k // 4] ^ (k % 4)
        packed[pl.ds(pl.multiple_of(block * PART, 8), PART), :] = ref[...]
    line = packed[740:741, 128:256]
    loss[0] = line[0, 4]
    count[0] = line[0, 5]
    scale = 1.0 / line[0:1, 5:6]

    def apply(group, at, grad):
        step = scale.reshape(1) if grad.ndim == 1 else scale
        made = adamw(weights[group][at], grad * step, firsts[group][at], seconds[group][at])
        for k in range(3):
            outs[3 * group + k][at] = made[k]

    copies = []

    def give(group):
        for k in range(3 * group, 3 * group + 3):
            copies.append(pltpu.make_async_copy(outs[k], results[k], sem.at[k]))
            copies[-1].start()

    everything = slice(None)
    apply(0, (everything, everything), packed[0:96, :])
    give(0)
    for k in range(2):
        apply(1, (k, everything, everything), packed[96 + 256 * k : 352 + 256 * k, :])
    give(1)
    for k in range(2):
        apply(2, (slice(128 * k, 128 * k + 128), everything), packed[608:736, 128 * k : 128 * k + 128])
    apply(2, (slice(256, 272), everything), packed[744:760, 0:128])
    apply(2, (slice(272, 283), everything), packed[744:755, 128:256])
    give(2)
    apply(3, (everything, everything), packed[741:744, 0:128])
    give(3)
    for k in range(9):
        line = packed[736 + k // 2 : 737 + k // 2, 128 * (k % 2) : 128 * (k % 2) + 128]
        apply(4, (pl.ds(128 * k, 128),), line.reshape(128))
    apply(4, (pl.ds(1152, 4),), packed[740:741, 128:132].reshape(4))
    give(4)
    for copy in copies:
        copy.wait()


def update(find_place, pieces, params, firsts, seconds):
    vmem = pl.BlockSpec(memory_space=pltpu.VMEM)
    smem = pl.BlockSpec(memory_space=pltpu.SMEM)
    shapes = [jax.ShapeDtypeStruct((1,), F32)] * 2
    for array in params:
        shapes += [jax.ShapeDtypeStruct(array.shape, F32)] * 3
    return pl.pallas_call(
        functools.partial(update_kernel, find_place),
        out_shape=shapes,
        in_specs=[vmem] * 23,
        out_specs=[smem, smem] + [pl.BlockSpec(memory_space=pl.ANY)] * 15,
        scratch_shapes=[pltpu.VMEM(shape.shape, F32) for shape in shapes[2:]]
        + [pltpu.VMEM((8 * PART, 256), F32), pltpu.SemaphoreType.DMA((15,))],
        compiler_params=pltpu.CompilerParams(vmem_limit_bytes=32 << 20),
    )(*pieces, *params, *firsts, *seconds)


def xor_pairs(total, mask_of):
    return [(i, i ^ mask_of(i)) for i in range(total)]


def place_small():
    ray = lax.axis_index("rays")
    rep = lax.axis_index("rep")
    y, x, core = ray % 2, rep // 2, rep % 2
    xy, yx = 2 * x + y, 2 * y + x
    return (
        jnp.where(core == 0, xy, 4 + yx),
        jnp.where(core == 0, 4 + yx, xy),
    )


def reduce_small(keep, send, axes):
    core = xor_pairs(32, lambda i: 1)
    one = xor_pairs(32, lambda i: 4 if i & 1 else 2)
    two = xor_pairs(32, lambda i: 2 if i & 1 else 4)
    both = xor_pairs(32, lambda i: 6)
    z_one = xor_pairs(32, lambda i: 16 if i & 1 else 8)
    z_two = xor_pairs(32, lambda i: 8 if i & 1 else 16)

    def swap(value, pairs):
        return lax.ppermute(value, axes, pairs)

    square = (two, one, both)
    came = swap(send, core)
    now = [keep[PART * k : PART * (k + 1)] + came[PART * k : PART * (k + 1)] for k in range(4)]
    got = [swap(lax.optimization_barrier(now[k + 1]), square[k]) for k in (2, 1, 0)]
    own = (now[0] + got[2]) + (got[1] + got[0])
    own = own + swap(own, z_one)
    own = own + swap(own, z_two)
    parts = [own] + [swap(own, pairs) for pairs in square]
    return parts + [swap(part, core) for part in parts]


def on_device(
    small_mesh,
    sample_means,
    sample_vars,
    sample_spacing,
    view_dirs,
    target_rgb,
    sample_counts,
    ray_mask,
    w_in,
    w_mid,
    w_head,
    w_rgb,
    vectors,
    first_in,
    first_mid,
    first_head,
    first_rgb,
    first_vec,
    second_in,
    second_mid,
    second_head,
    second_rgb,
    second_vec,
):
    axes = ("rays", "rep")
    find_place = place_small if small_mesh else lambda: (0, 4)
    params = (w_in, w_mid, w_head, w_rgb, vectors)
    local = (sample_means, sample_vars, sample_spacing, view_dirs, target_rgb, sample_counts, ray_mask)
    other, other_counts = second_half(local), sample_counts
    if small_mesh:
        core_pairs = xor_pairs(32, lambda i: 1)
        other, other_counts = (lax.ppermute(array, axes, core_pairs) for array in (other, other_counts))
    keep, send = field_gradients(find_place, local, other, other_counts, params)
    if small_mesh:
        pieces = reduce_small(keep, send, axes)
    else:
        whole = lax.psum(jnp.concatenate([keep, send], axis=0), axes)
        pieces = [whole[PART * k : PART * (k + 1)] for k in range(8)]
    outs = update(
        find_place,
        pieces,
        (w_in, w_mid, w_head, w_rgb.T, vectors),
        (first_in, first_mid, first_head, first_rgb.T, first_vec),
        (second_in, second_mid, second_head, second_rgb.T, second_vec),
    )
    rgb = [out.T for out in outs[11:14]]
    return (outs[0].reshape(()), outs[1].reshape(()), *outs[2:11], *rgb, *outs[14:17])


def solution(mesh):
    rays = ("rays", "rep")
    in_specs = (
        P(None, None, rays, None),
        P(None, None, rays, None),
        P(None, rays, None),
        P(None, rays),
        P(None, rays),
        P(None, rays),
        P(rays),
    ) + (P(),) * 15
    small_mesh = mesh.shape["rays"] == 8 and mesh.shape["rep"] == 4

    def step(*args):
        return on_device(small_mesh, *args)

    return jax.shard_map(step, mesh=mesh, in_specs=in_specs, out_specs=(P(),) * 17, check_vma=False)
```

```python
import functools
import math

import jax
import jax.numpy as jnp
from jax import lax
from jax.experimental import pallas as pl
from jax.experimental.pallas import tpu as pltpu
from jax.sharding import PartitionSpec as P

L_POS = 16
L_DIR = 4
STEP = 7
LEARN_RATE = 0.05
BETA_ONE = 0.9
BETA_TWO = 0.999
EPSILON = 1e-08
DECAY = 0.01
COARSE_SHARE = 0.1

BLOCK = 512
BACK = 1024
LANES = 128
PART = 96

TURN_HEAD = 0.1591796875
TURN_REST = 1.0 / (2.0 * math.pi) - TURN_HEAD
SIN_POLY = (3.1415926343, -5.1677091056, 2.5500551036, -0.5981303017, 0.0773037189)
COS_POLY = (0.9999999314, -4.9347894708, 4.0583337486, -1.3313191807, 0.2184639082)

F32 = jnp.float32
BF16 = jnp.bfloat16


def split_three(values):
    head = values.astype(BF16)
    rest = values - head.astype(F32)
    middle = rest.astype(BF16)
    tail = (rest - middle.astype(F32)).astype(BF16)
    return head, middle, tail


def dot_nt(left, right):
    return lax.dot_general(left, right, (((1,), (1,)), ((), ())), preferred_element_type=F32)


def dot_nn(left, right):
    return jnp.dot(left, right, preferred_element_type=F32)


def poly(coefficients, square):
    total = jnp.full_like(square, coefficients[-1])
    for c in coefficients[-2::-1]:
        total = total * square + c
    return total


def sin_cos_turns(r):
    square = r * r
    s = r * poly(SIN_POLY, square)
    c = poly(COS_POLY, square)
    return (s + s) * c, 1.0 - (s + s) * s


def field_kernel(
    find_place,
    counts,
    counts_two,
    means_two,
    variances_two,
    spacing_two,
    other,
    means,
    variances,
    spacing,
    dirs,
    target,
    mask,
    counts_vec,
    w_in,
    w_mid,
    w_head,
    w_rgb_t,
    vec,
    keep,
    send,
    pk,
    xs,
    x_planes,
    z_planes,
    g_planes,
    enc,
    hidden_a,
    hidden_b,
    hidden_c,
    pre_a,
    pre_b,
    pre_c,
    feat,
    feat_pre,
    one_hot,
    small_two,
    rows,
    wide,
    w0t,
    wmt,
    wm,
    wht,
    whd,
    wrt,
    wr,
    bias_b,
    view_t,
    venc,
    g_in,
    g_low,
    g_top,
    g_sum,
    packed,
    sem,
):
    place = find_place()
    rays = dirs.shape[1]
    own = rays // 2
    pitch = z_planes.shape[0] // 8
    pk_pitch = pk.shape[0] // 16
    capacity = hidden_c.shape[1] - LANES
    tiles = -(-capacity // (8 * LANES)) * 8
    copies = []
    for p in range(2):
        for k, sources in enumerate(((means, means_two), (variances, variances_two))):
            for c in range(3):
                for half, source in enumerate(sources):
                    to = (p * 8 + 4 * k + c) * pk_pitch + half * own
                    copies.append((source.at[p, c, pl.ds(half * own, own)], pk.at[pl.ds(to, own)]))
        for half, source in enumerate((spacing, spacing_two)):
            to = (p * 8 + 7) * pk_pitch + half * own
            copies.append((source.at[p, pl.ds(half * own, own)], pk.at[pl.ds(to, own)]))
    copies.append((other, small_two))
    copies = [pltpu.make_async_copy(a, b, sem.at[k]) for k, (a, b) in enumerate(copies)]
    for copy in copies:
        copy.start()

    half = 0.5
    rows[...] = jnp.zeros_like(rows)
    for k in range(9):
        rows[k : k + 1, :] = vec[pl.ds(k * LANES, LANES)].reshape(1, LANES)
    rows[9:10, 0:4] = vec[pl.ds(9 * LANES, 4)].reshape(1, 4)
    vec_t = rows[0:16, :].T
    wide[0:128, :] = jnp.zeros((128, 256), F32)
    rounded = w_in[...].astype(BF16).astype(F32) * half
    for a in range(4):
        for d in range(4):
            for k in range(2):
                to, at = 64 * k + 16 * d + 4 * a, 48 * k + 12 * a + 3 * d
                wide[to : to + 3, :] = rounded[at : at + 3, :]
    b0 = jnp.concatenate([rows[0:1, :], rows[1:2, :]], axis=1) * half
    for a, piece in enumerate(split_three(b0)):
        wide[67 + 4 * a : 68 + 4 * a, :] = piece.astype(F32)
    w0t[...] = wide[0:128, :].T.astype(BF16)
    for k in range(2):
        rounded = w_mid[k].astype(BF16).astype(F32) * half
        wm[k] = rounded.astype(BF16)
        wmt[k] = rounded.T.astype(BF16)
        bias_b[k, 0:128, :] = jnp.broadcast_to(vec_t[:, 2 + 2 * k : 3 + 2 * k], (128, 128)) * half
        bias_b[k, 128:256, :] = jnp.broadcast_to(vec_t[:, 3 + 2 * k : 4 + 2 * k], (128, 128)) * half
    top = (w_head[0:256, :].astype(BF16).astype(F32) * half).T
    u_row = jnp.concatenate([rows[6:7, :], rows[7:8, :]], axis=1).astype(BF16).astype(F32)
    row16 = lax.broadcasted_iota(jnp.int32, (16, 256), 0)
    last = jnp.where(row16 == 3, u_row, 0.0)
    wht[0:128, :] = top.astype(BF16)
    wht[128:144, :] = last.astype(BF16)
    whd[...] = jnp.concatenate([top, last * half], axis=0).T.astype(BF16)
    wide[0:16, 0:128] = jnp.zeros((16, 128), F32)
    wide[0:3, 0:128] = w_rgb_t[...].astype(BF16).astype(F32)
    wrt[...] = wide[0:16, 0:128].astype(BF16)
    wr[...] = (wide[0:16, 0:128].T * half).astype(BF16)

    copies[-1].wait()

    def both_halves(at, one, row):
        n = one.shape[0]
        wide[at : at + n, 0:own] = one[:, 0:own].astype(F32)
        wide[at : at + n, own:rays] = small_two[row : row + n, own:rays]

    wide[0:32, 0:128] = jnp.zeros((32, 128), F32)
    both_halves(0, dirs, 0)
    d = wide[0:3, 0:rays]
    for l in range(L_DIR):
        wide[3 + 3 * l : 6 + 3 * l, 0:rays] = jnp.sin(d * (2.0**l))
        wide[15 + 3 * l : 18 + 3 * l, 0:rays] = jnp.cos(d * (2.0**l))
    venc[...] = wide[0:32, 0:rays].astype(BF16)
    wide[0:32, 128:256] = jnp.zeros((32, 128), F32)
    wide[0:27, 128:256] = w_head[256:283, :].astype(BF16).astype(F32)
    view = lax.dot_general(
        wide[0:32, 128:256].astype(BF16), venc[...], (((0,), (0,)), ((), ())), preferred_element_type=F32
    )
    view = (view + vec_t[:, 8:9]) * half
    wide[0:16, 0:128] = jnp.zeros((16, 128), F32)
    wide[0:4, 0:rays] = jnp.broadcast_to(vec_t[0:4, 9:10], (4, rays))
    both_halves(4, target, 3)
    both_halves(7, mask, 6)
    count_here = jnp.sum(wide[7:8, 0:128])
    view_t[...] = jnp.concatenate(split_three(jnp.concatenate([view, wide[0:16, 0:rays]], axis=0)), axis=1)

    one_row = (lax.broadcasted_iota(jnp.int32, (16, hidden_a.shape[1]), 0) == 0).astype(BF16)
    hidden_a[256:272, :] = one_row
    hidden_b[256:272, :] = one_row
    for ref in (g_planes, g_in, g_low, g_top, g_sum, packed):
        ref[...] = jnp.zeros_like(ref)

    lane8 = lax.broadcasted_iota(jnp.int32, (8, LANES), 1)
    sub8 = lax.broadcasted_iota(jnp.int32, (8, LANES), 0)
    sub16 = lax.broadcasted_iota(jnp.int32, (16, LANES), 0)
    anchor = (jnp.int32(1) << (4 * (sub16 // 4))).astype(F32)
    decay_rate = anchor * anchor * (-0.5)

    for copy in copies[:-1]:
        copy.wait()

    size = BLOCK
    per = size // LANES

    def wide_of(tile):
        return jnp.concatenate([tile] * per, axis=1)

    def place_of(i):
        return pl.ds(pl.multiple_of(i * size, LANES), size)

    def encode(i):
        at = place_of(i)
        x = [xs[i * per + k] for k in range(per)]
        for k in range(per):
            x_planes[pl.ds(i * per + k, 8, stride=pitch), :] = x[k]
        x = jnp.concatenate(x, axis=1)
        sub = lax.broadcasted_iota(jnp.int32, (8, size), 0)
        turned = pltpu.roll(x, 4, 0)
        low = sub < 4
        used = sub % 4 < 3
        mean = jnp.where(used, jnp.where(low, x, turned), 0.0)
        var = jnp.where(used, jnp.where(low, turned, x), 0.0)
        m1 = jnp.round(mean * 2.0**11) * 2.0**-11
        p1 = m1 * TURN_HEAD
        p2 = m1 * TURN_REST + (mean - m1) * (TURN_HEAD + TURN_REST)
        hi = jnp.round((p1 + p2) * 2.0**20) * 2.0**-20
        lo = (p1 - hi) + p2
        pw = wide_of(anchor)
        a = jnp.concatenate([hi, hi], axis=0) * pw
        a = (a - jnp.round(a)) + jnp.concatenate([lo, lo], axis=0) * pw
        s, c = sin_cos_turns(a)
        var = jnp.concatenate([var, var], axis=0) * wide_of(decay_rate)
        for d in range(4):
            damp = jnp.exp(var * (4.0**d))
            enc[16 * d : 16 * d + 16, at] = (s * damp).astype(BF16)
            enc[64 + 16 * d : 80 + 16 * d, at] = (c * damp).astype(BF16)
            twice = s + s
            s, c = twice * c, 1.0 - twice * s
        item = x[3:4, :]
        ray = jnp.where(item >= rays, item - rays, item)
        hit = jnp.broadcast_to(ray, (rays, size)) == lax.broadcasted_iota(jnp.int32, (rays, size), 0).astype(F32)
        one_hot[:, at] = jnp.where(hit, 1.0, 0.0).astype(BF16)

    def activate(y, pre_ref, h_ref):
        pre_ref[...] = y
        h = (y * (1.0 + jnp.tanh(y))).astype(BF16)
        h_ref[...] = h
        return h

    def slope(y):
        a = jnp.tanh(y)
        return (1.0 + a) * (1.0 + y * (1.0 - a))

    def forward_all(blocks):
        def step(i, carry):
            first, second, third = (place_of(jnp.clip(i - k, 0, blocks - 1)) for k in range(3))
            hot = one_hot[:, third]
            y_head = dot_nn(wht[...], hidden_c[:, third]) + dot_nn(view_t[...], jnp.concatenate([hot, hot, hot], axis=0))
            y_two = dot_nn(wmt[0], hidden_a[0:256, second]) + wide_of(bias_b[0])
            encode(jnp.minimum(i, blocks - 1))
            f = activate(y_head[0:128, :], feat_pre.at[:, third], feat.at[:, third])
            h = activate(y_two, pre_b.at[:, second], hidden_b.at[0:256, second])
            y_one = dot_nn(w0t[...], enc[:, first])
            y_color = dot_nn(wrt[...], f)[0:8, :] + y_head[128:136, :]
            y_three = dot_nn(wmt[1], h) + wide_of(bias_b[1])
            activate(y_one, pre_a.at[:, first], hidden_a.at[0:256, first])
            tile_at = jnp.clip(i - 2, 0, blocks - 1) * per
            for k in range(per):
                z_planes[pl.ds(tile_at + k, 8, stride=pitch), :] = y_color[:, k * LANES : (k + 1) * LANES]
            activate(y_three, pre_c.at[:, second], hidden_c.at[:, second])
            return carry

        lax.fori_loop(0, blocks + 2, step, 0)

    def backward_all(blocks):
        def step(start, size):
            per = size // LANES
            at = pl.ds(pl.multiple_of(start, LANES), size)
            dz = jnp.concatenate(
                [g_planes[pl.ds(start // LANES + k, 8, stride=pitch), :] for k in range(per)], axis=1
            )
            dzw = dz.astype(BF16).astype(F32)
            part = dzw[:, 0:LANES]
            for k in range(1, per):
                part = part + dzw[:, k * LANES : (k + 1) * LANES]
            g_sum[...] += part
            dz = jnp.concatenate([dzw, jnp.zeros_like(dzw)], axis=0).astype(BF16)
            dz_f = (dot_nn(wr[...], dz) * slope(feat_pre[:, at])).astype(BF16)
            both = jnp.concatenate([dz_f, dz], axis=0)
            up = dot_nn(whd[...], both)
            g_top[:, 0:144] += dot_nt(jnp.concatenate([hidden_c[:, at], one_hot[:, at], feat[:, at]], axis=0), both)
            dz = (up * slope(pre_c[:, at])).astype(BF16)
            up = dot_nn(wm[1], dz)
            made = dot_nt(hidden_b[:, at], dz)
            packed[352:608, :] += made[0:256, :]
            g_low[1] += made[256:272, :]
            dz = (up * slope(pre_b[:, at])).astype(BF16)
            up = dot_nn(wm[0], dz)
            made = dot_nt(hidden_a[:, at], dz)
            packed[96:352, :] += made[0:256, :]
            g_low[0] += made[256:272, :]
            dz = (up * slope(pre_a[:, at])).astype(BF16)
            g_in[...] += dot_nt(enc[:, at], dz)

        def large(i, carry):
            step(i * BACK, BACK)
            return carry

        def small(i, carry):
            step(i * BLOCK, BLOCK)
            return carry

        lax.fori_loop(0, blocks // 2, large, 0)
        lax.fori_loop(blocks // 2 * 2, blocks, small, 0)

    group = 8

    def chunk(first, passes, loss):
        xs[...] = jnp.where(lax.broadcasted_iota(jnp.int32, xs.shape, 1) == 3, -1.0, 0.0)
        x_planes[...] = jnp.full_like(x_planes, -1.0)

        def pack(p, part, g, offset):
            r0 = part * own + g * group
            item0 = (p * rays + r0).astype(F32)
            base = p * 8 * pk_pitch + r0
            moved = []
            for j in range(group):
                count = (counts, counts_two)[part][p, r0 + j]
                here = pk[pl.ds(base + j, 8, stride=pk_pitch), :]
                item = jnp.where(lane8 < count, item0 + float(j), -1.0)
                here = jnp.where(sub8 == 3, item, here)
                o = offset & (LANES - 1)
                moved.append((pltpu.roll(here, o, 1), o, offset >> 7))
                offset = offset + count
            for turned, o, t in moved:
                keep_low = lane8 >= o
                pltpu.store(xs.at[t], turned, mask=keep_low)
                pltpu.store(xs.at[t + 1], turned, mask=jnp.logical_not(keep_low))
            return offset

        def pack_pass(p, offset):
            for part in range(2):
                offset = lax.fori_loop(0, own // group, lambda g, o: pack(p, part, g, o), offset)
            return offset

        total = lax.fori_loop(first, first + passes, pack_pass, jnp.int32(0))
        blocks = (total + BLOCK - 1) // BLOCK
        forward_all(blocks)

        def plane(ref, k):
            return ref[k * pitch : k * pitch + tiles, :]

        lane = lax.broadcasted_iota(jnp.int32, (tiles, LANES), 1)
        row = lax.broadcasted_iota(jnp.int32, (tiles, LANES), 0)
        item = plane(x_planes, 3)
        valid = item >= 0.0
        steps = (1, 2, 4, 8, 16, 32, 64)
        back = [jnp.logical_and(lane >= k, pltpu.roll(item, k, 1) == item) for k in steps]
        ahead = [jnp.logical_and(lane < LANES - k, pltpu.roll(item, LANES - k, 1) == item) for k in steps]
        end_before = jnp.broadcast_to(pltpu.roll(item[:, LANES - 1 : LANES], 1, 0), (tiles, LANES))
        start_after = jnp.broadcast_to(pltpu.roll(item[:, 0:1], tiles - 1, 0), (tiles, LANES))
        from_before = jnp.logical_and(row > 0, end_before == item)
        from_after = jnp.logical_and(row < tiles - 1, start_after == item)

        def scan(values):
            for k, near in zip(steps, back):
                values = values + jnp.where(near, pltpu.roll(values, k, 1), 0.0)
            carry = jnp.broadcast_to(pltpu.roll(values[:, LANES - 1 : LANES], 1, 0), (tiles, LANES))
            return values + jnp.where(from_before, carry, 0.0)

        def scan_back(values):
            for k, near in zip(steps, ahead):
                values = values + jnp.where(near, pltpu.roll(values, LANES - k, 1), 0.0)
            carry = jnp.broadcast_to(pltpu.roll(values[:, 0:1], tiles - 1, 0), (tiles, LANES))
            return values + jnp.where(from_after, carry, 0.0)

        def z_plane(k):
            return jnp.where(valid, plane(z_planes, k), 0.0)

        share = jnp.where(item >= rays, 1.0, COARSE_SHARE) * z_plane(7)
        space = jnp.where(valid, plane(x_planes, 7), 0.0)
        zd = z_plane(3) - 1.0
        density = jnp.maximum(zd, 0.0) + jnp.log1p(jnp.exp(-jnp.abs(zd)))
        tau = density * space
        inclusive = scan(tau)
        exclusive = inclusive - tau
        beyond = jnp.exp(-inclusive)
        weights = jnp.exp(-exclusive) - beyond
        weighted = jnp.zeros_like(tau)
        sums = jnp.zeros_like(tau)
        for c in range(3):
            sig = jax.nn.sigmoid(z_plane(c))
            rgb = 1.002 * sig - 0.001
            part = weights * rgb
            color = scan(part) + (scan_back(part) - part)
            error = color - z_plane(4 + c)
            sums = sums + error * error
            color_grad = (2.0 / 3.0) * share * error
            weighted = weighted + color_grad * rgb
            d_color = weights * color_grad * 1.002 * sig * (1.0 - sig)
            g_planes[c * pitch : c * pitch + tiles, :] = jnp.where(valid, d_color, 0.0)
        product = jnp.where(valid, weighted * weights, 0.0)
        after = scan_back(product) - product
        d_density = (beyond * weighted - after) * space * jax.nn.sigmoid(zd)
        g_planes[3 * pitch : 3 * pitch + tiles, :] = jnp.where(valid, d_density, 0.0)
        previous = jnp.where(lane >= 1, pltpu.roll(item, 1, 1), jnp.where(row > 0, end_before, -2.0))
        begins = jnp.logical_and(previous != item, valid)
        loss = loss + jnp.sum(jnp.where(begins, sums * share, 0.0)) * (1.0 / 3.0)

        backward_all(blocks)
        return loss

    wide[0:2, 0:own] = counts_vec[:, 0:own].astype(F32)
    wide[0:2, own:rays] = small_two[7:9, own:rays]
    everything = jnp.sum(wide[0:2, 0:rays])
    at_once = everything <= 1.0 * capacity
    chunks = jnp.where(at_once, 1, 2)
    passes = jnp.where(at_once, 2, 1)
    loss = lax.fori_loop(0, chunks, lambda i, loss: chunk(i, passes, loss), jnp.zeros((), F32))

    for a in range(4):
        for d in range(4):
            for k in range(2):
                at, to = 64 * k + 16 * d + 4 * a, 48 * k + 12 * a + 3 * d
                packed[to : to + 3, :] = g_in[at : at + 3, :]
    rays_sum = g_top[256 : 256 + rays, 0:128]
    packed[736:737, :] = g_in[67:68, :]
    packed[737:738, :] = g_low[0, 0:1, :]
    packed[738:739, :] = g_low[1, 0:1, :]
    for k in range(2):
        packed[608:736, 128 * k : 128 * k + 128] = g_top[128 * k : 128 * k + 128, 0:128]
        packed[739:740, 128 * k : 128 * k + 128] = g_top[128 * k : 128 * k + 128, 128:256].T[3:4, :]
    packed[740:741, 0:128] = jnp.sum(rays_sum, axis=0, keepdims=True)
    small = jnp.sum(g_sum[...], axis=1, keepdims=True)
    lane1 = lax.broadcasted_iota(jnp.int32, (1, LANES), 1)
    line = jnp.zeros((1, LANES), F32)
    for k in range(4):
        line = line + jnp.where(lane1 == k, jnp.broadcast_to(small[k : k + 1, :], (1, LANES)), 0.0)
    line = line + jnp.where(lane1 == 4, loss, 0.0)
    line = line + jnp.where(lane1 == 5, count_here, 0.0)
    packed[740:741, 128:256] = line
    packed[741:744, 0:128] = g_top[256 + rays : 384 + rays, 128:256].T[0:3, :]
    view_grad = jnp.zeros((32, 128), F32)
    for piece in split_three(rays_sum):
        view_grad = view_grad + dot_nn(venc[...], piece)
    packed[744:760, 0:128] = view_grad[0:16, :]
    packed[744:760, 128:256] = view_grad[16:32, :]
    for q in range(4):
        for ref, which in ((keep, place[0]), (send, place[1])):
            source = pl.multiple_of((which ^ q) * PART, 8)
            ref[q * PART : (q + 1) * PART, :] = packed[pl.ds(source, PART), :]


def field_gradients(find_place, local, other, params):
    means, variances, spacing, dirs, target, counts, mask = local
    means_two, variances_two, spacing_two, other_counts, other_rows = other
    w_in, w_mid, w_head, w_rgb, vec = params
    rays = dirs.shape[1]
    room = 17 * rays * LANES // 16 + LANES
    tiles = -(-(room - LANES) // (8 * LANES)) * 8
    pitch = tiles + 8 * (1 - tiles // 8 % 2)
    vmem = pl.BlockSpec(memory_space=pltpu.VMEM)
    smem = pl.BlockSpec(memory_space=pltpu.SMEM)
    hbm = pl.BlockSpec(memory_space=pl.ANY)
    scratch = [
        pltpu.VMEM((2 * 8 * (rays + 8), LANES), F32),
        pltpu.VMEM((room // LANES + 1, 8, LANES), F32),
        pltpu.VMEM((8 * pitch, LANES), F32),
        pltpu.VMEM((8 * pitch, LANES), F32),
        pltpu.VMEM((8 * pitch, LANES), F32),
        pltpu.VMEM((128, room), BF16),
        pltpu.VMEM((272, room), BF16),
        pltpu.VMEM((272, room), BF16),
        pltpu.VMEM((256, room), BF16),
        pltpu.VMEM((256, room), F32),
        pltpu.VMEM((256, room), F32),
        pltpu.VMEM((256, room), F32),
        pltpu.VMEM((128, room), BF16),
        pltpu.VMEM((128, room), F32),
        pltpu.VMEM((rays, room), BF16),
        pltpu.VMEM((16, LANES), F32),
        pltpu.VMEM((16, LANES), F32),
        pltpu.VMEM((128, 256), F32),
        pltpu.VMEM((256, 128), BF16),
        pltpu.VMEM((2, 256, 256), BF16),
        pltpu.VMEM((2, 256, 256), BF16),
        pltpu.VMEM((144, 256), BF16),
        pltpu.VMEM((256, 144), BF16),
        pltpu.VMEM((16, 128), BF16),
        pltpu.VMEM((128, 16), BF16),
        pltpu.VMEM((2, 256, 128), F32),
        pltpu.VMEM((144, 3 * rays), BF16),
        pltpu.VMEM((32, rays), BF16),
        pltpu.VMEM((128, 256), F32),
        pltpu.VMEM((2, 16, 256), F32),
        pltpu.VMEM((384 + rays, 256), F32),
        pltpu.VMEM((8, LANES), F32),
        pltpu.VMEM((8 * PART, 256), F32),
        pltpu.SemaphoreType.DMA((29,)),
    ]
    return pl.pallas_call(
        functools.partial(field_kernel, find_place),
        out_shape=[jax.ShapeDtypeStruct((4 * PART, 256), F32)] * 2,
        in_specs=[smem] * 2 + [hbm] * 7 + [vmem] * 9,
        out_specs=[vmem, vmem],
        scratch_shapes=scratch,
        compiler_params=pltpu.CompilerParams(vmem_limit_bytes=63 << 20),
    )(
        counts,
        other_counts,
        means_two,
        variances_two,
        spacing_two,
        other_rows,
        means,
        variances,
        spacing,
        dirs,
        target,
        mask.reshape(1, rays),
        counts,
        w_in,
        w_mid,
        w_head,
        w_rgb.T,
        vec,
    )


def ray_rows(local):
    dirs, target, counts, mask = local[3:]
    rows = jnp.concatenate([dirs, target, mask[None].astype(F32), counts.astype(F32)], axis=0)
    return jnp.pad(rows, ((0, 16 - rows.shape[0]), (0, LANES - rows.shape[1])))


def adamw(weight, grad, first, second):
    first = BETA_ONE * first + (1.0 - BETA_ONE) * grad
    second = BETA_TWO * second + (1.0 - BETA_TWO) * grad * grad
    first_hat = first * (1.0 / (1.0 - BETA_ONE**STEP))
    second_hat = second * (1.0 / (1.0 - BETA_TWO**STEP))
    fresh = weight - LEARN_RATE * (first_hat / (jnp.sqrt(second_hat) + EPSILON) + DECAY * weight)
    return first, second, fresh


def update_kernel(find_place, *refs):
    place = find_place()
    pieces, refs = refs[0:8], refs[8:]
    weights, firsts, seconds = refs[0:5], refs[5:10], refs[10:15]
    loss, count = refs[15], refs[16]
    outs = refs[17:32]
    packed = refs[32]
    for k, ref in enumerate(pieces):
        block = place[k // 4] ^ (k % 4)
        packed[pl.ds(pl.multiple_of(block * PART, 8), PART), :] = ref[...]
    line = packed[740:741, 128:256]
    loss[0] = line[0, 4]
    count[0] = line[0, 5]
    scale = 1.0 / line[0:1, 5:6]

    def apply(group, at, grad):
        step = scale.reshape(1) if grad.ndim == 1 else scale
        made = adamw(weights[group][at], grad * step, firsts[group][at], seconds[group][at])
        for k in range(3):
            outs[3 * group + k][at] = made[k]

    everything = slice(None)
    apply(0, (everything, everything), packed[0:96, :])
    for k in range(2):
        apply(1, (k, everything, everything), packed[96 + 256 * k : 352 + 256 * k, :])
    for k in range(2):
        apply(2, (slice(128 * k, 128 * k + 128), everything), packed[608:736, 128 * k : 128 * k + 128])
    apply(2, (slice(256, 272), everything), packed[744:760, 0:128])
    apply(2, (slice(272, 283), everything), packed[744:755, 128:256])
    apply(3, (everything, everything), packed[741:744, 0:128])
    for k in range(9):
        line = packed[736 + k // 2 : 737 + k // 2, 128 * (k % 2) : 128 * (k % 2) + 128]
        apply(4, (pl.ds(128 * k, 128),), line.reshape(128))
    apply(4, (pl.ds(1152, 4),), packed[740:741, 128:132].reshape(4))


def update(find_place, pieces, params, firsts, seconds):
    vmem = pl.BlockSpec(memory_space=pltpu.VMEM)
    smem = pl.BlockSpec(memory_space=pltpu.SMEM)
    shapes = [jax.ShapeDtypeStruct((1,), F32)] * 2
    for array in params:
        shapes += [jax.ShapeDtypeStruct(array.shape, F32)] * 3
    return pl.pallas_call(
        functools.partial(update_kernel, find_place),
        out_shape=shapes,
        in_specs=[vmem] * 23,
        out_specs=[smem, smem] + [vmem] * 15,
        scratch_shapes=[pltpu.VMEM((8 * PART, 256), F32)],
        compiler_params=pltpu.CompilerParams(vmem_limit_bytes=32 << 20),
    )(*pieces, *params, *firsts, *seconds)


def xor_pairs(total, mask_of):
    return [(i, i ^ mask_of(i)) for i in range(total)]


def place_small():
    ray = lax.axis_index("rays")
    rep = lax.axis_index("rep")
    y, x, core = ray % 2, rep // 2, rep % 2
    xy, yx = 2 * x + y, 2 * y + x
    return (
        jnp.where(core == 0, xy, 4 + yx),
        jnp.where(core == 0, 4 + yx, xy),
    )


def reduce_small(keep, send, axes):
    core = xor_pairs(32, lambda i: 1)
    one = xor_pairs(32, lambda i: 4 if i & 1 else 2)
    two = xor_pairs(32, lambda i: 2 if i & 1 else 4)
    both = xor_pairs(32, lambda i: 6)
    z_one = xor_pairs(32, lambda i: 16 if i & 1 else 8)
    z_two = xor_pairs(32, lambda i: 8 if i & 1 else 16)

    def swap(value, pairs):
        return lax.ppermute(value, axes, pairs)

    square = (two, one, both)
    now = keep + swap(send, core)
    got = [swap(now[PART * (k + 1) : PART * (k + 2)], pairs) for k, pairs in enumerate(square)]
    own = (now[:PART] + got[0]) + (got[1] + got[2])
    own = own + swap(own, z_one)
    own = own + swap(own, z_two)
    parts = [own] + [swap(own, pairs) for pairs in square]
    return parts + [swap(part, core) for part in parts]


def on_device(
    small_mesh,
    sample_means,
    sample_vars,
    sample_spacing,
    view_dirs,
    target_rgb,
    sample_counts,
    ray_mask,
    w_in,
    w_mid,
    w_head,
    w_rgb,
    vectors,
    first_in,
    first_mid,
    first_head,
    first_rgb,
    first_vec,
    second_in,
    second_mid,
    second_head,
    second_rgb,
    second_vec,
):
    axes = ("rays", "rep")
    find_place = place_small if small_mesh else lambda: (0, 4)
    params = (w_in, w_mid, w_head, w_rgb, vectors)
    local = (sample_means, sample_vars, sample_spacing, view_dirs, target_rgb, sample_counts, ray_mask)
    other = (sample_means, sample_vars, sample_spacing, sample_counts, ray_rows(local))
    if small_mesh:
        core_pairs = xor_pairs(32, lambda i: 1)
        other = tuple(lax.ppermute(array, axes, core_pairs) for array in other)
    keep, send = field_gradients(find_place, local, other, params)
    if small_mesh:
        pieces = reduce_small(keep, send, axes)
    else:
        whole = lax.psum(jnp.concatenate([keep, send], axis=0), axes)
        pieces = [whole[PART * k : PART * (k + 1)] for k in range(8)]
    outs = update(
        find_place,
        pieces,
        (w_in, w_mid, w_head, w_rgb.T, vectors),
        (first_in, first_mid, first_head, first_rgb.T, first_vec),
        (second_in, second_mid, second_head, second_rgb.T, second_vec),
    )
    rgb = [out.T for out in outs[11:14]]
    return (outs[0].reshape(()), outs[1].reshape(()), *outs[2:11], *rgb, *outs[14:17])


def solution(mesh):
    rays = ("rays", "rep")
    in_specs = (
        P(None, None, rays, None),
        P(None, None, rays, None),
        P(None, rays, None),
        P(None, rays),
        P(None, rays),
        P(None, rays),
        P(rays),
    ) + (P(),) * 15
    small_mesh = mesh.shape["rays"] == 8 and mesh.shape["rep"] == 4

    def step(*args):
        return on_device(small_mesh, *args)

    return jax.shard_map(step, mesh=mesh, in_specs=in_specs, out_specs=(P(),) * 17, check_vma=False)
```

```python
import functools
import math

import jax
import jax.numpy as jnp
from jax import lax
from jax.experimental import pallas as pl
from jax.experimental.pallas import tpu as pltpu
from jax.sharding import PartitionSpec as P

L_POS = 16
L_DIR = 4
STEP = 7
LEARN_RATE = 0.05
BETA_ONE = 0.9
BETA_TWO = 0.999
EPSILON = 1e-08
DECAY = 0.01
COARSE_SHARE = 0.1

BLOCK = 512
BACK = 1024
LANES = 128
PART = 96

TURN_HEAD = 0.1591796875
TURN_REST = 1.0 / (2.0 * math.pi) - TURN_HEAD
SIN_POLY = (3.1415926343, -5.1677091056, 2.5500551036, -0.5981303017, 0.0773037189)
COS_POLY = (0.9999999314, -4.9347894708, 4.0583337486, -1.3313191807, 0.2184639082)

F32 = jnp.float32
BF16 = jnp.bfloat16


def split_three(values):
    head = values.astype(BF16)
    rest = values - head.astype(F32)
    middle = rest.astype(BF16)
    tail = (rest - middle.astype(F32)).astype(BF16)
    return head, middle, tail


def dot_nt(left, right):
    return lax.dot_general(left, right, (((1,), (1,)), ((), ())), preferred_element_type=F32)


def dot_nn(left, right):
    return jnp.dot(left, right, preferred_element_type=F32)


def poly(coefficients, square):
    total = jnp.full_like(square, coefficients[-1])
    for c in coefficients[-2::-1]:
        total = total * square + c
    return total


def sin_cos_turns(r):
    square = r * r
    s = r * poly(SIN_POLY, square)
    c = poly(COS_POLY, square)
    return (s + s) * c, 1.0 - (s + s) * s


def field_kernel(
    find_place,
    counts,
    counts_two,
    means_two,
    variances_two,
    spacing_two,
    other,
    means,
    variances,
    spacing,
    dirs,
    target,
    mask,
    counts_vec,
    w_in,
    w_mid,
    w_head,
    w_rgb_t,
    vec,
    keep,
    send,
    pk,
    xs,
    x_planes,
    z_planes,
    g_planes,
    enc,
    hidden_a,
    hidden_b,
    hidden_c,
    pre_a,
    pre_b,
    pre_c,
    feat,
    feat_pre,
    one_hot,
    small_two,
    rows,
    wide,
    w0t,
    wmt,
    wm,
    wht,
    whd,
    wrt,
    wr,
    bias_b,
    view_t,
    venc,
    g_in,
    g_low,
    g_top,
    g_sum,
    packed,
    sem,
):
    place = find_place()
    rays = dirs.shape[1]
    own = rays // 2
    pitch = z_planes.shape[0] // 8
    pk_pitch = pk.shape[0] // 16
    capacity = hidden_c.shape[1] - LANES
    tiles = -(-capacity // (8 * LANES)) * 8
    copies = []
    for p in range(2):
        for k, sources in enumerate(((means, means_two), (variances, variances_two))):
            for c in range(3):
                for half, source in enumerate(sources):
                    to = (p * 8 + 4 * k + c) * pk_pitch + half * own
                    copies.append((source.at[p, c, pl.ds(half * own, own)], pk.at[pl.ds(to, own)]))
        for half, source in enumerate((spacing, spacing_two)):
            to = (p * 8 + 7) * pk_pitch + half * own
            copies.append((source.at[p, pl.ds(half * own, own)], pk.at[pl.ds(to, own)]))
    copies.append((other, small_two))
    copies = [pltpu.make_async_copy(a, b, sem.at[k]) for k, (a, b) in enumerate(copies)]
    for copy in copies:
        copy.start()

    half = 0.5
    rows[...] = jnp.zeros_like(rows)
    for k in range(9):
        rows[k : k + 1, :] = vec[pl.ds(k * LANES, LANES)].reshape(1, LANES)
    rows[9:10, 0:4] = vec[pl.ds(9 * LANES, 4)].reshape(1, 4)
    vec_t = rows[0:16, :].T
    wide[0:128, :] = jnp.zeros((128, 256), F32)
    rounded = w_in[...].astype(BF16).astype(F32) * half
    for a in range(4):
        for d in range(4):
            for k in range(2):
                to, at = 64 * k + 16 * d + 4 * a, 48 * k + 12 * a + 3 * d
                wide[to : to + 3, :] = rounded[at : at + 3, :]
    b0 = jnp.concatenate([rows[0:1, :], rows[1:2, :]], axis=1) * half
    for a, piece in enumerate(split_three(b0)):
        wide[67 + 4 * a : 68 + 4 * a, :] = piece.astype(F32)
    w0t[...] = wide[0:128, :].T.astype(BF16)
    for k in range(2):
        rounded = w_mid[k].astype(BF16).astype(F32) * half
        wm[k] = rounded.astype(BF16)
        wmt[k] = rounded.T.astype(BF16)
        bias_b[k, 0:128, :] = jnp.broadcast_to(vec_t[:, 2 + 2 * k : 3 + 2 * k], (128, 128)) * half
        bias_b[k, 128:256, :] = jnp.broadcast_to(vec_t[:, 3 + 2 * k : 4 + 2 * k], (128, 128)) * half
    top = (w_head[0:256, :].astype(BF16).astype(F32) * half).T
    u_row = jnp.concatenate([rows[6:7, :], rows[7:8, :]], axis=1).astype(BF16).astype(F32)
    row16 = lax.broadcasted_iota(jnp.int32, (16, 256), 0)
    last = jnp.where(row16 == 3, u_row, 0.0)
    wht[0:128, :] = top.astype(BF16)
    wht[128:144, :] = last.astype(BF16)
    whd[...] = jnp.concatenate([top, last * half], axis=0).T.astype(BF16)
    wide[0:16, 0:128] = jnp.zeros((16, 128), F32)
    wide[0:3, 0:128] = w_rgb_t[...].astype(BF16).astype(F32)
    wrt[...] = wide[0:16, 0:128].astype(BF16)
    wr[...] = (wide[0:16, 0:128].T * half).astype(BF16)

    copies[-1].wait()

    def both_halves(at, one, row):
        n = one.shape[0]
        wide[at : at + n, 0:own] = one[:, 0:own].astype(F32)
        wide[at : at + n, own:rays] = small_two[row : row + n, own:rays]

    wide[0:32, 0:128] = jnp.zeros((32, 128), F32)
    both_halves(0, dirs, 0)
    d = wide[0:3, 0:rays]
    for l in range(L_DIR):
        wide[3 + 3 * l : 6 + 3 * l, 0:rays] = jnp.sin(d * (2.0**l))
        wide[15 + 3 * l : 18 + 3 * l, 0:rays] = jnp.cos(d * (2.0**l))
    venc[...] = wide[0:32, 0:rays].astype(BF16)
    wide[0:32, 128:256] = jnp.zeros((32, 128), F32)
    wide[0:27, 128:256] = w_head[256:283, :].astype(BF16).astype(F32)
    view = lax.dot_general(
        wide[0:32, 128:256].astype(BF16), venc[...], (((0,), (0,)), ((), ())), preferred_element_type=F32
    )
    view = (view + vec_t[:, 8:9]) * half
    wide[0:16, 0:128] = jnp.zeros((16, 128), F32)
    wide[0:4, 0:rays] = jnp.broadcast_to(vec_t[0:4, 9:10], (4, rays))
    both_halves(4, target, 3)
    both_halves(7, mask, 6)
    count_here = jnp.sum(wide[7:8, 0:128])
    view_t[...] = jnp.concatenate(split_three(jnp.concatenate([view, wide[0:16, 0:rays]], axis=0)), axis=1)

    one_row = (lax.broadcasted_iota(jnp.int32, (16, hidden_a.shape[1]), 0) == 0).astype(BF16)
    hidden_a[256:272, :] = one_row
    hidden_b[256:272, :] = one_row
    for ref in (g_planes, g_in, g_low, g_top, g_sum, packed):
        ref[...] = jnp.zeros_like(ref)

    lane8 = lax.broadcasted_iota(jnp.int32, (8, LANES), 1)
    sub8 = lax.broadcasted_iota(jnp.int32, (8, LANES), 0)
    sub16 = lax.broadcasted_iota(jnp.int32, (16, LANES), 0)
    anchor = (jnp.int32(1) << (4 * (sub16 // 4))).astype(F32)
    decay_rate = anchor * anchor * (-0.5)

    for copy in copies[:-1]:
        copy.wait()

    size = BLOCK
    per = size // LANES

    def wide_of(tile):
        return jnp.concatenate([tile] * per, axis=1)

    def place_of(i):
        return pl.ds(pl.multiple_of(i * size, LANES), size)

    def encode(i):
        at = place_of(i)
        x = [xs[i * per + k] for k in range(per)]
        for k in range(per):
            x_planes[pl.ds(i * per + k, 8, stride=pitch), :] = x[k]
        x = jnp.concatenate(x, axis=1)
        sub = lax.broadcasted_iota(jnp.int32, (8, size), 0)
        turned = pltpu.roll(x, 4, 0)
        low = sub < 4
        used = sub % 4 < 3
        mean = jnp.where(used, jnp.where(low, x, turned), 0.0)
        var = jnp.where(used, jnp.where(low, turned, x), 0.0)
        m1 = jnp.round(mean * 2.0**11) * 2.0**-11
        p1 = m1 * TURN_HEAD
        p2 = m1 * TURN_REST + (mean - m1) * (TURN_HEAD + TURN_REST)
        hi = jnp.round((p1 + p2) * 2.0**20) * 2.0**-20
        lo = (p1 - hi) + p2
        pw = wide_of(anchor)
        a = jnp.concatenate([hi, hi], axis=0) * pw
        a = (a - jnp.round(a)) + jnp.concatenate([lo, lo], axis=0) * pw
        s, c = sin_cos_turns(a)
        var = jnp.concatenate([var, var], axis=0) * wide_of(decay_rate)
        for d in range(4):
            damp = jnp.exp(var * (4.0**d))
            enc[16 * d : 16 * d + 16, at] = (s * damp).astype(BF16)
            enc[64 + 16 * d : 80 + 16 * d, at] = (c * damp).astype(BF16)
            twice = s + s
            s, c = twice * c, 1.0 - twice * s
        item = x[3:4, :]
        ray = jnp.where(item >= rays, item - rays, item)
        hit = jnp.broadcast_to(ray, (rays, size)) == lax.broadcasted_iota(jnp.int32, (rays, size), 0).astype(F32)
        one_hot[:, at] = jnp.where(hit, 1.0, 0.0).astype(BF16)

    def activate(y, pre_ref, h_ref):
        pre_ref[...] = y
        h = (y * (1.0 + jnp.tanh(y))).astype(BF16)
        h_ref[...] = h
        return h

    def slope(y):
        a = jnp.tanh(y)
        return (1.0 + a) * (1.0 + y * (1.0 - a))

    def forward_all(blocks):
        def step(i, groups):
            first, second, third = (place_of(i - k) for k in range(3))
            if 3 in groups:
                hot = one_hot[:, third]
                y_head = dot_nn(wht[...], hidden_c[:, third]) + dot_nn(view_t[...], jnp.concatenate([hot, hot, hot], axis=0))
            if 2 in groups:
                y_two = dot_nn(wmt[0], hidden_a[0:256, second]) + wide_of(bias_b[0])
            if 1 in groups:
                encode(i)
            if 3 in groups:
                f = activate(y_head[0:128, :], feat_pre.at[:, third], feat.at[:, third])
            if 2 in groups:
                h = activate(y_two, pre_b.at[:, second], hidden_b.at[0:256, second])
            if 1 in groups:
                y_one = dot_nn(w0t[...], enc[:, first])
            if 3 in groups:
                y_color = dot_nn(wrt[...], f)[0:8, :] + y_head[128:136, :]
            if 2 in groups:
                y_three = dot_nn(wmt[1], h) + wide_of(bias_b[1])
            if 1 in groups:
                activate(y_one, pre_a.at[:, first], hidden_a.at[0:256, first])
            if 3 in groups:
                for k in range(per):
                    z_planes[pl.ds((i - 2) * per + k, 8, stride=pitch), :] = y_color[:, k * LANES : (k + 1) * LANES]
            if 2 in groups:
                activate(y_three, pre_c.at[:, second], hidden_c.at[:, second])

        def full_step(i, carry):
            step(i, (1, 2, 3))
            return carry

        step(jnp.int32(0), (1,))
        step(jnp.int32(1), (1, 2))
        lax.fori_loop(2, blocks, full_step, 0)
        step(blocks, (2, 3))
        step(blocks + 1, (3,))

    def backward_all(blocks):
        def step(start, size):
            per = size // LANES
            at = pl.ds(pl.multiple_of(start, LANES), size)
            dz = jnp.concatenate(
                [g_planes[pl.ds(start // LANES + k, 8, stride=pitch), :] for k in range(per)], axis=1
            )
            dzw = dz.astype(BF16).astype(F32)
            part = dzw[:, 0:LANES]
            for k in range(1, per):
                part = part + dzw[:, k * LANES : (k + 1) * LANES]
            g_sum[...] += part
            dz = jnp.concatenate([dzw, jnp.zeros_like(dzw)], axis=0).astype(BF16)
            dz_f = (dot_nn(wr[...], dz) * slope(feat_pre[:, at])).astype(BF16)
            both = jnp.concatenate([dz_f, dz], axis=0)
            up = dot_nn(whd[...], both)
            g_top[:, 0:144] += dot_nt(jnp.concatenate([hidden_c[:, at], one_hot[:, at], feat[:, at]], axis=0), both)
            dz = (up * slope(pre_c[:, at])).astype(BF16)
            up = dot_nn(wm[1], dz)
            made = dot_nt(hidden_b[:, at], dz)
            packed[352:608, :] += made[0:256, :]
            g_low[1] += made[256:272, :]
            dz = (up * slope(pre_b[:, at])).astype(BF16)
            up = dot_nn(wm[0], dz)
            made = dot_nt(hidden_a[:, at], dz)
            packed[96:352, :] += made[0:256, :]
            g_low[0] += made[256:272, :]
            dz = (up * slope(pre_a[:, at])).astype(BF16)
            g_in[...] += dot_nt(enc[:, at], dz)

        def large(i, carry):
            step(i * BACK, BACK)
            return carry

        def small(i, carry):
            step(i * BLOCK, BLOCK)
            return carry

        lax.fori_loop(0, blocks // 2, large, 0)
        lax.fori_loop(blocks // 2 * 2, blocks, small, 0)

    group = 8

    def chunk(first, passes, loss):
        xs[...] = jnp.where(lax.broadcasted_iota(jnp.int32, xs.shape, 1) == 3, -1.0, 0.0)
        x_planes[...] = jnp.full_like(x_planes, -1.0)

        def pack(p, part, g, offset):
            r0 = part * own + g * group
            item0 = (p * rays + r0).astype(F32)
            base = p * 8 * pk_pitch + r0
            moved = []
            for j in range(group):
                count = (counts, counts_two)[part][p, r0 + j]
                here = pk[pl.ds(base + j, 8, stride=pk_pitch), :]
                item = jnp.where(lane8 < count, item0 + float(j), -1.0)
                here = jnp.where(sub8 == 3, item, here)
                o = offset & (LANES - 1)
                moved.append((pltpu.roll(here, o, 1), o, offset >> 7))
                offset = offset + count
            for turned, o, t in moved:
                keep_low = lane8 >= o
                pltpu.store(xs.at[t], turned, mask=keep_low)
                pltpu.store(xs.at[t + 1], turned, mask=jnp.logical_not(keep_low))
            return offset

        def pack_pass(p, offset):
            for part in range(2):
                offset = lax.fori_loop(0, own // group, lambda g, o: pack(p, part, g, o), offset)
            return offset

        total = lax.fori_loop(first, first + passes, pack_pass, jnp.int32(0))
        blocks = jnp.maximum((total + BLOCK - 1) // BLOCK, 2)
        forward_all(blocks)

        def plane(ref, k):
            return ref[k * pitch : k * pitch + tiles, :]

        lane = lax.broadcasted_iota(jnp.int32, (tiles, LANES), 1)
        row = lax.broadcasted_iota(jnp.int32, (tiles, LANES), 0)
        item = plane(x_planes, 3)
        valid = item >= 0.0
        steps = (1, 2, 4, 8, 16, 32, 64)
        back = [jnp.logical_and(lane >= k, pltpu.roll(item, k, 1) == item) for k in steps]
        ahead = [jnp.logical_and(lane < LANES - k, pltpu.roll(item, LANES - k, 1) == item) for k in steps]
        end_before = jnp.broadcast_to(pltpu.roll(item[:, LANES - 1 : LANES], 1, 0), (tiles, LANES))
        start_after = jnp.broadcast_to(pltpu.roll(item[:, 0:1], tiles - 1, 0), (tiles, LANES))
        from_before = jnp.logical_and(row > 0, end_before == item)
        from_after = jnp.logical_and(row < tiles - 1, start_after == item)

        def scan(values):
            for k, near in zip(steps, back):
                values = values + jnp.where(near, pltpu.roll(values, k, 1), 0.0)
            carry = jnp.broadcast_to(pltpu.roll(values[:, LANES - 1 : LANES], 1, 0), (tiles, LANES))
            return values + jnp.where(from_before, carry, 0.0)

        def scan_back(values):
            for k, near in zip(steps, ahead):
                values = values + jnp.where(near, pltpu.roll(values, LANES - k, 1), 0.0)
            carry = jnp.broadcast_to(pltpu.roll(values[:, 0:1], tiles - 1, 0), (tiles, LANES))
            return values + jnp.where(from_after, carry, 0.0)

        def z_plane(k):
            return jnp.where(valid, plane(z_planes, k), 0.0)

        share = jnp.where(item >= rays, 1.0, COARSE_SHARE) * z_plane(7)
        space = jnp.where(valid, plane(x_planes, 7), 0.0)
        zd = z_plane(3) - 1.0
        density = jnp.maximum(zd, 0.0) + jnp.log1p(jnp.exp(-jnp.abs(zd)))
        tau = density * space
        inclusive = scan(tau)
        exclusive = inclusive - tau
        beyond = jnp.exp(-inclusive)
        weights = jnp.exp(-exclusive) - beyond
        weighted = jnp.zeros_like(tau)
        sums = jnp.zeros_like(tau)
        for c in range(3):
            sig = jax.nn.sigmoid(z_plane(c))
            rgb = 1.002 * sig - 0.001
            part = weights * rgb
            color = scan(part) + (scan_back(part) - part)
            error = color - z_plane(4 + c)
            sums = sums + error * error
            color_grad = (2.0 / 3.0) * share * error
            weighted = weighted + color_grad * rgb
            d_color = weights * color_grad * 1.002 * sig * (1.0 - sig)
            g_planes[c * pitch : c * pitch + tiles, :] = jnp.where(valid, d_color, 0.0)
        product = jnp.where(valid, weighted * weights, 0.0)
        after = scan_back(product) - product
        d_density = (beyond * weighted - after) * space * jax.nn.sigmoid(zd)
        g_planes[3 * pitch : 3 * pitch + tiles, :] = jnp.where(valid, d_density, 0.0)
        previous = jnp.where(lane >= 1, pltpu.roll(item, 1, 1), jnp.where(row > 0, end_before, -2.0))
        begins = jnp.logical_and(previous != item, valid)
        loss = loss + jnp.sum(jnp.where(begins, sums * share, 0.0)) * (1.0 / 3.0)

        backward_all(blocks)
        return loss

    wide[0:2, 0:own] = counts_vec[:, 0:own].astype(F32)
    wide[0:2, own:rays] = small_two[7:9, own:rays]
    everything = jnp.sum(wide[0:2, 0:rays])
    at_once = everything <= 1.0 * capacity
    chunks = jnp.where(at_once, 1, 2)
    passes = jnp.where(at_once, 2, 1)
    loss = lax.fori_loop(0, chunks, lambda i, loss: chunk(i, passes, loss), jnp.zeros((), F32))

    for a in range(4):
        for d in range(4):
            for k in range(2):
                at, to = 64 * k + 16 * d + 4 * a, 48 * k + 12 * a + 3 * d
                packed[to : to + 3, :] = g_in[at : at + 3, :]
    rays_sum = g_top[256 : 256 + rays, 0:128]
    packed[736:737, :] = g_in[67:68, :]
    packed[737:738, :] = g_low[0, 0:1, :]
    packed[738:739, :] = g_low[1, 0:1, :]
    for k in range(2):
        packed[608:736, 128 * k : 128 * k + 128] = g_top[128 * k : 128 * k + 128, 0:128]
        packed[739:740, 128 * k : 128 * k + 128] = g_top[128 * k : 128 * k + 128, 128:256].T[3:4, :]
    packed[740:741, 0:128] = jnp.sum(rays_sum, axis=0, keepdims=True)
    small = jnp.sum(g_sum[...], axis=1, keepdims=True)
    lane1 = lax.broadcasted_iota(jnp.int32, (1, LANES), 1)
    line = jnp.zeros((1, LANES), F32)
    for k in range(4):
        line = line + jnp.where(lane1 == k, jnp.broadcast_to(small[k : k + 1, :], (1, LANES)), 0.0)
    line = line + jnp.where(lane1 == 4, loss, 0.0)
    line = line + jnp.where(lane1 == 5, count_here, 0.0)
    packed[740:741, 128:256] = line
    packed[741:744, 0:128] = g_top[256 + rays : 384 + rays, 128:256].T[0:3, :]
    view_grad = jnp.zeros((32, 128), F32)
    for piece in split_three(rays_sum):
        view_grad = view_grad + dot_nn(venc[...], piece)
    packed[744:760, 0:128] = view_grad[0:16, :]
    packed[744:760, 128:256] = view_grad[16:32, :]
    for q in range(4):
        for ref, which in ((keep, place[0]), (send, place[1])):
            source = pl.multiple_of((which ^ q) * PART, 8)
            ref[q * PART : (q + 1) * PART, :] = packed[pl.ds(source, PART), :]


def field_gradients(find_place, local, other, params):
    means, variances, spacing, dirs, target, counts, mask = local
    means_two, variances_two, spacing_two, other_counts, other_rows = other
    w_in, w_mid, w_head, w_rgb, vec = params
    rays = dirs.shape[1]
    room = 17 * rays * LANES // 16 + LANES
    tiles = -(-(room - LANES) // (8 * LANES)) * 8
    pitch = tiles + 8 * (1 - tiles // 8 % 2)
    vmem = pl.BlockSpec(memory_space=pltpu.VMEM)
    smem = pl.BlockSpec(memory_space=pltpu.SMEM)
    hbm = pl.BlockSpec(memory_space=pl.ANY)
    scratch = [
        pltpu.VMEM((2 * 8 * (rays + 8), LANES), F32),
        pltpu.VMEM((room // LANES + 1, 8, LANES), F32),
        pltpu.VMEM((8 * pitch, LANES), F32),
        pltpu.VMEM((8 * pitch, LANES), F32),
        pltpu.VMEM((8 * pitch, LANES), F32),
        pltpu.VMEM((128, room), BF16),
        pltpu.VMEM((272, room), BF16),
        pltpu.VMEM((272, room), BF16),
        pltpu.VMEM((256, room), BF16),
        pltpu.VMEM((256, room), F32),
        pltpu.VMEM((256, room), F32),
        pltpu.VMEM((256, room), F32),
        pltpu.VMEM((128, room), BF16),
        pltpu.VMEM((128, room), F32),
        pltpu.VMEM((rays, room), BF16),
        pltpu.VMEM((16, LANES), F32),
        pltpu.VMEM((16, LANES), F32),
        pltpu.VMEM((128, 256), F32),
        pltpu.VMEM((256, 128), BF16),
        pltpu.VMEM((2, 256, 256), BF16),
        pltpu.VMEM((2, 256, 256), BF16),
        pltpu.VMEM((144, 256), BF16),
        pltpu.VMEM((256, 144), BF16),
        pltpu.VMEM((16, 128), BF16),
        pltpu.VMEM((128, 16), BF16),
        pltpu.VMEM((2, 256, 128), F32),
        pltpu.VMEM((144, 3 * rays), BF16),
        pltpu.VMEM((32, rays), BF16),
        pltpu.VMEM((128, 256), F32),
        pltpu.VMEM((2, 16, 256), F32),
        pltpu.VMEM((384 + rays, 256), F32),
        pltpu.VMEM((8, LANES), F32),
        pltpu.VMEM((8 * PART, 256), F32),
        pltpu.SemaphoreType.DMA((29,)),
    ]
    return pl.pallas_call(
        functools.partial(field_kernel, find_place),
        out_shape=[pltpu.VMEM((4 * PART, 256), F32)] * 2,
        in_specs=[smem] * 2 + [hbm] * 7 + [vmem] * 9,
        out_specs=[vmem, vmem],
        scratch_shapes=scratch,
        compiler_params=pltpu.CompilerParams(vmem_limit_bytes=63 << 20),
    )(
        counts,
        other_counts,
        means_two,
        variances_two,
        spacing_two,
        other_rows,
        means,
        variances,
        spacing,
        dirs,
        target,
        mask.reshape(1, rays),
        counts,
        w_in,
        w_mid,
        w_head,
        w_rgb.T,
        vec,
    )


def ray_rows(local):
    dirs, target, counts, mask = local[3:]
    rows = jnp.concatenate([dirs, target, mask[None].astype(F32), counts.astype(F32)], axis=0)
    return jnp.pad(rows, ((0, 16 - rows.shape[0]), (0, LANES - rows.shape[1])))


def adamw(weight, grad, first, second):
    first = BETA_ONE * first + (1.0 - BETA_ONE) * grad
    second = BETA_TWO * second + (1.0 - BETA_TWO) * grad * grad
    first_hat = first * (1.0 / (1.0 - BETA_ONE**STEP))
    second_hat = second * (1.0 / (1.0 - BETA_TWO**STEP))
    fresh = weight - LEARN_RATE * (first_hat / (jnp.sqrt(second_hat) + EPSILON) + DECAY * weight)
    return first, second, fresh


def update_kernel(find_place, *refs):
    place = find_place()
    pieces, refs = refs[0:8], refs[8:]
    weights, firsts, seconds = refs[0:5], refs[5:10], refs[10:15]
    loss, count = refs[15], refs[16]
    outs = refs[17:32]
    packed = refs[32]
    for k, ref in enumerate(pieces):
        block = place[k // 4] ^ (k % 4)
        packed[pl.ds(pl.multiple_of(block * PART, 8), PART), :] = ref[...]
    line = packed[740:741, 128:256]
    loss[0] = line[0, 4]
    count[0] = line[0, 5]
    scale = 1.0 / line[0:1, 5:6]

    def apply(group, at, grad):
        step = scale.reshape(1) if grad.ndim == 1 else scale
        made = adamw(weights[group][at], grad * step, firsts[group][at], seconds[group][at])
        for k in range(3):
            outs[3 * group + k][at] = made[k]

    everything = slice(None)
    apply(0, (everything, everything), packed[0:96, :])
    for k in range(2):
        apply(1, (k, everything, everything), packed[96 + 256 * k : 352 + 256 * k, :])
    for k in range(2):
        apply(2, (slice(128 * k, 128 * k + 128), everything), packed[608:736, 128 * k : 128 * k + 128])
    apply(2, (slice(256, 272), everything), packed[744:760, 0:128])
    apply(2, (slice(272, 283), everything), packed[744:755, 128:256])
    apply(3, (everything, everything), packed[741:744, 0:128])
    for k in range(9):
        line = packed[736 + k // 2 : 737 + k // 2, 128 * (k % 2) : 128 * (k % 2) + 128]
        apply(4, (pl.ds(128 * k, 128),), line.reshape(128))
    apply(4, (pl.ds(1152, 4),), packed[740:741, 128:132].reshape(4))


def update(find_place, pieces, params, firsts, seconds):
    vmem = pl.BlockSpec(memory_space=pltpu.VMEM)
    smem = pl.BlockSpec(memory_space=pltpu.SMEM)
    shapes = [jax.ShapeDtypeStruct((1,), F32)] * 2
    for array in params:
        shapes += [jax.ShapeDtypeStruct(array.shape, F32)] * 3
    return pl.pallas_call(
        functools.partial(update_kernel, find_place),
        out_shape=shapes,
        in_specs=[vmem] * 23,
        out_specs=[smem, smem] + [vmem] * 15,
        scratch_shapes=[pltpu.VMEM((8 * PART, 256), F32)],
        compiler_params=pltpu.CompilerParams(vmem_limit_bytes=32 << 20),
    )(*pieces, *params, *firsts, *seconds)


def xor_pairs(total, mask_of):
    return [(i, i ^ mask_of(i)) for i in range(total)]


def place_small():
    ray = lax.axis_index("rays")
    rep = lax.axis_index("rep")
    y, x, core = ray % 2, rep // 2, rep % 2
    xy, yx = 2 * x + y, 2 * y + x
    return (
        jnp.where(core == 0, xy, 4 + yx),
        jnp.where(core == 0, 4 + yx, xy),
    )


def reduce_small(keep, send, axes):
    core = xor_pairs(32, lambda i: 1)
    one = xor_pairs(32, lambda i: 4 if i & 1 else 2)
    two = xor_pairs(32, lambda i: 2 if i & 1 else 4)
    both = xor_pairs(32, lambda i: 6)
    z_one = xor_pairs(32, lambda i: 16 if i & 1 else 8)
    z_two = xor_pairs(32, lambda i: 8 if i & 1 else 16)

    def swap(value, pairs):
        return lax.ppermute(value, axes, pairs)

    square = (two, one, both)
    now = keep + swap(send, core)
    got = [swap(now[PART * (k + 1) : PART * (k + 2)], pairs) for k, pairs in enumerate(square)]
    own = (now[:PART] + got[0]) + (got[1] + got[2])
    own = own + swap(own, z_one)
    own = own + swap(own, z_two)
    parts = [own] + [swap(own, pairs) for pairs in square]
    return parts + [swap(part, core) for part in parts]


def on_device(
    small_mesh,
    sample_means,
    sample_vars,
    sample_spacing,
    view_dirs,
    target_rgb,
    sample_counts,
    ray_mask,
    w_in,
    w_mid,
    w_head,
    w_rgb,
    vectors,
    first_in,
    first_mid,
    first_head,
    first_rgb,
    first_vec,
    second_in,
    second_mid,
    second_head,
    second_rgb,
    second_vec,
):
    axes = ("rays", "rep")
    find_place = place_small if small_mesh else lambda: (0, 4)
    params = (w_in, w_mid, w_head, w_rgb, vectors)
    local = (sample_means, sample_vars, sample_spacing, view_dirs, target_rgb, sample_counts, ray_mask)
    other = (sample_means, sample_vars, sample_spacing, sample_counts, ray_rows(local))
    if small_mesh:
        core_pairs = xor_pairs(32, lambda i: 1)
        other = tuple(lax.ppermute(array, axes, core_pairs) for array in other)
    keep, send = field_gradients(find_place, local, other, params)
    if small_mesh:
        pieces = reduce_small(keep, send, axes)
    else:
        whole = lax.psum(jnp.concatenate([keep, send], axis=0), axes)
        pieces = [whole[PART * k : PART * (k + 1)] for k in range(8)]
    outs = update(
        find_place,
        pieces,
        (w_in, w_mid, w_head, w_rgb.T, vectors),
        (first_in, first_mid, first_head, first_rgb.T, first_vec),
        (second_in, second_mid, second_head, second_rgb.T, second_vec),
    )
    rgb = [out.T for out in outs[11:14]]
    return (outs[0].reshape(()), outs[1].reshape(()), *outs[2:11], *rgb, *outs[14:17])


def solution(mesh):
    rays = ("rays", "rep")
    in_specs = (
        P(None, None, rays, None),
        P(None, None, rays, None),
        P(None, rays, None),
        P(None, rays),
        P(None, rays),
        P(None, rays),
        P(rays),
    ) + (P(),) * 15
    small_mesh = mesh.shape["rays"] == 8 and mesh.shape["rep"] == 4

    def step(*args):
        return on_device(small_mesh, *args)

    return jax.shard_map(step, mesh=mesh, in_specs=in_specs, out_specs=(P(),) * 17, check_vma=False)
```

```python
import functools
import math

import jax
import jax.numpy as jnp
from jax import lax
from jax.experimental import pallas as pl
from jax.experimental.pallas import tpu as pltpu
from jax.sharding import PartitionSpec as P

L_POS = 16
L_DIR = 4
STEP = 7
LEARN_RATE = 0.05
BETA_ONE = 0.9
BETA_TWO = 0.999
EPSILON = 1e-08
DECAY = 0.01
COARSE_SHARE = 0.1

BLOCK = 512
BACK = 1024
LANES = 128
PART = 96

TURN_HEAD = 0.1591796875
TURN_REST = 1.0 / (2.0 * math.pi) - TURN_HEAD
SIN_POLY = (3.1415926343, -5.1677091056, 2.5500551036, -0.5981303017, 0.0773037189)
COS_POLY = (0.9999999314, -4.9347894708, 4.0583337486, -1.3313191807, 0.2184639082)

F32 = jnp.float32
BF16 = jnp.bfloat16


def split_three(values):
    head = values.astype(BF16)
    rest = values - head.astype(F32)
    middle = rest.astype(BF16)
    tail = (rest - middle.astype(F32)).astype(BF16)
    return head, middle, tail


def dot_nt(left, right):
    return lax.dot_general(left, right, (((1,), (1,)), ((), ())), preferred_element_type=F32)


def dot_nn(left, right):
    return jnp.dot(left, right, preferred_element_type=F32)


def poly(coefficients, square):
    total = jnp.full_like(square, coefficients[-1])
    for c in coefficients[-2::-1]:
        total = total * square + c
    return total


def sin_cos_turns(r):
    square = r * r
    s = r * poly(SIN_POLY, square)
    c = poly(COS_POLY, square)
    return (s + s) * c, 1.0 - (s + s) * s


def field_kernel(
    find_place,
    counts,
    counts_two,
    means_two,
    variances_two,
    spacing_two,
    dirs_two,
    target_two,
    mask_two,
    counts_vec_two,
    means,
    variances,
    spacing,
    dirs,
    target,
    mask,
    counts_vec,
    w_in,
    w_mid,
    w_head,
    w_rgb_t,
    vec,
    keep,
    send,
    pk,
    xs,
    x_planes,
    z_planes,
    g_planes,
    enc,
    hidden_a,
    hidden_b,
    hidden_c,
    pre_a,
    pre_b,
    pre_c,
    feat,
    feat_pre,
    one_hot,
    rows,
    wide,
    w0t,
    wmt,
    wm,
    wht,
    whd,
    wrt,
    wr,
    bias_b,
    view_t,
    venc,
    g_in,
    g_low,
    g_top,
    g_sum,
    packed,
    sem,
):
    place = find_place()
    rays = dirs.shape[1]
    own = rays // 2
    pitch = z_planes.shape[0] // 8
    pk_pitch = pk.shape[0] // 16
    capacity = hidden_c.shape[1] - LANES
    tiles = -(-capacity // (8 * LANES)) * 8
    copies = []
    for p in range(2):
        for k, sources in enumerate(((means, means_two), (variances, variances_two))):
            for c in range(3):
                for half, source in enumerate(sources):
                    to = (p * 8 + 4 * k + c) * pk_pitch + half * own
                    copies.append((source.at[p, c, pl.ds(half * own, own)], pk.at[pl.ds(to, own)]))
        for half, source in enumerate((spacing, spacing_two)):
            to = (p * 8 + 7) * pk_pitch + half * own
            copies.append((source.at[p, pl.ds(half * own, own)], pk.at[pl.ds(to, own)]))
    copies = [pltpu.make_async_copy(a, b, sem.at[k]) for k, (a, b) in enumerate(copies)]
    for copy in copies:
        copy.start()

    half = 0.5
    rows[...] = jnp.zeros_like(rows)
    for k in range(9):
        rows[k : k + 1, :] = vec[pl.ds(k * LANES, LANES)].reshape(1, LANES)
    rows[9:10, 0:4] = vec[pl.ds(9 * LANES, 4)].reshape(1, 4)
    vec_t = rows[0:16, :].T
    wide[0:128, :] = jnp.zeros((128, 256), F32)
    rounded = w_in[...].astype(BF16).astype(F32) * half
    for a in range(4):
        for d in range(4):
            for k in range(2):
                to, at = 64 * k + 16 * d + 4 * a, 48 * k + 12 * a + 3 * d
                wide[to : to + 3, :] = rounded[at : at + 3, :]
    b0 = jnp.concatenate([rows[0:1, :], rows[1:2, :]], axis=1) * half
    for a, piece in enumerate(split_three(b0)):
        wide[67 + 4 * a : 68 + 4 * a, :] = piece.astype(F32)
    w0t[...] = wide[0:128, :].T.astype(BF16)
    for k in range(2):
        rounded = w_mid[k].astype(BF16).astype(F32) * half
        wm[k] = rounded.astype(BF16)
        wmt[k] = rounded.T.astype(BF16)
        bias_b[k, 0:128, :] = jnp.broadcast_to(vec_t[:, 2 + 2 * k : 3 + 2 * k], (128, 128)) * half
        bias_b[k, 128:256, :] = jnp.broadcast_to(vec_t[:, 3 + 2 * k : 4 + 2 * k], (128, 128)) * half
    top = (w_head[0:256, :].astype(BF16).astype(F32) * half).T
    u_row = jnp.concatenate([rows[6:7, :], rows[7:8, :]], axis=1).astype(BF16).astype(F32)
    row16 = lax.broadcasted_iota(jnp.int32, (16, 256), 0)
    last = jnp.where(row16 == 3, u_row, 0.0)
    wht[0:128, :] = top.astype(BF16)
    wht[128:144, :] = last.astype(BF16)
    whd[...] = jnp.concatenate([top, last * half], axis=0).T.astype(BF16)
    wide[0:16, 0:128] = jnp.zeros((16, 128), F32)
    wide[0:3, 0:128] = w_rgb_t[...].astype(BF16).astype(F32)
    wrt[...] = wide[0:16, 0:128].astype(BF16)
    wr[...] = (wide[0:16, 0:128].T * half).astype(BF16)

    def both_halves(at, one, two):
        n = one.shape[0]
        wide[at : at + n, 0:own] = one[:, 0:own].astype(F32)
        wide[at : at + n, own:rays] = two[:, own:rays].astype(F32)

    wide[0:32, 0:128] = jnp.zeros((32, 128), F32)
    both_halves(0, dirs, dirs_two)
    d = wide[0:3, 0:rays]
    for l in range(L_DIR):
        wide[3 + 3 * l : 6 + 3 * l, 0:rays] = jnp.sin(d * (2.0**l))
        wide[15 + 3 * l : 18 + 3 * l, 0:rays] = jnp.cos(d * (2.0**l))
    venc[...] = wide[0:32, 0:rays].astype(BF16)
    wide[0:32, 128:256] = jnp.zeros((32, 128), F32)
    wide[0:27, 128:256] = w_head[256:283, :].astype(BF16).astype(F32)
    view = lax.dot_general(
        wide[0:32, 128:256].astype(BF16), venc[...], (((0,), (0,)), ((), ())), preferred_element_type=F32
    )
    view = (view + vec_t[:, 8:9]) * half
    wide[0:16, 0:128] = jnp.zeros((16, 128), F32)
    wide[0:4, 0:rays] = jnp.broadcast_to(vec_t[0:4, 9:10], (4, rays))
    both_halves(4, target, target_two)
    both_halves(7, mask, mask_two)
    count_here = jnp.sum(wide[7:8, 0:128])
    view_t[...] = jnp.concatenate(split_three(jnp.concatenate([view, wide[0:16, 0:rays]], axis=0)), axis=1)

    one_row = (lax.broadcasted_iota(jnp.int32, (16, hidden_a.shape[1]), 0) == 0).astype(BF16)
    hidden_a[256:272, :] = one_row
    hidden_b[256:272, :] = one_row
    for ref in (g_planes, g_in, g_low, g_top, g_sum, packed):
        ref[...] = jnp.zeros_like(ref)

    lane8 = lax.broadcasted_iota(jnp.int32, (8, LANES), 1)
    sub8 = lax.broadcasted_iota(jnp.int32, (8, LANES), 0)
    sub16 = lax.broadcasted_iota(jnp.int32, (16, LANES), 0)
    anchor = (jnp.int32(1) << (4 * (sub16 // 4))).astype(F32)
    decay_rate = anchor * anchor * (-0.5)

    for copy in copies:
        copy.wait()

    size = BLOCK
    per = size // LANES

    def wide_of(tile):
        return jnp.concatenate([tile] * per, axis=1)

    def place_of(i):
        return pl.ds(pl.multiple_of(i * size, LANES), size)

    def encode(i):
        at = place_of(i)
        x = [xs[i * per + k] for k in range(per)]
        for k in range(per):
            x_planes[pl.ds(i * per + k, 8, stride=pitch), :] = x[k]
        x = jnp.concatenate(x, axis=1)
        sub = lax.broadcasted_iota(jnp.int32, (8, size), 0)
        turned = pltpu.roll(x, 4, 0)
        low = sub < 4
        used = sub % 4 < 3
        mean = jnp.where(used, jnp.where(low, x, turned), 0.0)
        var = jnp.where(used, jnp.where(low, turned, x), 0.0)
        m1 = jnp.round(mean * 2.0**11) * 2.0**-11
        p1 = m1 * TURN_HEAD
        p2 = m1 * TURN_REST + (mean - m1) * (TURN_HEAD + TURN_REST)
        hi = jnp.round((p1 + p2) * 2.0**20) * 2.0**-20
        lo = (p1 - hi) + p2
        pw = wide_of(anchor)
        a = jnp.concatenate([hi, hi], axis=0) * pw
        a = (a - jnp.round(a)) + jnp.concatenate([lo, lo], axis=0) * pw
        s, c = sin_cos_turns(a)
        var = jnp.concatenate([var, var], axis=0) * wide_of(decay_rate)
        for d in range(4):
            damp = jnp.exp(var * (4.0**d))
            enc[16 * d : 16 * d + 16, at] = (s * damp).astype(BF16)
            enc[64 + 16 * d : 80 + 16 * d, at] = (c * damp).astype(BF16)
            twice = s + s
            s, c = twice * c, 1.0 - twice * s
        item = x[3:4, :]
        ray = jnp.where(item >= rays, item - rays, item)
        hit = jnp.broadcast_to(ray, (rays, size)) == lax.broadcasted_iota(jnp.int32, (rays, size), 0).astype(F32)
        one_hot[:, at] = jnp.where(hit, 1.0, 0.0).astype(BF16)

    def activate(y, pre_ref, h_ref):
        pre_ref[...] = y
        h = (y * (1.0 + jnp.tanh(y))).astype(BF16)
        h_ref[...] = h
        return h

    def slope(y):
        a = jnp.tanh(y)
        return (1.0 + a) * (1.0 + y * (1.0 - a))

    def forward_all(blocks):
        def step(i, groups):
            first, second, third = (place_of(i - k) for k in range(3))
            if 3 in groups:
                hot = one_hot[:, third]
                y_head = dot_nn(wht[...], hidden_c[:, third]) + dot_nn(view_t[...], jnp.concatenate([hot, hot, hot], axis=0))
            if 2 in groups:
                y_two = dot_nn(wmt[0], hidden_a[0:256, second]) + wide_of(bias_b[0])
            if 1 in groups:
                encode(i)
            if 3 in groups:
                f = activate(y_head[0:128, :], feat_pre.at[:, third], feat.at[:, third])
            if 2 in groups:
                h = activate(y_two, pre_b.at[:, second], hidden_b.at[0:256, second])
            if 1 in groups:
                y_one = dot_nn(w0t[...], enc[:, first])
            if 3 in groups:
                y_color = dot_nn(wrt[...], f)[0:8, :] + y_head[128:136, :]
            if 2 in groups:
                y_three = dot_nn(wmt[1], h) + wide_of(bias_b[1])
            if 1 in groups:
                activate(y_one, pre_a.at[:, first], hidden_a.at[0:256, first])
            if 3 in groups:
                for k in range(per):
                    z_planes[pl.ds((i - 2) * per + k, 8, stride=pitch), :] = y_color[:, k * LANES : (k + 1) * LANES]
            if 2 in groups:
                activate(y_three, pre_c.at[:, second], hidden_c.at[:, second])

        def full_step(i, carry):
            step(i, (1, 2, 3))
            return carry

        step(jnp.int32(0), (1,))
        step(jnp.int32(1), (1, 2))
        lax.fori_loop(2, blocks, full_step, 0)
        step(blocks, (2, 3))
        step(blocks + 1, (3,))

    def backward_all(blocks):
        def step(start, size):
            per = size // LANES
            at = pl.ds(pl.multiple_of(start, LANES), size)
            dz = jnp.concatenate(
                [g_planes[pl.ds(start // LANES + k, 8, stride=pitch), :] for k in range(per)], axis=1
            )
            dzw = dz.astype(BF16).astype(F32)
            part = dzw[:, 0:LANES]
            for k in range(1, per):
                part = part + dzw[:, k * LANES : (k + 1) * LANES]
            g_sum[...] += part
            dz = jnp.concatenate([dzw, jnp.zeros_like(dzw)], axis=0).astype(BF16)
            dz_f = (dot_nn(wr[...], dz) * slope(feat_pre[:, at])).astype(BF16)
            both = jnp.concatenate([dz_f, dz], axis=0)
            up = dot_nn(whd[...], both)
            g_top[:, 0:144] += dot_nt(jnp.concatenate([hidden_c[:, at], one_hot[:, at], feat[:, at]], axis=0), both)
            dz = (up * slope(pre_c[:, at])).astype(BF16)
            up = dot_nn(wm[1], dz)
            made = dot_nt(hidden_b[:, at], dz)
            packed[352:608, :] += made[0:256, :]
            g_low[1] += made[256:272, :]
            dz = (up * slope(pre_b[:, at])).astype(BF16)
            up = dot_nn(wm[0], dz)
            made = dot_nt(hidden_a[:, at], dz)
            packed[96:352, :] += made[0:256, :]
            g_low[0] += made[256:272, :]
            dz = (up * slope(pre_a[:, at])).astype(BF16)
            g_in[...] += dot_nt(enc[:, at], dz)

        def large(i, carry):
            step(i * BACK, BACK)
            return carry

        def small(i, carry):
            step(i * BLOCK, BLOCK)
            return carry

        lax.fori_loop(0, blocks // 2, large, 0)
        lax.fori_loop(blocks // 2 * 2, blocks, small, 0)

    group = 8

    def chunk(first, passes, loss):
        xs[...] = jnp.where(lax.broadcasted_iota(jnp.int32, xs.shape, 1) == 3, -1.0, 0.0)
        x_planes[...] = jnp.full_like(x_planes, -1.0)

        def pack(p, part, g, offset):
            r0 = part * own + g * group
            item0 = (p * rays + r0).astype(F32)
            base = p * 8 * pk_pitch + r0
            moved = []
            for j in range(group):
                count = (counts, counts_two)[part][p, r0 + j]
                here = pk[pl.ds(base + j, 8, stride=pk_pitch), :]
                item = jnp.where(lane8 < count, item0 + float(j), -1.0)
                here = jnp.where(sub8 == 3, item, here)
                o = offset & (LANES - 1)
                moved.append((pltpu.roll(here, o, 1), o, offset >> 7))
                offset = offset + count
            for turned, o, t in moved:
                keep_low = lane8 >= o
                pltpu.store(xs.at[t], turned, mask=keep_low)
                pltpu.store(xs.at[t + 1], turned, mask=jnp.logical_not(keep_low))
            return offset

        def pack_pass(p, offset):
            for part in range(2):
                offset = lax.fori_loop(0, own // group, lambda g, o: pack(p, part, g, o), offset)
            return offset

        total = lax.fori_loop(first, first + passes, pack_pass, jnp.int32(0))
        blocks = jnp.maximum((total + BLOCK - 1) // BLOCK, 2)
        forward_all(blocks)

        def plane(ref, k):
            return ref[k * pitch : k * pitch + tiles, :]

        lane = lax.broadcasted_iota(jnp.int32, (tiles, LANES), 1)
        row = lax.broadcasted_iota(jnp.int32, (tiles, LANES), 0)
        item = plane(x_planes, 3)
        valid = item >= 0.0
        steps = (1, 2, 4, 8, 16, 32, 64)
        back = [jnp.logical_and(lane >= k, pltpu.roll(item, k, 1) == item) for k in steps]
        ahead = [jnp.logical_and(lane < LANES - k, pltpu.roll(item, LANES - k, 1) == item) for k in steps]
        end_before = jnp.broadcast_to(pltpu.roll(item[:, LANES - 1 : LANES], 1, 0), (tiles, LANES))
        start_after = jnp.broadcast_to(pltpu.roll(item[:, 0:1], tiles - 1, 0), (tiles, LANES))
        from_before = jnp.logical_and(row > 0, end_before == item)
        from_after = jnp.logical_and(row < tiles - 1, start_after == item)

        def scan(values):
            for k, near in zip(steps, back):
                values = values + jnp.where(near, pltpu.roll(values, k, 1), 0.0)
            carry = jnp.broadcast_to(pltpu.roll(values[:, LANES - 1 : LANES], 1, 0), (tiles, LANES))
            return values + jnp.where(from_before, carry, 0.0)

        def scan_back(values):
            for k, near in zip(steps, ahead):
                values = values + jnp.where(near, pltpu.roll(values, LANES - k, 1), 0.0)
            carry = jnp.broadcast_to(pltpu.roll(values[:, 0:1], tiles - 1, 0), (tiles, LANES))
            return values + jnp.where(from_after, carry, 0.0)

        def z_plane(k):
            return jnp.where(valid, plane(z_planes, k), 0.0)

        share = jnp.where(item >= rays, 1.0, COARSE_SHARE) * z_plane(7)
        space = jnp.where(valid, plane(x_planes, 7), 0.0)
        zd = z_plane(3) - 1.0
        density = jnp.maximum(zd, 0.0) + jnp.log1p(jnp.exp(-jnp.abs(zd)))
        tau = density * space
        inclusive = scan(tau)
        exclusive = inclusive - tau
        beyond = jnp.exp(-inclusive)
        weights = jnp.exp(-exclusive) - beyond
        weighted = jnp.zeros_like(tau)
        sums = jnp.zeros_like(tau)
        for c in range(3):
            sig = jax.nn.sigmoid(z_plane(c))
            rgb = 1.002 * sig - 0.001
            part = weights * rgb
            color = scan(part) + (scan_back(part) - part)
            error = color - z_plane(4 + c)
            sums = sums + error * error
            color_grad = (2.0 / 3.0) * share * error
            weighted = weighted + color_grad * rgb
            d_color = weights * color_grad * 1.002 * sig * (1.0 - sig)
            g_planes[c * pitch : c * pitch + tiles, :] = jnp.where(valid, d_color, 0.0)
        product = jnp.where(valid, weighted * weights, 0.0)
        after = scan_back(product) - product
        d_density = (beyond * weighted - after) * space * jax.nn.sigmoid(zd)
        g_planes[3 * pitch : 3 * pitch + tiles, :] = jnp.where(valid, d_density, 0.0)
        previous = jnp.where(lane >= 1, pltpu.roll(item, 1, 1), jnp.where(row > 0, end_before, -2.0))
        begins = jnp.logical_and(previous != item, valid)
        loss = loss + jnp.sum(jnp.where(begins, sums * share, 0.0)) * (1.0 / 3.0)

        backward_all(blocks)
        return loss

    both_halves(0, counts_vec, counts_vec_two)
    everything = jnp.sum(wide[0:2, 0:rays])
    at_once = everything <= 1.0 * capacity
    chunks = jnp.where(at_once, 1, 2)
    passes = jnp.where(at_once, 2, 1)
    loss = lax.fori_loop(0, chunks, lambda i, loss: chunk(i, passes, loss), jnp.zeros((), F32))

    for a in range(4):
        for d in range(4):
            for k in range(2):
                at, to = 64 * k + 16 * d + 4 * a, 48 * k + 12 * a + 3 * d
                packed[to : to + 3, :] = g_in[at : at + 3, :]
    rays_sum = g_top[256 : 256 + rays, 0:128]
    packed[736:737, :] = g_in[67:68, :]
    packed[737:738, :] = g_low[0, 0:1, :]
    packed[738:739, :] = g_low[1, 0:1, :]
    for k in range(2):
        packed[608:736, 128 * k : 128 * k + 128] = g_top[128 * k : 128 * k + 128, 0:128]
        packed[739:740, 128 * k : 128 * k + 128] = g_top[128 * k : 128 * k + 128, 128:256].T[3:4, :]
    packed[740:741, 0:128] = jnp.sum(rays_sum, axis=0, keepdims=True)
    small = jnp.sum(g_sum[...], axis=1, keepdims=True)
    lane1 = lax.broadcasted_iota(jnp.int32, (1, LANES), 1)
    line = jnp.zeros((1, LANES), F32)
    for k in range(4):
        line = line + jnp.where(lane1 == k, jnp.broadcast_to(small[k : k + 1, :], (1, LANES)), 0.0)
    line = line + jnp.where(lane1 == 4, loss, 0.0)
    line = line + jnp.where(lane1 == 5, count_here, 0.0)
    packed[740:741, 128:256] = line
    packed[741:744, 0:128] = g_top[256 + rays : 384 + rays, 128:256].T[0:3, :]
    view_grad = jnp.zeros((32, 128), F32)
    for piece in split_three(rays_sum):
        view_grad = view_grad + dot_nn(venc[...], piece)
    packed[744:760, 0:128] = view_grad[0:16, :]
    packed[744:760, 128:256] = view_grad[16:32, :]
    for q in range(4):
        for ref, which in ((keep, place[0]), (send, place[1])):
            source = pl.multiple_of((which ^ q) * PART, 8)
            ref[q * PART : (q + 1) * PART, :] = packed[pl.ds(source, PART), :]


def field_gradients(find_place, local, other, params):
    means, variances, spacing, dirs, target, counts, mask = local
    means_two, variances_two, spacing_two, dirs_two, target_two, other_counts, mask_two = other
    w_in, w_mid, w_head, w_rgb, vec = params
    rays = dirs.shape[1]
    room = 17 * rays * LANES // 16 + LANES
    tiles = -(-(room - LANES) // (8 * LANES)) * 8
    pitch = tiles + 8 * (1 - tiles // 8 % 2)
    vmem = pl.BlockSpec(memory_space=pltpu.VMEM)
    smem = pl.BlockSpec(memory_space=pltpu.SMEM)
    hbm = pl.BlockSpec(memory_space=pl.ANY)
    scratch = [
        pltpu.VMEM((2 * 8 * (rays + 8), LANES), F32),
        pltpu.VMEM((room // LANES + 1, 8, LANES), F32),
        pltpu.VMEM((8 * pitch, LANES), F32),
        pltpu.VMEM((8 * pitch, LANES), F32),
        pltpu.VMEM((8 * pitch, LANES), F32),
        pltpu.VMEM((128, room), BF16),
        pltpu.VMEM((272, room), BF16),
        pltpu.VMEM((272, room), BF16),
        pltpu.VMEM((256, room), BF16),
        pltpu.VMEM((256, room), F32),
        pltpu.VMEM((256, room), F32),
        pltpu.VMEM((256, room), F32),
        pltpu.VMEM((128, room), BF16),
        pltpu.VMEM((128, room), F32),
        pltpu.VMEM((rays, room), BF16),
        pltpu.VMEM((16, LANES), F32),
        pltpu.VMEM((128, 256), F32),
        pltpu.VMEM((256, 128), BF16),
        pltpu.VMEM((2, 256, 256), BF16),
        pltpu.VMEM((2, 256, 256), BF16),
        pltpu.VMEM((144, 256), BF16),
        pltpu.VMEM((256, 144), BF16),
        pltpu.VMEM((16, 128), BF16),
        pltpu.VMEM((128, 16), BF16),
        pltpu.VMEM((2, 256, 128), F32),
        pltpu.VMEM((144, 3 * rays), BF16),
        pltpu.VMEM((32, rays), BF16),
        pltpu.VMEM((128, 256), F32),
        pltpu.VMEM((2, 16, 256), F32),
        pltpu.VMEM((384 + rays, 256), F32),
        pltpu.VMEM((8, LANES), F32),
        pltpu.VMEM((8 * PART, 256), F32),
        pltpu.SemaphoreType.DMA((28,)),
    ]
    return pl.pallas_call(
        functools.partial(field_kernel, find_place),
        out_shape=[pltpu.VMEM((4 * PART, 256), F32)] * 2,
        in_specs=[smem] * 2 + [hbm] * 3 + [vmem] * 4 + [hbm] * 3 + [vmem] * 9,
        out_specs=[vmem, vmem],
        scratch_shapes=scratch,
        compiler_params=pltpu.CompilerParams(vmem_limit_bytes=63 << 20),
    )(
        counts,
        other_counts,
        means_two,
        variances_two,
        spacing_two,
        dirs_two,
        target_two,
        mask_two.reshape(1, rays),
        other_counts,
        means,
        variances,
        spacing,
        dirs,
        target,
        mask.reshape(1, rays),
        counts,
        w_in,
        w_mid,
        w_head,
        w_rgb.T,
        vec,
    )


def adamw(weight, grad, first, second):
    first = BETA_ONE * first + (1.0 - BETA_ONE) * grad
    second = BETA_TWO * second + (1.0 - BETA_TWO) * grad * grad
    first_hat = first * (1.0 / (1.0 - BETA_ONE**STEP))
    second_hat = second * (1.0 / (1.0 - BETA_TWO**STEP))
    fresh = weight - LEARN_RATE * (first_hat / (jnp.sqrt(second_hat) + EPSILON) + DECAY * weight)
    return first, second, fresh


def update_kernel(find_place, *refs):
    place = find_place()
    pieces, refs = refs[0:8], refs[8:]
    weights, firsts, seconds = refs[0:5], refs[5:10], refs[10:15]
    loss, count = refs[15], refs[16]
    outs = refs[17:32]
    packed = refs[32]
    for k, ref in enumerate(pieces):
        block = place[k // 4] ^ (k % 4)
        packed[pl.ds(pl.multiple_of(block * PART, 8), PART), :] = ref[...]
    line = packed[740:741, 128:256]
    loss[0] = line[0, 4]
    count[0] = line[0, 5]
    scale = 1.0 / line[0:1, 5:6]

    def apply(group, at, grad):
        step = scale.reshape(1) if grad.ndim == 1 else scale
        made = adamw(weights[group][at], grad * step, firsts[group][at], seconds[group][at])
        for k in range(3):
            outs[3 * group + k][at] = made[k]

    everything = slice(None)
    apply(0, (everything, everything), packed[0:96, :])
    for k in range(2):
        apply(1, (k, everything, everything), packed[96 + 256 * k : 352 + 256 * k, :])
    for k in range(2):
        apply(2, (slice(128 * k, 128 * k + 128), everything), packed[608:736, 128 * k : 128 * k + 128])
    apply(2, (slice(256, 272), everything), packed[744:760, 0:128])
    apply(2, (slice(272, 283), everything), packed[744:755, 128:256])
    apply(3, (everything, everything), packed[741:744, 0:128])
    for k in range(9):
        line = packed[736 + k // 2 : 737 + k // 2, 128 * (k % 2) : 128 * (k % 2) + 128]
        apply(4, (pl.ds(128 * k, 128),), line.reshape(128))
    apply(4, (pl.ds(1152, 4),), packed[740:741, 128:132].reshape(4))


def update(find_place, pieces, params, firsts, seconds):
    vmem = pl.BlockSpec(memory_space=pltpu.VMEM)
    smem = pl.BlockSpec(memory_space=pltpu.SMEM)
    shapes = [jax.ShapeDtypeStruct((1,), F32)] * 2
    for array in params:
        shapes += [jax.ShapeDtypeStruct(array.shape, F32)] * 3
    return pl.pallas_call(
        functools.partial(update_kernel, find_place),
        out_shape=shapes,
        in_specs=[vmem] * 23,
        out_specs=[smem, smem] + [vmem] * 15,
        scratch_shapes=[pltpu.VMEM((8 * PART, 256), F32)],
        compiler_params=pltpu.CompilerParams(vmem_limit_bytes=32 << 20),
    )(*pieces, *params, *firsts, *seconds)


def xor_pairs(total, mask_of):
    return [(i, i ^ mask_of(i)) for i in range(total)]


def place_small():
    ray = lax.axis_index("rays")
    rep = lax.axis_index("rep")
    y, x, core = ray % 2, rep // 2, rep % 2
    xy, yx = 2 * x + y, 2 * y + x
    return (
        jnp.where(core == 0, xy, 4 + yx),
        jnp.where(core == 0, 4 + yx, xy),
    )


def reduce_small(keep, send, axes):
    core = xor_pairs(32, lambda i: 1)
    one = xor_pairs(32, lambda i: 4 if i & 1 else 2)
    two = xor_pairs(32, lambda i: 2 if i & 1 else 4)
    both = xor_pairs(32, lambda i: 6)
    z_one = xor_pairs(32, lambda i: 16 if i & 1 else 8)
    z_two = xor_pairs(32, lambda i: 8 if i & 1 else 16)

    def swap(value, pairs):
        return lax.ppermute(value, axes, pairs)

    square = (two, one, both)
    now = keep + swap(send, core)
    got = [swap(now[PART * (k + 1) : PART * (k + 2)], pairs) for k, pairs in enumerate(square)]
    own = (now[:PART] + got[0]) + (got[1] + got[2])
    own = own + swap(own, z_one)
    own = own + swap(own, z_two)
    parts = [own] + [swap(own, pairs) for pairs in square]
    return parts + [swap(part, core) for part in parts]


def on_device(
    small_mesh,
    sample_means,
    sample_vars,
    sample_spacing,
    view_dirs,
    target_rgb,
    sample_counts,
    ray_mask,
    w_in,
    w_mid,
    w_head,
    w_rgb,
    vectors,
    first_in,
    first_mid,
    first_head,
    first_rgb,
    first_vec,
    second_in,
    second_mid,
    second_head,
    second_rgb,
    second_vec,
):
    axes = ("rays", "rep")
    find_place = place_small if small_mesh else lambda: (0, 4)
    params = (w_in, w_mid, w_head, w_rgb, vectors)
    local = (sample_means, sample_vars, sample_spacing, view_dirs, target_rgb, sample_counts, ray_mask)
    other = local
    if small_mesh:
        core_pairs = xor_pairs(32, lambda i: 1)
        other = tuple(lax.ppermute(array, axes, core_pairs) for array in other)
    keep, send = field_gradients(find_place, local, other, params)
    if small_mesh:
        pieces = reduce_small(keep, send, axes)
    else:
        whole = lax.psum(jnp.concatenate([keep, send], axis=0), axes)
        pieces = [whole[PART * k : PART * (k + 1)] for k in range(8)]
    outs = update(
        find_place,
        pieces,
        (w_in, w_mid, w_head, w_rgb.T, vectors),
        (first_in, first_mid, first_head, first_rgb.T, first_vec),
        (second_in, second_mid, second_head, second_rgb.T, second_vec),
    )
    rgb = [out.T for out in outs[11:14]]
    return (outs[0].reshape(()), outs[1].reshape(()), *outs[2:11], *rgb, *outs[14:17])


def solution(mesh):
    rays = ("rays", "rep")
    in_specs = (
        P(None, None, rays, None),
        P(None, None, rays, None),
        P(None, rays, None),
        P(None, rays),
        P(None, rays),
        P(None, rays),
        P(rays),
    ) + (P(),) * 15
    small_mesh = mesh.shape["rays"] == 8 and mesh.shape["rep"] == 4

    def step(*args):
        return on_device(small_mesh, *args)

    return jax.shard_map(step, mesh=mesh, in_specs=in_specs, out_specs=(P(),) * 17, check_vma=False)
```

```python
import functools
import math

import jax
import jax.numpy as jnp
from jax import lax
from jax.experimental import pallas as pl
from jax.experimental.pallas import tpu as pltpu
from jax.sharding import PartitionSpec as P

L_POS = 16
L_DIR = 4
STEP = 7
LEARN_RATE = 0.05
BETA_ONE = 0.9
BETA_TWO = 0.999
EPSILON = 1e-08
DECAY = 0.01
COARSE_SHARE = 0.1

BLOCK = 512
BACK = 1024
LANES = 128
PART = 96

TURN_HEAD = 0.1591796875
TURN_REST = 1.0 / (2.0 * math.pi) - TURN_HEAD
SIN_POLY = (3.1415926343, -5.1677091056, 2.5500551036, -0.5981303017, 0.0773037189)
COS_POLY = (0.9999999314, -4.9347894708, 4.0583337486, -1.3313191807, 0.2184639082)

F32 = jnp.float32
BF16 = jnp.bfloat16


def split_three(values):
    head = values.astype(BF16)
    rest = values - head.astype(F32)
    middle = rest.astype(BF16)
    tail = (rest - middle.astype(F32)).astype(BF16)
    return head, middle, tail


def dot_nt(left, right):
    return lax.dot_general(left, right, (((1,), (1,)), ((), ())), preferred_element_type=F32)


def dot_nn(left, right):
    return jnp.dot(left, right, preferred_element_type=F32)


def poly(coefficients, square):
    total = jnp.full_like(square, coefficients[-1])
    for c in coefficients[-2::-1]:
        total = total * square + c
    return total


def sin_cos_turns(r):
    square = r * r
    s = r * poly(SIN_POLY, square)
    c = poly(COS_POLY, square)
    return (s + s) * c, 1.0 - (s + s) * s


def field_kernel(
    find_place,
    counts,
    counts_other,
    means_two,
    variances_two,
    spacing_two,
    other,
    means,
    variances,
    spacing,
    dirs,
    target,
    mask,
    counts_vec,
    w_in,
    w_mid,
    w_head,
    w_rgb_t,
    vec,
    keep,
    send,
    pk,
    xs,
    x_planes,
    z_planes,
    g_planes,
    enc,
    hidden_a,
    hidden_b,
    hidden_c,
    pre_a,
    pre_b,
    pre_c,
    feat,
    feat_pre,
    one_hot,
    small_two,
    counts_two,
    rows,
    wide,
    w0t,
    wmt,
    wm,
    wht,
    whd,
    wrt,
    wr,
    bias_b,
    view_t,
    venc,
    g_in,
    g_low,
    g_top,
    g_sum,
    packed,
    sem,
):
    place = find_place()
    rays = dirs.shape[1]
    own = rays // 2
    pitch = z_planes.shape[0] // 8
    pk_pitch = pk.shape[0] // 16
    capacity = hidden_c.shape[1] - LANES
    tiles = -(-capacity // (8 * LANES)) * 8
    copies = []
    for p in range(2):
        for k, sources in enumerate(((means, means_two), (variances, variances_two))):
            for c in range(3):
                for half, source in enumerate(sources):
                    to = (p * 8 + 4 * k + c) * pk_pitch + half * own
                    copies.append((source.at[p, c, pl.ds(half * own, own)], pk.at[pl.ds(to, own)]))
        for half, source in enumerate((spacing, spacing_two)):
            to = (p * 8 + 7) * pk_pitch + half * own
            copies.append((source.at[p, pl.ds(half * own, own)], pk.at[pl.ds(to, own)]))
    copies.append((counts_other, counts_two))
    copies.append((other, small_two))
    copies = [pltpu.make_async_copy(a, b, sem.at[k]) for k, (a, b) in enumerate(copies)]
    for copy in copies:
        copy.start()

    half = 0.5
    rows[...] = jnp.zeros_like(rows)
    for k in range(9):
        rows[k : k + 1, :] = vec[pl.ds(k * LANES, LANES)].reshape(1, LANES)
    rows[9:10, 0:4] = vec[pl.ds(9 * LANES, 4)].reshape(1, 4)
    vec_t = rows[0:16, :].T
    wide[0:128, :] = jnp.zeros((128, 256), F32)
    rounded = w_in[...].astype(BF16).astype(F32) * half
    for a in range(4):
        for d in range(4):
            for k in range(2):
                to, at = 64 * k + 16 * d + 4 * a, 48 * k + 12 * a + 3 * d
                wide[to : to + 3, :] = rounded[at : at + 3, :]
    b0 = jnp.concatenate([rows[0:1, :], rows[1:2, :]], axis=1) * half
    for a, piece in enumerate(split_three(b0)):
        wide[67 + 4 * a : 68 + 4 * a, :] = piece.astype(F32)
    w0t[...] = wide[0:128, :].T.astype(BF16)
    for k in range(2):
        rounded = w_mid[k].astype(BF16).astype(F32) * half
        wm[k] = rounded.astype(BF16)
        wmt[k] = rounded.T.astype(BF16)
        bias_b[k, 0:128, :] = jnp.broadcast_to(vec_t[:, 2 + 2 * k : 3 + 2 * k], (128, 128)) * half
        bias_b[k, 128:256, :] = jnp.broadcast_to(vec_t[:, 3 + 2 * k : 4 + 2 * k], (128, 128)) * half
    top = (w_head[0:256, :].astype(BF16).astype(F32) * half).T
    u_row = jnp.concatenate([rows[6:7, :], rows[7:8, :]], axis=1).astype(BF16).astype(F32)
    row16 = lax.broadcasted_iota(jnp.int32, (16, 256), 0)
    last = jnp.where(row16 == 3, u_row, 0.0)
    wht[0:128, :] = top.astype(BF16)
    wht[128:144, :] = last.astype(BF16)
    whd[...] = jnp.concatenate([top, last * half], axis=0).T.astype(BF16)
    wide[0:16, 0:128] = jnp.zeros((16, 128), F32)
    wide[0:3, 0:128] = w_rgb_t[...].astype(BF16).astype(F32)
    wrt[...] = wide[0:16, 0:128].astype(BF16)
    wr[...] = (wide[0:16, 0:128].T * half).astype(BF16)

    copies[-1].wait()

    def both_halves(at, one, row):
        n = one.shape[0]
        wide[at : at + n, 0:own] = one[:, 0:own].astype(F32)
        wide[at : at + n, own:rays] = small_two[row : row + n, own:rays]

    wide[0:32, 0:128] = jnp.zeros((32, 128), F32)
    both_halves(0, dirs, 0)
    d = wide[0:3, 0:rays]
    for l in range(L_DIR):
        wide[3 + 3 * l : 6 + 3 * l, 0:rays] = jnp.sin(d * (2.0**l))
        wide[15 + 3 * l : 18 + 3 * l, 0:rays] = jnp.cos(d * (2.0**l))
    venc[...] = wide[0:32, 0:rays].astype(BF16)
    wide[0:32, 128:256] = jnp.zeros((32, 128), F32)
    wide[0:27, 128:256] = w_head[256:283, :].astype(BF16).astype(F32)
    view = lax.dot_general(
        wide[0:32, 128:256].astype(BF16), venc[...], (((0,), (0,)), ((), ())), preferred_element_type=F32
    )
    view = (view + vec_t[:, 8:9]) * half
    wide[0:16, 0:128] = jnp.zeros((16, 128), F32)
    wide[0:4, 0:rays] = jnp.broadcast_to(vec_t[0:4, 9:10], (4, rays))
    both_halves(4, target, 3)
    both_halves(7, mask, 6)
    count_here = jnp.sum(wide[7:8, 0:128])
    view_t[...] = jnp.concatenate(split_three(jnp.concatenate([view, wide[0:16, 0:rays]], axis=0)), axis=1)

    one_row = (lax.broadcasted_iota(jnp.int32, (16, hidden_a.shape[1]), 0) == 0).astype(BF16)
    hidden_a[256:272, :] = one_row
    hidden_b[256:272, :] = one_row
    for ref in (g_planes, g_in, g_low, g_top, g_sum, packed):
        ref[...] = jnp.zeros_like(ref)

    lane8 = lax.broadcasted_iota(jnp.int32, (8, LANES), 1)
    sub8 = lax.broadcasted_iota(jnp.int32, (8, LANES), 0)
    sub16 = lax.broadcasted_iota(jnp.int32, (16, LANES), 0)
    anchor = (jnp.int32(1) << (4 * (sub16 // 4))).astype(F32)
    decay_rate = anchor * anchor * (-0.5)

    for copy in copies[:-1]:
        copy.wait()

    size = BLOCK
    per = size // LANES

    def wide_of(tile):
        return jnp.concatenate([tile] * per, axis=1)

    def place_of(i):
        return pl.ds(pl.multiple_of(i * size, LANES), size)

    def encode(i):
        at = place_of(i)
        x = [xs[i * per + k] for k in range(per)]
        for k in range(per):
            x_planes[pl.ds(i * per + k, 8, stride=pitch), :] = x[k]
        x = jnp.concatenate(x, axis=1)
        sub = lax.broadcasted_iota(jnp.int32, (8, size), 0)
        turned = pltpu.roll(x, 4, 0)
        low = sub < 4
        used = sub % 4 < 3
        mean = jnp.where(used, jnp.where(low, x, turned), 0.0)
        var = jnp.where(used, jnp.where(low, turned, x), 0.0)
        m1 = jnp.round(mean * 2.0**11) * 2.0**-11
        p1 = m1 * TURN_HEAD
        p2 = m1 * TURN_REST + (mean - m1) * (TURN_HEAD + TURN_REST)
        hi = jnp.round((p1 + p2) * 2.0**20) * 2.0**-20
        lo = (p1 - hi) + p2
        pw = wide_of(anchor)
        a = jnp.concatenate([hi, hi], axis=0) * pw
        a = (a - jnp.round(a)) + jnp.concatenate([lo, lo], axis=0) * pw
        s, c = sin_cos_turns(a)
        var = jnp.concatenate([var, var], axis=0) * wide_of(decay_rate)
        for d in range(4):
            damp = jnp.exp(var * (4.0**d))
            enc[16 * d : 16 * d + 16, at] = (s * damp).astype(BF16)
            enc[64 + 16 * d : 80 + 16 * d, at] = (c * damp).astype(BF16)
            twice = s + s
            s, c = twice * c, 1.0 - twice * s
        item = x[3:4, :]
        ray = jnp.where(item >= rays, item - rays, item)
        hit = jnp.broadcast_to(ray, (rays, size)) == lax.broadcasted_iota(jnp.int32, (rays, size), 0).astype(F32)
        one_hot[:, at] = jnp.where(hit, 1.0, 0.0).astype(BF16)

    def activate(y, pre_ref, h_ref):
        pre_ref[...] = y
        h = (y * (1.0 + jnp.tanh(y))).astype(BF16)
        h_ref[...] = h
        return h

    def slope(y):
        a = jnp.tanh(y)
        return (1.0 + a) * (1.0 + y * (1.0 - a))

    def forward_all(blocks):
        def step(i, groups):
            first, second, third = (place_of(i - k) for k in range(3))
            if 3 in groups:
                hot = one_hot[:, third]
                y_head = dot_nn(wht[...], hidden_c[:, third]) + dot_nn(view_t[...], jnp.concatenate([hot, hot, hot], axis=0))
            if 2 in groups:
                y_two = dot_nn(wmt[0], hidden_a[0:256, second]) + wide_of(bias_b[0])
            if 1 in groups:
                encode(i)
            if 3 in groups:
                f = activate(y_head[0:128, :], feat_pre.at[:, third], feat.at[:, third])
            if 2 in groups:
                h = activate(y_two, pre_b.at[:, second], hidden_b.at[0:256, second])
            if 1 in groups:
                y_one = dot_nn(w0t[...], enc[:, first])
            if 3 in groups:
                y_color = dot_nn(wrt[...], f)[0:8, :] + y_head[128:136, :]
            if 2 in groups:
                y_three = dot_nn(wmt[1], h) + wide_of(bias_b[1])
            if 1 in groups:
                activate(y_one, pre_a.at[:, first], hidden_a.at[0:256, first])
            if 3 in groups:
                for k in range(per):
                    z_planes[pl.ds((i - 2) * per + k, 8, stride=pitch), :] = y_color[:, k * LANES : (k + 1) * LANES]
            if 2 in groups:
                activate(y_three, pre_c.at[:, second], hidden_c.at[:, second])

        def full_step(i, carry):
            step(i, (1, 2, 3))
            return carry

        step(jnp.int32(0), (1,))
        step(jnp.int32(1), (1, 2))
        lax.fori_loop(2, blocks, full_step, 0)
        step(blocks, (2, 3))
        step(blocks + 1, (3,))

    def backward_all(blocks):
        def step(start, size):
            per = size // LANES
            at = pl.ds(pl.multiple_of(start, LANES), size)
            dz = jnp.concatenate(
                [g_planes[pl.ds(start // LANES + k, 8, stride=pitch), :] for k in range(per)], axis=1
            )
            dzw = dz.astype(BF16).astype(F32)
            part = dzw[:, 0:LANES]
            for k in range(1, per):
                part = part + dzw[:, k * LANES : (k + 1) * LANES]
            g_sum[...] += part
            dz = jnp.concatenate([dzw, jnp.zeros_like(dzw)], axis=0).astype(BF16)
            dz_f = (dot_nn(wr[...], dz) * slope(feat_pre[:, at])).astype(BF16)
            both = jnp.concatenate([dz_f, dz], axis=0)
            up = dot_nn(whd[...], both)
            g_top[:, 0:144] += dot_nt(jnp.concatenate([hidden_c[:, at], one_hot[:, at], feat[:, at]], axis=0), both)
            dz = (up * slope(pre_c[:, at])).astype(BF16)
            up = dot_nn(wm[1], dz)
            made = dot_nt(hidden_b[:, at], dz)
            packed[352:608, :] += made[0:256, :]
            g_low[1] += made[256:272, :]
            dz = (up * slope(pre_b[:, at])).astype(BF16)
            up = dot_nn(wm[0], dz)
            made = dot_nt(hidden_a[:, at], dz)
            packed[96:352, :] += made[0:256, :]
            g_low[0] += made[256:272, :]
            dz = (up * slope(pre_a[:, at])).astype(BF16)
            g_in[...] += dot_nt(enc[:, at], dz)

        def large(i, carry):
            step(i * BACK, BACK)
            return carry

        def small(i, carry):
            step(i * BLOCK, BLOCK)
            return carry

        lax.fori_loop(0, blocks // 2, large, 0)
        lax.fori_loop(blocks // 2 * 2, blocks, small, 0)

    group = 8

    def chunk(first, passes, loss):
        xs[...] = jnp.where(lax.broadcasted_iota(jnp.int32, xs.shape, 1) == 3, -1.0, 0.0)
        x_planes[...] = jnp.full_like(x_planes, -1.0)

        def pack(p, part, g, offset):
            r0 = part * own + g * group
            item0 = (p * rays + r0).astype(F32)
            base = p * 8 * pk_pitch + r0
            moved = []
            for j in range(group):
                count = (counts, counts_two)[part][p, r0 + j]
                here = pk[pl.ds(base + j, 8, stride=pk_pitch), :]
                item = jnp.where(lane8 < count, item0 + float(j), -1.0)
                here = jnp.where(sub8 == 3, item, here)
                o = offset & (LANES - 1)
                moved.append((pltpu.roll(here, o, 1), o, offset >> 7))
                offset = offset + count
            for turned, o, t in moved:
                keep_low = lane8 >= o
                pltpu.store(xs.at[t], turned, mask=keep_low)
                pltpu.store(xs.at[t + 1], turned, mask=jnp.logical_not(keep_low))
            return offset

        def pack_pass(p, offset):
            for part in range(2):
                offset = lax.fori_loop(0, own // group, lambda g, o: pack(p, part, g, o), offset)
            return offset

        total = lax.fori_loop(first, first + passes, pack_pass, jnp.int32(0))
        blocks = jnp.maximum((total + BLOCK - 1) // BLOCK, 2)
        forward_all(blocks)

        def plane(ref, k):
            return ref[k * pitch : k * pitch + tiles, :]

        lane = lax.broadcasted_iota(jnp.int32, (tiles, LANES), 1)
        row = lax.broadcasted_iota(jnp.int32, (tiles, LANES), 0)
        item = plane(x_planes, 3)
        valid = item >= 0.0
        steps = (1, 2, 4, 8, 16, 32, 64)
        back = [jnp.logical_and(lane >= k, pltpu.roll(item, k, 1) == item) for k in steps]
        ahead = [jnp.logical_and(lane < LANES - k, pltpu.roll(item, LANES - k, 1) == item) for k in steps]
        end_before = jnp.broadcast_to(pltpu.roll(item[:, LANES - 1 : LANES], 1, 0), (tiles, LANES))
        start_after = jnp.broadcast_to(pltpu.roll(item[:, 0:1], tiles - 1, 0), (tiles, LANES))
        from_before = jnp.logical_and(row > 0, end_before == item)
        from_after = jnp.logical_and(row < tiles - 1, start_after == item)

        def scan(values):
            for k, near in zip(steps, back):
                values = values + jnp.where(near, pltpu.roll(values, k, 1), 0.0)
            carry = jnp.broadcast_to(pltpu.roll(values[:, LANES - 1 : LANES], 1, 0), (tiles, LANES))
            return values + jnp.where(from_before, carry, 0.0)

        def scan_back(values):
            for k, near in zip(steps, ahead):
                values = values + jnp.where(near, pltpu.roll(values, LANES - k, 1), 0.0)
            carry = jnp.broadcast_to(pltpu.roll(values[:, 0:1], tiles - 1, 0), (tiles, LANES))
            return values + jnp.where(from_after, carry, 0.0)

        def z_plane(k):
            return jnp.where(valid, plane(z_planes, k), 0.0)

        share = jnp.where(item >= rays, 1.0, COARSE_SHARE) * z_plane(7)
        space = jnp.where(valid, plane(x_planes, 7), 0.0)
        zd = z_plane(3) - 1.0
        density = jnp.maximum(zd, 0.0) + jnp.log1p(jnp.exp(-jnp.abs(zd)))
        tau = density * space
        inclusive = scan(tau)
        exclusive = inclusive - tau
        beyond = jnp.exp(-inclusive)
        weights = jnp.exp(-exclusive) - beyond
        weighted = jnp.zeros_like(tau)
        sums = jnp.zeros_like(tau)
        for c in range(3):
            sig = jax.nn.sigmoid(z_plane(c))
            rgb = 1.002 * sig - 0.001
            part = weights * rgb
            color = scan(part) + (scan_back(part) - part)
            error = color - z_plane(4 + c)
            sums = sums + error * error
            color_grad = (2.0 / 3.0) * share * error
            weighted = weighted + color_grad * rgb
            d_color = weights * color_grad * 1.002 * sig * (1.0 - sig)
            g_planes[c * pitch : c * pitch + tiles, :] = jnp.where(valid, d_color, 0.0)
        product = jnp.where(valid, weighted * weights, 0.0)
        after = scan_back(product) - product
        d_density = (beyond * weighted - after) * space * jax.nn.sigmoid(zd)
        g_planes[3 * pitch : 3 * pitch + tiles, :] = jnp.where(valid, d_density, 0.0)
        previous = jnp.where(lane >= 1, pltpu.roll(item, 1, 1), jnp.where(row > 0, end_before, -2.0))
        begins = jnp.logical_and(previous != item, valid)
        loss = loss + jnp.sum(jnp.where(begins, sums * share, 0.0)) * (1.0 / 3.0)

        backward_all(blocks)
        return loss

    wide[0:2, 0:own] = counts_vec[:, 0:own].astype(F32)
    wide[0:2, own:rays] = small_two[7:9, own:rays]
    everything = jnp.sum(wide[0:2, 0:rays])
    at_once = everything <= 1.0 * capacity
    chunks = jnp.where(at_once, 1, 2)
    passes = jnp.where(at_once, 2, 1)
    loss = lax.fori_loop(0, chunks, lambda i, loss: chunk(i, passes, loss), jnp.zeros((), F32))

    for a in range(4):
        for d in range(4):
            for k in range(2):
                at, to = 64 * k + 16 * d + 4 * a, 48 * k + 12 * a + 3 * d
                packed[to : to + 3, :] = g_in[at : at + 3, :]
    rays_sum = g_top[256 : 256 + rays, 0:128]
    packed[736:737, :] = g_in[67:68, :]
    packed[737:738, :] = g_low[0, 0:1, :]
    packed[738:739, :] = g_low[1, 0:1, :]
    for k in range(2):
        packed[608:736, 128 * k : 128 * k + 128] = g_top[128 * k : 128 * k + 128, 0:128]
        packed[739:740, 128 * k : 128 * k + 128] = g_top[128 * k : 128 * k + 128, 128:256].T[3:4, :]
    packed[740:741, 0:128] = jnp.sum(rays_sum, axis=0, keepdims=True)
    small = jnp.sum(g_sum[...], axis=1, keepdims=True)
    lane1 = lax.broadcasted_iota(jnp.int32, (1, LANES), 1)
    line = jnp.zeros((1, LANES), F32)
    for k in range(4):
        line = line + jnp.where(lane1 == k, jnp.broadcast_to(small[k : k + 1, :], (1, LANES)), 0.0)
    line = line + jnp.where(lane1 == 4, loss, 0.0)
    line = line + jnp.where(lane1 == 5, count_here, 0.0)
    packed[740:741, 128:256] = line
    packed[741:744, 0:128] = g_top[256 + rays : 384 + rays, 128:256].T[0:3, :]
    view_grad = jnp.zeros((32, 128), F32)
    for piece in split_three(rays_sum):
        view_grad = view_grad + dot_nn(venc[...], piece)
    packed[744:760, 0:128] = view_grad[0:16, :]
    packed[744:760, 128:256] = view_grad[16:32, :]
    for q in range(4):
        for ref, which in ((keep, place[0]), (send, place[1])):
            source = pl.multiple_of((which ^ q) * PART, 8)
            ref[q * PART : (q + 1) * PART, :] = packed[pl.ds(source, PART), :]


def field_gradients(find_place, local, other, params):
    means, variances, spacing, dirs, target, counts, mask = local
    means_two, variances_two, spacing_two, other_counts, other_rows = (
        pltpu.with_memory_space_constraint(array, pltpu.VMEM) for array in other
    )
    w_in, w_mid, w_head, w_rgb, vec = params
    rays = dirs.shape[1]
    room = 17 * rays * LANES // 16 + LANES
    tiles = -(-(room - LANES) // (8 * LANES)) * 8
    pitch = tiles + 8 * (1 - tiles // 8 % 2)
    vmem = pl.BlockSpec(memory_space=pltpu.VMEM)
    smem = pl.BlockSpec(memory_space=pltpu.SMEM)
    hbm = pl.BlockSpec(memory_space=pl.ANY)
    scratch = [
        pltpu.VMEM((2 * 8 * (rays + 8), LANES), F32),
        pltpu.VMEM((room // LANES + 1, 8, LANES), F32),
        pltpu.VMEM((8 * pitch, LANES), F32),
        pltpu.VMEM((8 * pitch, LANES), F32),
        pltpu.VMEM((8 * pitch, LANES), F32),
        pltpu.VMEM((128, room), BF16),
        pltpu.VMEM((272, room), BF16),
        pltpu.VMEM((272, room), BF16),
        pltpu.VMEM((256, room), BF16),
        pltpu.VMEM((256, room), F32),
        pltpu.VMEM((256, room), F32),
        pltpu.VMEM((256, room), F32),
        pltpu.VMEM((128, room), BF16),
        pltpu.VMEM((128, room), F32),
        pltpu.VMEM((rays, room), BF16),
        pltpu.VMEM((16, LANES), F32),
        pltpu.SMEM((2, rays), jnp.int32),
        pltpu.VMEM((16, LANES), F32),
        pltpu.VMEM((128, 256), F32),
        pltpu.VMEM((256, 128), BF16),
        pltpu.VMEM((2, 256, 256), BF16),
        pltpu.VMEM((2, 256, 256), BF16),
        pltpu.VMEM((144, 256), BF16),
        pltpu.VMEM((256, 144), BF16),
        pltpu.VMEM((16, 128), BF16),
        pltpu.VMEM((128, 16), BF16),
        pltpu.VMEM((2, 256, 128), F32),
        pltpu.VMEM((144, 3 * rays), BF16),
        pltpu.VMEM((32, rays), BF16),
        pltpu.VMEM((128, 256), F32),
        pltpu.VMEM((2, 16, 256), F32),
        pltpu.VMEM((384 + rays, 256), F32),
        pltpu.VMEM((8, LANES), F32),
        pltpu.VMEM((8 * PART, 256), F32),
        pltpu.SemaphoreType.DMA((30,)),
    ]
    return pl.pallas_call(
        functools.partial(field_kernel, find_place),
        out_shape=[pltpu.VMEM((4 * PART, 256), F32)] * 2,
        in_specs=[smem] + [vmem] * 5 + [hbm] * 3 + [vmem] * 9,
        out_specs=[vmem, vmem],
        scratch_shapes=scratch,
        compiler_params=pltpu.CompilerParams(vmem_limit_bytes=62 << 20),
    )(
        counts,
        other_counts,
        means_two,
        variances_two,
        spacing_two,
        other_rows,
        means,
        variances,
        spacing,
        dirs,
        target,
        mask.reshape(1, rays),
        counts,
        w_in,
        w_mid,
        w_head,
        w_rgb.T,
        vec,
    )


def ray_rows(local):
    dirs, target, counts, mask = local[3:]
    rows = jnp.concatenate([dirs, target, mask[None].astype(F32), counts.astype(F32)], axis=0)
    return jnp.pad(rows, ((0, 16 - rows.shape[0]), (0, LANES - rows.shape[1])))


def adamw(weight, grad, first, second):
    first = BETA_ONE * first + (1.0 - BETA_ONE) * grad
    second = BETA_TWO * second + (1.0 - BETA_TWO) * grad * grad
    first_hat = first * (1.0 / (1.0 - BETA_ONE**STEP))
    second_hat = second * (1.0 / (1.0 - BETA_TWO**STEP))
    fresh = weight - LEARN_RATE * (first_hat / (jnp.sqrt(second_hat) + EPSILON) + DECAY * weight)
    return first, second, fresh


def update_kernel(find_place, *refs):
    place = find_place()
    pieces, refs = refs[0:8], refs[8:]
    weights, firsts, seconds = refs[0:5], refs[5:10], refs[10:15]
    loss, count = refs[15], refs[16]
    outs = refs[17:32]
    packed = refs[32]
    for k, ref in enumerate(pieces):
        block = place[k // 4] ^ (k % 4)
        packed[pl.ds(pl.multiple_of(block * PART, 8), PART), :] = ref[...]
    line = packed[740:741, 128:256]
    loss[0] = line[0, 4]
    count[0] = line[0, 5]
    scale = 1.0 / line[0:1, 5:6]

    def apply(group, at, grad):
        step = scale.reshape(1) if grad.ndim == 1 else scale
        made = adamw(weights[group][at], grad * step, firsts[group][at], seconds[group][at])
        for k in range(3):
            outs[3 * group + k][at] = made[k]

    everything = slice(None)
    apply(0, (everything, everything), packed[0:96, :])
    for k in range(2):
        apply(1, (k, everything, everything), packed[96 + 256 * k : 352 + 256 * k, :])
    for k in range(2):
        apply(2, (slice(128 * k, 128 * k + 128), everything), packed[608:736, 128 * k : 128 * k + 128])
    apply(2, (slice(256, 272), everything), packed[744:760, 0:128])
    apply(2, (slice(272, 283), everything), packed[744:755, 128:256])
    apply(3, (everything, everything), packed[741:744, 0:128])
    for k in range(9):
        line = packed[736 + k // 2 : 737 + k // 2, 128 * (k % 2) : 128 * (k % 2) + 128]
        apply(4, (pl.ds(128 * k, 128),), line.reshape(128))
    apply(4, (pl.ds(1152, 4),), packed[740:741, 128:132].reshape(4))


def update(find_place, pieces, params, firsts, seconds):
    vmem = pl.BlockSpec(memory_space=pltpu.VMEM)
    smem = pl.BlockSpec(memory_space=pltpu.SMEM)
    shapes = [jax.ShapeDtypeStruct((1,), F32)] * 2
    for array in params:
        shapes += [jax.ShapeDtypeStruct(array.shape, F32)] * 3
    return pl.pallas_call(
        functools.partial(update_kernel, find_place),
        out_shape=shapes,
        in_specs=[vmem] * 23,
        out_specs=[smem, smem] + [vmem] * 15,
        scratch_shapes=[pltpu.VMEM((8 * PART, 256), F32)],
        compiler_params=pltpu.CompilerParams(vmem_limit_bytes=32 << 20),
    )(*pieces, *params, *firsts, *seconds)


def xor_pairs(total, mask_of):
    return [(i, i ^ mask_of(i)) for i in range(total)]


def place_small():
    ray = lax.axis_index("rays")
    rep = lax.axis_index("rep")
    y, x, core = ray % 2, rep // 2, rep % 2
    xy, yx = 2 * x + y, 2 * y + x
    return (
        jnp.where(core == 0, xy, 4 + yx),
        jnp.where(core == 0, 4 + yx, xy),
    )


def reduce_small(keep, send, axes):
    core = xor_pairs(32, lambda i: 1)
    one = xor_pairs(32, lambda i: 4 if i & 1 else 2)
    two = xor_pairs(32, lambda i: 2 if i & 1 else 4)
    both = xor_pairs(32, lambda i: 6)
    z_one = xor_pairs(32, lambda i: 16 if i & 1 else 8)
    z_two = xor_pairs(32, lambda i: 8 if i & 1 else 16)

    def swap(value, pairs):
        return lax.ppermute(value, axes, pairs)

    square = (two, one, both)
    now = keep + swap(send, core)
    got = [swap(now[PART * (k + 1) : PART * (k + 2)], pairs) for k, pairs in enumerate(square)]
    own = (now[:PART] + got[0]) + (got[1] + got[2])
    own = own + swap(own, z_one)
    own = own + swap(own, z_two)
    parts = [own] + [swap(own, pairs) for pairs in square]
    return parts + [swap(part, core) for part in parts]


def on_device(
    small_mesh,
    sample_means,
    sample_vars,
    sample_spacing,
    view_dirs,
    target_rgb,
    sample_counts,
    ray_mask,
    w_in,
    w_mid,
    w_head,
    w_rgb,
    vectors,
    first_in,
    first_mid,
    first_head,
    first_rgb,
    first_vec,
    second_in,
    second_mid,
    second_head,
    second_rgb,
    second_vec,
):
    axes = ("rays", "rep")
    find_place = place_small if small_mesh else lambda: (0, 4)
    params = (w_in, w_mid, w_head, w_rgb, vectors)
    local = (sample_means, sample_vars, sample_spacing, view_dirs, target_rgb, sample_counts, ray_mask)
    other = (sample_means, sample_vars, sample_spacing, sample_counts, ray_rows(local))
    if small_mesh:
        core_pairs = xor_pairs(32, lambda i: 1)
        other = tuple(lax.ppermute(array, axes, core_pairs) for array in other)
    keep, send = field_gradients(find_place, local, other, params)
    if small_mesh:
        pieces = reduce_small(keep, send, axes)
    else:
        whole = lax.psum(jnp.concatenate([keep, send], axis=0), axes)
        pieces = [whole[PART * k : PART * (k + 1)] for k in range(8)]
    outs = update(
        find_place,
        pieces,
        (w_in, w_mid, w_head, w_rgb.T, vectors),
        (first_in, first_mid, first_head, first_rgb.T, first_vec),
        (second_in, second_mid, second_head, second_rgb.T, second_vec),
    )
    rgb = [out.T for out in outs[11:14]]
    return (outs[0].reshape(()), outs[1].reshape(()), *outs[2:11], *rgb, *outs[14:17])


def solution(mesh):
    rays = ("rays", "rep")
    in_specs = (
        P(None, None, rays, None),
        P(None, None, rays, None),
        P(None, rays, None),
        P(None, rays),
        P(None, rays),
        P(None, rays),
        P(rays),
    ) + (P(),) * 15
    small_mesh = mesh.shape["rays"] == 8 and mesh.shape["rep"] == 4

    def step(*args):
        return on_device(small_mesh, *args)

    return jax.shard_map(step, mesh=mesh, in_specs=in_specs, out_specs=(P(),) * 17, check_vma=False)
```

```python
import functools
import math

import jax
import jax.numpy as jnp
from jax import lax
from jax.experimental import pallas as pl
from jax.experimental.pallas import tpu as pltpu
from jax.sharding import PartitionSpec as P

L_POS = 16
L_DIR = 4
STEP = 7
LEARN_RATE = 0.05
BETA_ONE = 0.9
BETA_TWO = 0.999
EPSILON = 1e-08
DECAY = 0.01
COARSE_SHARE = 0.1

BLOCK = 512
BACK = 1024
LANES = 128
PART = 96

TURN_HEAD = 0.1591796875
TURN_REST = 1.0 / (2.0 * math.pi) - TURN_HEAD
SIN_POLY = (3.1415926343, -5.1677091056, 2.5500551036, -0.5981303017, 0.0773037189)
COS_POLY = (0.9999999314, -4.9347894708, 4.0583337486, -1.3313191807, 0.2184639082)

F32 = jnp.float32
BF16 = jnp.bfloat16


def split_three(values):
    head = values.astype(BF16)
    rest = values - head.astype(F32)
    middle = rest.astype(BF16)
    tail = (rest - middle.astype(F32)).astype(BF16)
    return head, middle, tail


def dot_nt(left, right):
    return lax.dot_general(left, right, (((1,), (1,)), ((), ())), preferred_element_type=F32)


def dot_nn(left, right):
    return jnp.dot(left, right, preferred_element_type=F32)


def poly(coefficients, square):
    total = jnp.full_like(square, coefficients[-1])
    for c in coefficients[-2::-1]:
        total = total * square + c
    return total


def sin_cos_turns(r):
    square = r * r
    s = r * poly(SIN_POLY, square)
    c = poly(COS_POLY, square)
    return (s + s) * c, 1.0 - (s + s) * s


def field_kernel(
    find_place,
    counts,
    counts_other,
    mask_two,
    means_two,
    variances_two,
    spacing_two,
    other,
    means,
    variances,
    spacing,
    dirs,
    target,
    mask,
    counts_vec,
    w_in,
    w_mid,
    w_head,
    w_rgb_t,
    vec,
    keep,
    send,
    pk,
    xs,
    x_planes,
    z_planes,
    g_planes,
    enc,
    hidden_a,
    hidden_b,
    hidden_c,
    pre_a,
    pre_b,
    pre_c,
    feat,
    feat_pre,
    one_hot,
    small_two,
    counts_two,
    rows,
    wide,
    w0t,
    wmt,
    wm,
    wht,
    whd,
    wrt,
    wr,
    bias_b,
    view_t,
    venc,
    g_in,
    g_low,
    g_top,
    g_sum,
    packed,
    sem,
):
    place = find_place()
    rays = dirs.shape[1]
    own = rays // 2
    pitch = z_planes.shape[0] // 8
    pk_pitch = pk.shape[0] // 16
    capacity = hidden_c.shape[1] - LANES
    tiles = -(-capacity // (8 * LANES)) * 8
    copies = []
    for p in range(2):
        for k, sources in enumerate(((means, means_two), (variances, variances_two))):
            for c in range(3):
                for half, source in enumerate(sources):
                    to = (p * 8 + 4 * k + c) * pk_pitch + half * own
                    copies.append((source.at[p, c, pl.ds(half * own, own)], pk.at[pl.ds(to, own)]))
        for half, source in enumerate((spacing, spacing_two)):
            to = (p * 8 + 7) * pk_pitch + half * own
            copies.append((source.at[p, pl.ds(half * own, own)], pk.at[pl.ds(to, own)]))
    copies.append((counts_other, counts_two))
    copies.append((other, small_two))
    copies = [pltpu.make_async_copy(a, b, sem.at[k]) for k, (a, b) in enumerate(copies)]
    for copy in copies:
        copy.start()

    half = 0.5
    rows[...] = jnp.zeros_like(rows)
    for k in range(9):
        rows[k : k + 1, :] = vec[pl.ds(k * LANES, LANES)].reshape(1, LANES)
    rows[9:10, 0:4] = vec[pl.ds(9 * LANES, 4)].reshape(1, 4)
    vec_t = rows[0:16, :].T
    wide[0:128, :] = jnp.zeros((128, 256), F32)
    rounded = w_in[...].astype(BF16).astype(F32) * half
    for a in range(4):
        for d in range(4):
            for k in range(2):
                to, at = 64 * k + 16 * d + 4 * a, 48 * k + 12 * a + 3 * d
                wide[to : to + 3, :] = rounded[at : at + 3, :]
    b0 = jnp.concatenate([rows[0:1, :], rows[1:2, :]], axis=1) * half
    for a, piece in enumerate(split_three(b0)):
        wide[67 + 4 * a : 68 + 4 * a, :] = piece.astype(F32)
    w0t[...] = wide[0:128, :].T.astype(BF16)
    for k in range(2):
        rounded = w_mid[k].astype(BF16).astype(F32) * half
        wm[k] = rounded.astype(BF16)
        wmt[k] = rounded.T.astype(BF16)
        bias_b[k, 0:128, :] = jnp.broadcast_to(vec_t[:, 2 + 2 * k : 3 + 2 * k], (128, 128)) * half
        bias_b[k, 128:256, :] = jnp.broadcast_to(vec_t[:, 3 + 2 * k : 4 + 2 * k], (128, 128)) * half
    top = (w_head[0:256, :].astype(BF16).astype(F32) * half).T
    u_row = jnp.concatenate([rows[6:7, :], rows[7:8, :]], axis=1).astype(BF16).astype(F32)
    row16 = lax.broadcasted_iota(jnp.int32, (16, 256), 0)
    last = jnp.where(row16 == 3, u_row, 0.0)
    wht[0:128, :] = top.astype(BF16)
    wht[128:144, :] = last.astype(BF16)
    whd[...] = jnp.concatenate([top, last * half], axis=0).T.astype(BF16)
    wide[0:16, 0:128] = jnp.zeros((16, 128), F32)
    wide[0:3, 0:128] = w_rgb_t[...].astype(BF16).astype(F32)
    wrt[...] = wide[0:16, 0:128].astype(BF16)
    wr[...] = (wide[0:16, 0:128].T * half).astype(BF16)

    copies[-1].wait()

    def both_halves_of(at, one, two):
        n = one.shape[0]
        wide[at : at + n, 0:own] = one[:, 0:own].astype(F32)
        wide[at : at + n, own:rays] = two[:, own:rays].astype(F32)

    def both_halves(at, one, row):
        n = one.shape[0]
        wide[at : at + n, 0:own] = one[:, 0:own].astype(F32)
        wide[at : at + n, own:rays] = small_two[row : row + n, own:rays]

    wide[0:32, 0:128] = jnp.zeros((32, 128), F32)
    both_halves(0, dirs, 0)
    d = wide[0:3, 0:rays]
    for l in range(L_DIR):
        wide[3 + 3 * l : 6 + 3 * l, 0:rays] = jnp.sin(d * (2.0**l))
        wide[15 + 3 * l : 18 + 3 * l, 0:rays] = jnp.cos(d * (2.0**l))
    venc[...] = wide[0:32, 0:rays].astype(BF16)
    wide[0:32, 128:256] = jnp.zeros((32, 128), F32)
    wide[0:27, 128:256] = w_head[256:283, :].astype(BF16).astype(F32)
    view = lax.dot_general(
        wide[0:32, 128:256].astype(BF16), venc[...], (((0,), (0,)), ((), ())), preferred_element_type=F32
    )
    view = (view + vec_t[:, 8:9]) * half
    wide[0:16, 0:128] = jnp.zeros((16, 128), F32)
    wide[0:4, 0:rays] = jnp.broadcast_to(vec_t[0:4, 9:10], (4, rays))
    both_halves(4, target, 3)
    both_halves_of(7, mask, mask_two)
    count_here = jnp.sum(wide[7:8, 0:128])
    view_t[...] = jnp.concatenate(split_three(jnp.concatenate([view, wide[0:16, 0:rays]], axis=0)), axis=1)

    one_row = (lax.broadcasted_iota(jnp.int32, (16, hidden_a.shape[1]), 0) == 0).astype(BF16)
    hidden_a[256:272, :] = one_row
    hidden_b[256:272, :] = one_row
    for ref in (g_planes, g_in, g_low, g_top, g_sum, packed):
        ref[...] = jnp.zeros_like(ref)

    lane8 = lax.broadcasted_iota(jnp.int32, (8, LANES), 1)
    sub8 = lax.broadcasted_iota(jnp.int32, (8, LANES), 0)
    sub16 = lax.broadcasted_iota(jnp.int32, (16, LANES), 0)
    anchor = (jnp.int32(1) << (4 * (sub16 // 4))).astype(F32)
    decay_rate = anchor * anchor * (-0.5)

    for copy in copies[:-1]:
        copy.wait()

    size = BLOCK
    per = size // LANES

    def wide_of(tile):
        return jnp.concatenate([tile] * per, axis=1)

    def place_of(i):
        return pl.ds(pl.multiple_of(i * size, LANES), size)

    def encode(i):
        at = place_of(i)
        x = [xs[i * per + k] for k in range(per)]
        for k in range(per):
            x_planes[pl.ds(i * per + k, 8, stride=pitch), :] = x[k]
        x = jnp.concatenate(x, axis=1)
        sub = lax.broadcasted_iota(jnp.int32, (8, size), 0)
        turned = pltpu.roll(x, 4, 0)
        low = sub < 4
        used = sub % 4 < 3
        mean = jnp.where(used, jnp.where(low, x, turned), 0.0)
        var = jnp.where(used, jnp.where(low, turned, x), 0.0)
        m1 = jnp.round(mean * 2.0**11) * 2.0**-11
        p1 = m1 * TURN_HEAD
        p2 = m1 * TURN_REST + (mean - m1) * (TURN_HEAD + TURN_REST)
        hi = jnp.round((p1 + p2) * 2.0**20) * 2.0**-20
        lo = (p1 - hi) + p2
        pw = wide_of(anchor)
        a = jnp.concatenate([hi, hi], axis=0) * pw
        a = (a - jnp.round(a)) + jnp.concatenate([lo, lo], axis=0) * pw
        s, c = sin_cos_turns(a)
        var = jnp.concatenate([var, var], axis=0) * wide_of(decay_rate)
        for d in range(4):
            damp = jnp.exp(var * (4.0**d))
            enc[16 * d : 16 * d + 16, at] = (s * damp).astype(BF16)
            enc[64 + 16 * d : 80 + 16 * d, at] = (c * damp).astype(BF16)
            twice = s + s
            s, c = twice * c, 1.0 - twice * s
        item = x[3:4, :]
        ray = jnp.where(item >= rays, item - rays, item)
        hit = jnp.broadcast_to(ray, (rays, size)) == lax.broadcasted_iota(jnp.int32, (rays, size), 0).astype(F32)
        one_hot[:, at] = jnp.where(hit, 1.0, 0.0).astype(BF16)

    def activate(y, pre_ref, h_ref):
        pre_ref[...] = y
        h = (y * (1.0 + jnp.tanh(y))).astype(BF16)
        h_ref[...] = h
        return h

    def slope(y):
        a = jnp.tanh(y)
        return (1.0 + a) * (1.0 + y * (1.0 - a))

    def forward_all(blocks):
        def step(i, groups):
            first, second, third = (place_of(i - k) for k in range(3))
            if 3 in groups:
                hot = one_hot[:, third]
                y_head = dot_nn(wht[...], hidden_c[:, third]) + dot_nn(view_t[...], jnp.concatenate([hot, hot, hot], axis=0))
            if 2 in groups:
                y_two = dot_nn(wmt[0], hidden_a[0:256, second]) + wide_of(bias_b[0])
            if 1 in groups:
                encode(i)
            if 3 in groups:
                f = activate(y_head[0:128, :], feat_pre.at[:, third], feat.at[:, third])
            if 2 in groups:
                h = activate(y_two, pre_b.at[:, second], hidden_b.at[0:256, second])
            if 1 in groups:
                y_one = dot_nn(w0t[...], enc[:, first])
            if 3 in groups:
                y_color = dot_nn(wrt[...], f)[0:8, :] + y_head[128:136, :]
            if 2 in groups:
                y_three = dot_nn(wmt[1], h) + wide_of(bias_b[1])
            if 1 in groups:
                activate(y_one, pre_a.at[:, first], hidden_a.at[0:256, first])
            if 3 in groups:
                for k in range(per):
                    z_planes[pl.ds((i - 2) * per + k, 8, stride=pitch), :] = y_color[:, k * LANES : (k + 1) * LANES]
            if 2 in groups:
                activate(y_three, pre_c.at[:, second], hidden_c.at[:, second])

        def full_step(i, carry):
            step(i, (1, 2, 3))
            return carry

        step(jnp.int32(0), (1,))
        step(jnp.int32(1), (1, 2))
        lax.fori_loop(2, blocks, full_step, 0)
        step(blocks, (2, 3))
        step(blocks + 1, (3,))

    def backward_all(blocks):
        def step(start, size):
            per = size // LANES
            at = pl.ds(pl.multiple_of(start, LANES), size)
            dz = jnp.concatenate(
                [g_planes[pl.ds(start // LANES + k, 8, stride=pitch), :] for k in range(per)], axis=1
            )
            dzw = dz.astype(BF16).astype(F32)
            part = dzw[:, 0:LANES]
            for k in range(1, per):
                part = part + dzw[:, k * LANES : (k + 1) * LANES]
            g_sum[...] += part
            dz = jnp.concatenate([dzw, jnp.zeros_like(dzw)], axis=0).astype(BF16)
            dz_f = (dot_nn(wr[...], dz) * slope(feat_pre[:, at])).astype(BF16)
            both = jnp.concatenate([dz_f, dz], axis=0)
            up = dot_nn(whd[...], both)
            g_top[:, 0:144] += dot_nt(jnp.concatenate([hidden_c[:, at], one_hot[:, at], feat[:, at]], axis=0), both)
            dz = (up * slope(pre_c[:, at])).astype(BF16)
            up = dot_nn(wm[1], dz)
            made = dot_nt(hidden_b[:, at], dz)
            packed[352:608, :] += made[0:256, :]
            g_low[1] += made[256:272, :]
            dz = (up * slope(pre_b[:, at])).astype(BF16)
            up = dot_nn(wm[0], dz)
            made = dot_nt(hidden_a[:, at], dz)
            packed[96:352, :] += made[0:256, :]
            g_low[0] += made[256:272, :]
            dz = (up * slope(pre_a[:, at])).astype(BF16)
            g_in[...] += dot_nt(enc[:, at], dz)

        def large(i, carry):
            step(i * BACK, BACK)
            return carry

        def small(i, carry):
            step(i * BLOCK, BLOCK)
            return carry

        lax.fori_loop(0, blocks // 2, large, 0)
        lax.fori_loop(blocks // 2 * 2, blocks, small, 0)

    group = 8

    def chunk(first, passes, loss):
        xs[...] = jnp.where(lax.broadcasted_iota(jnp.int32, xs.shape, 1) == 3, -1.0, 0.0)
        x_planes[...] = jnp.full_like(x_planes, -1.0)

        def pack(p, part, g, offset):
            r0 = part * own + g * group
            item0 = (p * rays + r0).astype(F32)
            base = p * 8 * pk_pitch + r0
            moved = []
            for j in range(group):
                count = (counts, counts_two)[part][p, r0 + j]
                here = pk[pl.ds(base + j, 8, stride=pk_pitch), :]
                item = jnp.where(lane8 < count, item0 + float(j), -1.0)
                here = jnp.where(sub8 == 3, item, here)
                o = offset & (LANES - 1)
                moved.append((pltpu.roll(here, o, 1), o, offset >> 7))
                offset = offset + count
            for turned, o, t in moved:
                keep_low = lane8 >= o
                pltpu.store(xs.at[t], turned, mask=keep_low)
                pltpu.store(xs.at[t + 1], turned, mask=jnp.logical_not(keep_low))
            return offset

        def pack_pass(p, offset):
            for part in range(2):
                offset = lax.fori_loop(0, own // group, lambda g, o: pack(p, part, g, o), offset)
            return offset

        total = lax.fori_loop(first, first + passes, pack_pass, jnp.int32(0))
        blocks = jnp.maximum((total + BLOCK - 1) // BLOCK, 2)
        forward_all(blocks)

        def plane(ref, k):
            return ref[k * pitch : k * pitch + tiles, :]

        lane = lax.broadcasted_iota(jnp.int32, (tiles, LANES), 1)
        row = lax.broadcasted_iota(jnp.int32, (tiles, LANES), 0)
        item = plane(x_planes, 3)
        valid = item >= 0.0
        steps = (1, 2, 4, 8, 16, 32, 64)
        back = [jnp.logical_and(lane >= k, pltpu.roll(item, k, 1) == item) for k in steps]
        ahead = [jnp.logical_and(lane < LANES - k, pltpu.roll(item, LANES - k, 1) == item) for k in steps]
        end_before = jnp.broadcast_to(pltpu.roll(item[:, LANES - 1 : LANES], 1, 0), (tiles, LANES))
        start_after = jnp.broadcast_to(pltpu.roll(item[:, 0:1], tiles - 1, 0), (tiles, LANES))
        from_before = jnp.logical_and(row > 0, end_before == item)
        from_after = jnp.logical_and(row < tiles - 1, start_after == item)

        def scan(values):
            for k, near in zip(steps, back):
                values = values + jnp.where(near, pltpu.roll(values, k, 1), 0.0)
            carry = jnp.broadcast_to(pltpu.roll(values[:, LANES - 1 : LANES], 1, 0), (tiles, LANES))
            return values + jnp.where(from_before, carry, 0.0)

        def scan_back(values):
            for k, near in zip(steps, ahead):
                values = values + jnp.where(near, pltpu.roll(values, LANES - k, 1), 0.0)
            carry = jnp.broadcast_to(pltpu.roll(values[:, 0:1], tiles - 1, 0), (tiles, LANES))
            return values + jnp.where(from_after, carry, 0.0)

        def z_plane(k):
            return jnp.where(valid, plane(z_planes, k), 0.0)

        share = jnp.where(item >= rays, 1.0, COARSE_SHARE) * z_plane(7)
        space = jnp.where(valid, plane(x_planes, 7), 0.0)
        zd = z_plane(3) - 1.0
        density = jnp.maximum(zd, 0.0) + jnp.log1p(jnp.exp(-jnp.abs(zd)))
        tau = density * space
        inclusive = scan(tau)
        exclusive = inclusive - tau
        beyond = jnp.exp(-inclusive)
        weights = jnp.exp(-exclusive) - beyond
        weighted = jnp.zeros_like(tau)
        sums = jnp.zeros_like(tau)
        for c in range(3):
            sig = jax.nn.sigmoid(z_plane(c))
            rgb = 1.002 * sig - 0.001
            part = weights * rgb
            color = scan(part) + (scan_back(part) - part)
            error = color - z_plane(4 + c)
            sums = sums + error * error
            color_grad = (2.0 / 3.0) * share * error
            weighted = weighted + color_grad * rgb
            d_color = weights * color_grad * 1.002 * sig * (1.0 - sig)
            g_planes[c * pitch : c * pitch + tiles, :] = jnp.where(valid, d_color, 0.0)
        product = jnp.where(valid, weighted * weights, 0.0)
        after = scan_back(product) - product
        d_density = (beyond * weighted - after) * space * jax.nn.sigmoid(zd)
        g_planes[3 * pitch : 3 * pitch + tiles, :] = jnp.where(valid, d_density, 0.0)
        previous = jnp.where(lane >= 1, pltpu.roll(item, 1, 1), jnp.where(row > 0, end_before, -2.0))
        begins = jnp.logical_and(previous != item, valid)
        loss = loss + jnp.sum(jnp.where(begins, sums * share, 0.0)) * (1.0 / 3.0)

        backward_all(blocks)
        return loss

    both_halves_of(0, counts_vec, counts_other)
    everything = jnp.sum(wide[0:2, 0:rays])
    at_once = everything <= 1.0 * capacity
    chunks = jnp.where(at_once, 1, 2)
    passes = jnp.where(at_once, 2, 1)
    loss = lax.fori_loop(0, chunks, lambda i, loss: chunk(i, passes, loss), jnp.zeros((), F32))

    for a in range(4):
        for d in range(4):
            for k in range(2):
                at, to = 64 * k + 16 * d + 4 * a, 48 * k + 12 * a + 3 * d
                packed[to : to + 3, :] = g_in[at : at + 3, :]
    rays_sum = g_top[256 : 256 + rays, 0:128]
    packed[736:737, :] = g_in[67:68, :]
    packed[737:738, :] = g_low[0, 0:1, :]
    packed[738:739, :] = g_low[1, 0:1, :]
    for k in range(2):
        packed[608:736, 128 * k : 128 * k + 128] = g_top[128 * k : 128 * k + 128, 0:128]
        packed[739:740, 128 * k : 128 * k + 128] = g_top[128 * k : 128 * k + 128, 128:256].T[3:4, :]
    packed[740:741, 0:128] = jnp.sum(rays_sum, axis=0, keepdims=True)
    small = jnp.sum(g_sum[...], axis=1, keepdims=True)
    lane1 = lax.broadcasted_iota(jnp.int32, (1, LANES), 1)
    line = jnp.zeros((1, LANES), F32)
    for k in range(4):
        line = line + jnp.where(lane1 == k, jnp.broadcast_to(small[k : k + 1, :], (1, LANES)), 0.0)
    line = line + jnp.where(lane1 == 4, loss, 0.0)
    line = line + jnp.where(lane1 == 5, count_here, 0.0)
    packed[740:741, 128:256] = line
    packed[741:744, 0:128] = g_top[256 + rays : 384 + rays, 128:256].T[0:3, :]
    view_grad = jnp.zeros((32, 128), F32)
    for piece in split_three(rays_sum):
        view_grad = view_grad + dot_nn(venc[...], piece)
    packed[744:760, 0:128] = view_grad[0:16, :]
    packed[744:760, 128:256] = view_grad[16:32, :]
    for q in range(4):
        for ref, which in ((keep, place[0]), (send, place[1])):
            source = pl.multiple_of((which ^ q) * PART, 8)
            ref[q * PART : (q + 1) * PART, :] = packed[pl.ds(source, PART), :]


def field_gradients(find_place, local, other, params):
    means, variances, spacing, dirs, target, counts, mask = local
    means_two, variances_two, spacing_two, other_counts, other_rows, mask_two = (
        pltpu.with_memory_space_constraint(array, pltpu.VMEM) for array in other[:5] + (other[5].reshape(1, -1),)
    )
    w_in, w_mid, w_head, w_rgb, vec = params
    rays = dirs.shape[1]
    room = 17 * rays * LANES // 16 + LANES
    tiles = -(-(room - LANES) // (8 * LANES)) * 8
    pitch = tiles + 8 * (1 - tiles // 8 % 2)
    vmem = pl.BlockSpec(memory_space=pltpu.VMEM)
    smem = pl.BlockSpec(memory_space=pltpu.SMEM)
    hbm = pl.BlockSpec(memory_space=pl.ANY)
    scratch = [
        pltpu.VMEM((2 * 8 * (rays + 8), LANES), F32),
        pltpu.VMEM((room // LANES + 1, 8, LANES), F32),
        pltpu.VMEM((8 * pitch, LANES), F32),
        pltpu.VMEM((8 * pitch, LANES), F32),
        pltpu.VMEM((8 * pitch, LANES), F32),
        pltpu.VMEM((128, room), BF16),
        pltpu.VMEM((272, room), BF16),
        pltpu.VMEM((272, room), BF16),
        pltpu.VMEM((256, room), BF16),
        pltpu.VMEM((256, room), F32),
        pltpu.VMEM((256, room), F32),
        pltpu.VMEM((256, room), F32),
        pltpu.VMEM((128, room), BF16),
        pltpu.VMEM((128, room), F32),
        pltpu.VMEM((rays, room), BF16),
        pltpu.VMEM((16, LANES), F32),
        pltpu.SMEM((2, rays), jnp.int32),
        pltpu.VMEM((16, LANES), F32),
        pltpu.VMEM((128, 256), F32),
        pltpu.VMEM((256, 128), BF16),
        pltpu.VMEM((2, 256, 256), BF16),
        pltpu.VMEM((2, 256, 256), BF16),
        pltpu.VMEM((144, 256), BF16),
        pltpu.VMEM((256, 144), BF16),
        pltpu.VMEM((16, 128), BF16),
        pltpu.VMEM((128, 16), BF16),
        pltpu.VMEM((2, 256, 128), F32),
        pltpu.VMEM((144, 3 * rays), BF16),
        pltpu.VMEM((32, rays), BF16),
        pltpu.VMEM((128, 256), F32),
        pltpu.VMEM((2, 16, 256), F32),
        pltpu.VMEM((384 + rays, 256), F32),
        pltpu.VMEM((8, LANES), F32),
        pltpu.VMEM((8 * PART, 256), F32),
        pltpu.SemaphoreType.DMA((30,)),
    ]
    return pl.pallas_call(
        functools.partial(field_kernel, find_place),
        out_shape=[pltpu.VMEM((4 * PART, 256), F32)] * 2,
        in_specs=[smem] + [vmem] * 6 + [hbm] * 3 + [vmem] * 9,
        out_specs=[vmem, vmem],
        scratch_shapes=scratch,
        compiler_params=pltpu.CompilerParams(vmem_limit_bytes=62 << 20),
    )(
        counts,
        other_counts,
        mask_two,
        means_two,
        variances_two,
        spacing_two,
        other_rows,
        means,
        variances,
        spacing,
        dirs,
        target,
        mask.reshape(1, rays),
        counts,
        w_in,
        w_mid,
        w_head,
        w_rgb.T,
        vec,
    )


def ray_rows(local):
    dirs, target = local[3:5]
    rows = jnp.concatenate([dirs, target], axis=0)
    return jnp.pad(rows, ((0, 16 - rows.shape[0]), (0, LANES - rows.shape[1])))


def adamw(weight, grad, first, second):
    first = BETA_ONE * first + (1.0 - BETA_ONE) * grad
    second = BETA_TWO * second + (1.0 - BETA_TWO) * grad * grad
    first_hat = first * (1.0 / (1.0 - BETA_ONE**STEP))
    second_hat = second * (1.0 / (1.0 - BETA_TWO**STEP))
    fresh = weight - LEARN_RATE * (first_hat / (jnp.sqrt(second_hat) + EPSILON) + DECAY * weight)
    return first, second, fresh


def update_kernel(find_place, *refs):
    place = find_place()
    pieces, refs = refs[0:8], refs[8:]
    weights, firsts, seconds = refs[0:5], refs[5:10], refs[10:15]
    loss, count = refs[15], refs[16]
    outs = refs[17:32]
    packed = refs[32]
    for k, ref in enumerate(pieces):
        block = place[k // 4] ^ (k % 4)
        packed[pl.ds(pl.multiple_of(block * PART, 8), PART), :] = ref[...]
    line = packed[740:741, 128:256]
    loss[0] = line[0, 4]
    count[0] = line[0, 5]
    scale = 1.0 / line[0:1, 5:6]

    def apply(group, at, grad):
        step = scale.reshape(1) if grad.ndim == 1 else scale
        made = adamw(weights[group][at], grad * step, firsts[group][at], seconds[group][at])
        for k in range(3):
            outs[3 * group + k][at] = made[k]

    everything = slice(None)
    apply(0, (everything, everything), packed[0:96, :])
    for k in range(2):
        apply(1, (k, everything, everything), packed[96 + 256 * k : 352 + 256 * k, :])
    for k in range(2):
        apply(2, (slice(128 * k, 128 * k + 128), everything), packed[608:736, 128 * k : 128 * k + 128])
    apply(2, (slice(256, 272), everything), packed[744:760, 0:128])
    apply(2, (slice(272, 283), everything), packed[744:755, 128:256])
    apply(3, (everything, everything), packed[741:744, 0:128])
    for k in range(9):
        line = packed[736 + k // 2 : 737 + k // 2, 128 * (k % 2) : 128 * (k % 2) + 128]
        apply(4, (pl.ds(128 * k, 128),), line.reshape(128))
    apply(4, (pl.ds(1152, 4),), packed[740:741, 128:132].reshape(4))


def update(find_place, pieces, params, firsts, seconds):
    vmem = pl.BlockSpec(memory_space=pltpu.VMEM)
    smem = pl.BlockSpec(memory_space=pltpu.SMEM)
    shapes = [jax.ShapeDtypeStruct((1,), F32)] * 2
    for array in params:
        shapes += [jax.ShapeDtypeStruct(array.shape, F32)] * 3
    return pl.pallas_call(
        functools.partial(update_kernel, find_place),
        out_shape=shapes,
        in_specs=[vmem] * 23,
        out_specs=[smem, smem] + [vmem] * 15,
        scratch_shapes=[pltpu.VMEM((8 * PART, 256), F32)],
        compiler_params=pltpu.CompilerParams(vmem_limit_bytes=32 << 20),
    )(*pieces, *params, *firsts, *seconds)


def xor_pairs(total, mask_of):
    return [(i, i ^ mask_of(i)) for i in range(total)]


def place_small():
    ray = lax.axis_index("rays")
    rep = lax.axis_index("rep")
    y, x, core = ray % 2, rep // 2, rep % 2
    xy, yx = 2 * x + y, 2 * y + x
    return (
        jnp.where(core == 0, xy, 4 + yx),
        jnp.where(core == 0, 4 + yx, xy),
    )


def reduce_small(keep, send, axes):
    core = xor_pairs(32, lambda i: 1)
    one = xor_pairs(32, lambda i: 4 if i & 1 else 2)
    two = xor_pairs(32, lambda i: 2 if i & 1 else 4)
    both = xor_pairs(32, lambda i: 6)
    z_one = xor_pairs(32, lambda i: 16 if i & 1 else 8)
    z_two = xor_pairs(32, lambda i: 8 if i & 1 else 16)

    def swap(value, pairs):
        return lax.ppermute(value, axes, pairs)

    square = (two, one, both)
    now = keep + swap(send, core)
    got = [swap(now[PART * (k + 1) : PART * (k + 2)], pairs) for k, pairs in enumerate(square)]
    own = (now[:PART] + got[0]) + (got[1] + got[2])
    own = own + swap(own, z_one)
    own = own + swap(own, z_two)
    parts = [own] + [swap(own, pairs) for pairs in square]
    return parts + [swap(part, core) for part in parts]


def on_device(
    small_mesh,
    sample_means,
    sample_vars,
    sample_spacing,
    view_dirs,
    target_rgb,
    sample_counts,
    ray_mask,
    w_in,
    w_mid,
    w_head,
    w_rgb,
    vectors,
    first_in,
    first_mid,
    first_head,
    first_rgb,
    first_vec,
    second_in,
    second_mid,
    second_head,
    second_rgb,
    second_vec,
):
    axes = ("rays", "rep")
    find_place = place_small if small_mesh else lambda: (0, 4)
    params = (w_in, w_mid, w_head, w_rgb, vectors)
    local = (sample_means, sample_vars, sample_spacing, view_dirs, target_rgb, sample_counts, ray_mask)
    other = (sample_means, sample_vars, sample_spacing, sample_counts, ray_rows(local), ray_mask)
    if small_mesh:
        core_pairs = xor_pairs(32, lambda i: 1)
        other = tuple(lax.ppermute(array, axes, core_pairs) for array in other)
    keep, send = field_gradients(find_place, local, other, params)
    if small_mesh:
        pieces = reduce_small(keep, send, axes)
    else:
        whole = lax.psum(jnp.concatenate([keep, send], axis=0), axes)
        pieces = [whole[PART * k : PART * (k + 1)] for k in range(8)]
    outs = update(
        find_place,
        pieces,
        (w_in, w_mid, w_head, w_rgb.T, vectors),
        (first_in, first_mid, first_head, first_rgb.T, first_vec),
        (second_in, second_mid, second_head, second_rgb.T, second_vec),
    )
    rgb = [out.T for out in outs[11:14]]
    return (outs[0].reshape(()), outs[1].reshape(()), *outs[2:11], *rgb, *outs[14:17])


def solution(mesh):
    rays = ("rays", "rep")
    in_specs = (
        P(None, None, rays, None),
        P(None, None, rays, None),
        P(None, rays, None),
        P(None, rays),
        P(None, rays),
        P(None, rays),
        P(rays),
    ) + (P(),) * 15
    small_mesh = mesh.shape["rays"] == 8 and mesh.shape["rep"] == 4

    def step(*args):
        return on_device(small_mesh, *args)

    return jax.shard_map(step, mesh=mesh, in_specs=in_specs, out_specs=(P(),) * 17, check_vma=False)
```
